512 devices in a mesh: lat: 16 (over y, x_lo, core), lon: 32 (over x_hi, z).
Axes of the slice: x: 4 (x_hi: 2, x_lo: 2; x = x_hi * 2 + x_lo), y: 4, z: 16, core: 2. Of those that a mesh axis runs over, the one named last changes fastest.
Arguments:
- height: float32 [1, 1536, 12288], P(None, 'lat', 'lon'), may hold values from -6 to 6
- east_wind: float32 [1, 1536, 12288], P(None, 'lat', 'lon'), may hold values from -6 to 6
- north_wind: float32 [1, 1536, 12288], P(None, 'lat', 'lon'), may hold values from -6 to 6
- wave_speed_sq: float32 [1], replicated, may hold values from 0.25 to 1
Outputs:
- height_new: float32 [1, 1536, 12288], P(None, 'lat', 'lon')
- east_new: float32 [1, 1536, 12288], P(None, 'lat', 'lon')
- north_new: float32 [1, 1536, 12288], P(None, 'lat', 'lon')
The draws below stay inside these ranges and needn't reach their ends.
All inputs are finite; a program needn't handle non-finite values.
Results may differ from the reference program's by a relative error of at most 0.0003.
Values sent between devices are 32-bit elements; how exact they have to be, the bound alone decides.
A program may use at most 64 MiB of HBM per device.

```python
import math
import jax
import jax.numpy as jnp

NLON = 12288
LAYERS = 1
SUBSTEPS = 2
NLAT = 1536


def block_levels(own_key, dims, shards, low, largest):
    def one(dim, parts):
        heights = jax.random.uniform(jax.random.fold_in(jax.random.fold_in(own_key, 6), dim), (parts,), jnp.float32, low / len(shards), largest / len(shards))
        return jnp.repeat(jnp.exp(heights), dims[dim] // parts).reshape((-1,) + (1,) * (len(dims) - dim - 1))

    level = one(*shards[0])
    for cut in shards[1:]:
        level = level * one(*cut)
    return level


def gaussian(stream_key, dims, scale, most, cuts=(), kind=jnp.bfloat16):
    values = scale * jax.random.normal(stream_key, dims, jnp.float32)
    if cuts:
        values = values * block_levels(stream_key, dims, cuts, -0.22, 0.18)
    return jnp.clip(values, -most, most).astype(kind)


def setup_inputs(seed: int = 0) -> dict:
    arg_keys = jax.random.split(jax.random.key(seed), 5)
    height = gaussian(arg_keys[0], (LAYERS, NLAT, NLON), 1.0, 6.0, ((1, 16), (2, 32)), jnp.float32)
    east_wind = gaussian(arg_keys[1], (LAYERS, NLAT, NLON), 1.0, 6.0, ((1, 16), (2, 32)), jnp.float32)
    north_wind = gaussian(arg_keys[2], (LAYERS, NLAT, NLON), 1.0, 6.0, ((1, 16), (2, 32)), jnp.float32)
    wave_speed_sq = jnp.clip(jnp.exp(jax.random.uniform(arg_keys[3], (LAYERS,), jnp.float32, math.log(0.25), math.log(1.0))), 0.25, 1.0)
    return dict(height=height, east_wind=east_wind, north_wind=north_wind, wave_speed_sq=wave_speed_sq)


COURANT = 0.45
SPIN = 0.3


def east_diff(field):
    return (jnp.roll(field, -1, axis=2) - jnp.roll(field, 1, axis=2)) * 0.5


def north_diff(field):
    padded = jnp.pad(field, ((0, 0), (1, 1), (0, 0)))
    return (padded[:, 2:] - padded[:, :-2]) * 0.5


def polar_filter(field, cosine):
    spectrum = jnp.fft.rfft(field, axis=2)
    wave = jnp.arange(NLON // 2 + 1).astype(jnp.float32)
    half_sine = 0.5 * jnp.abs(jnp.sin(wave * (math.pi / NLON)))
    factor = cosine[:, None] / jnp.maximum(half_sine[None, :], cosine[:, None])
    return jnp.fft.irfft(spectrum * factor[None], n=NLON, axis=2).astype(field.dtype)


def reference(height, east_wind, north_wind, wave_speed_sq):
    index = jnp.arange(NLAT).astype(jnp.float32)
    latitude = -0.5 * math.pi + (index + 0.5) * (math.pi / NLAT)
    cosine = jnp.cos(latitude)
    sine = jnp.sin(latitude)
    col_cos = cosine[None, :, None]
    col_sin = sine[None, :, None]
    north_scale = COURANT * 2.0 * NLAT / NLON
    speed = wave_speed_sq[:, None, None]
    thick, east, north = height, east_wind, north_wind
    for step in range(SUBSTEPS):
        east_inc = -(COURANT / col_cos) * east_diff(thick) + SPIN * col_sin * north
        north_inc = -north_scale * north_diff(thick) - SPIN * col_sin * east
        east = east + polar_filter(east_inc, cosine)
        north = north + polar_filter(north_inc, cosine)
        spread = (COURANT / col_cos) * east_diff(east) + (north_scale / col_cos) * north_diff(north * col_cos)
        thick = thick + polar_filter(-speed * spread, cosine)
    return thick, east, north
```

```python
import math

import jax
import jax.numpy as jnp
import ml_dtypes
import numpy as np
from jax import lax
from jax.experimental import pallas as pl
from jax.experimental.pallas import tpu as pltpu
from jax.sharding import PartitionSpec as P

NLON, NLAT = 12288, 1536
ROWS, CELLS = 96, 384
OUTER, INNER = 96, 128
HALF = 56
COURANT, SPIN = 0.45, 0.3
NORTH = COURANT * 2.0 * NLAT / NLON
FINAL = 260
LAST = 264
MESH = pl.DeviceIdType.MESH
F32, BF16 = jnp.float32, jnp.bfloat16
GROUPS = ((0,), (1, 2))


def split(table):
    high = table.astype(ml_dtypes.bfloat16)
    low = (table - high.astype(np.float64)).astype(ml_dtypes.bfloat16)
    return high, low


def tables():
    a = np.array([3 * d + s for s in range(3) for d in range(32)])
    k1 = np.arange(HALF)
    live = (k1 <= OUTER // 2).astype(np.float64)
    angle = 2 * np.pi * ((k1[:, None] * a[None, :]) % OUTER) / OUTER
    first = np.concatenate([np.cos(angle) * live[:, None], -np.sin(angle) * live[:, None]], axis=0)
    weight = live * np.where((k1 == 0) | (k1 == OUTER // 2), 1.0, 2.0) / NLON
    last = np.concatenate([np.cos(angle) * weight[:, None], -np.sin(angle) * weight[:, None]], axis=0).T
    n = np.arange(INNER)
    turn = 2 * np.pi * (k1[:, None] * n[None, :]) / NLON
    inner = 2 * np.pi * ((n[:, None] * n[None, :]) % INNER) / INNER
    cos, sin = np.cos(inner), np.sin(inner)
    forward = np.block([[cos, -sin], [sin, cos]])
    backward = np.block([[cos, sin], [-sin, cos]])
    wave = k1[:, None] + OUTER * n[None, :]
    steep = np.sin(2 * np.pi * wave / NLON) * live[:, None]
    half_sine = np.where(live[:, None] > 0, 0.5 * np.abs(np.sin(np.pi * wave / NLON)), 1.0)
    first_high, first_low = split(first)
    last_high, last_low = split(last)
    forward_high, forward_low = split(forward)
    backward_high, backward_low = split(backward)
    grid = np.stack([np.cos(turn), np.sin(turn), steep, half_sine]).astype(np.float32)
    row = np.arange(-1, LAST + 1)
    latitude = -0.5 * np.pi + (row + 0.5) * np.pi / NLAT
    ring = np.stack([np.cos(latitude), np.sin(latitude)]).astype(np.float32)
    return (
        np.concatenate([first_high, first_low, first_high], axis=1),
        np.concatenate([last_high, last_low, last_high], axis=1),
        np.stack([forward_high, forward_low]),
        np.stack([backward_high, backward_low]),
        grid,
        ring,
    )


def parts(value):
    high = value.astype(BF16)
    return high, (value - high.astype(F32)).astype(BF16)


def dot(left, right):
    return jnp.dot(left, right, preferred_element_type=F32)


def outer_step(table, value):
    high, low = parts(value)
    return dot(table, jnp.concatenate([high, high, low], axis=0))


def inner_step(table, value):
    high, low = parts(value)
    return dot(high, table[0]) + dot(low, table[0]) + dot(high, table[1])


def kernel(
    h_ref, u_ref, v_ref, speed_ref, ring_ref, first_ref, last_ref, fore_ref, back_ref, grid_ref,
    h_out, u_out, v_out,
    src0, src1, relay0, relay1, recv0, recv1, snd0, snd1, home0, home1, ret0, ret1,
    nb, state, packed, sides, ext,
    send_a, recv_a, send_b, recv_b, send_c, recv_c, send_d, recv_d,
    send_x, recv_x, send_s, recv_s, send_r, recv_r,
):
    fields, outs = (h_ref, u_ref, v_ref), (h_out, u_out, v_out)
    src, relay, recv = (src0, src1), (relay0, relay1), (recv0, recv1)
    snd, home, ret = (snd0, snd1), (home0, home1), (ret0, ret1)
    lat, lon = lax.axis_index("lat"), lax.axis_index("lon")
    south = lat >= 8
    band = jnp.where(south, 15 - lat, lat)
    core = lax.rem(band, 2)
    x_hi, z = lax.div(lon, 16), lax.rem(lon, 16)
    x = 2 * x_hi + lax.rem(lax.div(band, 2), 2)
    line = jnp.where(band < 4, x, 7 - x)
    place = 2 * z + core
    slab = 16 * core + z
    wide = line >= 6
    double = jnp.logical_and(wide, place >= 28)
    count = jnp.where(double, 2, 1)
    chain = 32 * line + place
    line_rows = jnp.where(wide, 36, 32)
    line_row = place + jnp.where(double, place - 28, 0)
    row0 = 32 * line + jnp.where(line == 7, 4, 0) + line_row
    flip = jnp.where(south, -1.0, 1.0).astype(F32)
    source = band <= 2
    stencil = band >= 2

    def member(to_line, to_z, to_core):
        to_x = jnp.where(to_line < 4, to_line, 7 - to_line)
        to_band = 4 * lax.div(to_line, 4) + 2 * lax.rem(to_x, 2) + to_core
        return jnp.where(south, 15 - to_band, to_band), 16 * lax.div(to_x, 2) + to_z

    def send(here, there, send_sem, recv_sem, target):
        same = jnp.logical_and(target[0] == lat, target[1] == lon)

        @pl.when(same)
        def _():
            pltpu.make_async_copy(here, there, recv_sem).start()

        @pl.when(jnp.logical_not(same))
        def _():
            pltpu.make_async_remote_copy(
                src_ref=here, dst_ref=there, send_sem=send_sem, recv_sem=recv_sem, device_id=target, device_id_type=MESH
            ).start()

    def remote(here, there, send_sem, recv_sem, target):
        pltpu.make_async_remote_copy(
            src_ref=here, dst_ref=there, send_sem=send_sem, recv_sem=recv_sem, device_id=target, device_id_type=MESH
        ).start()

    def landed(ref, sem):
        pltpu.make_async_copy(ref, ref, sem).wait()

    def each_size(act):
        pl.when(jnp.logical_not(wide))(lambda: act(32))
        pl.when(wide)(lambda: act(36))

    def line_start(k, size):
        return jnp.where(south, ROWS - size * (k + 1), size * k)

    def turned(row):
        return jnp.where(south, line_rows - 1 - row, row)

    def send_lines(g):
        per = 3 * len(GROUPS[g])
        for pos, f in enumerate(GROUPS[g]):
            for s in range(3):
                src[g][pl.ds(3 * pos + s, ROWS, stride=per), :] = fields[f][0, :, 128 * s : 128 * (s + 1)]

        def to_line(k, size):
            start = line_start(k, size)
            send(
                src[g].at[pl.ds(start * per, size * per)], relay[g].at[pl.ds(0, size * per)],
                send_a.at[g, k], recv_a.at[g], member(3 * band + k, z, x_hi),
            )

        @pl.when(band < 2)
        def _():
            for k in range(3):
                to_line(k, 32)

        @pl.when(band == 2)
        def _():
            for k in range(2):
                to_line(k, 36)

    @pl.when(source)
    def _():
        for g in range(2):
            send_lines(g)

    right = jnp.where(lon == 31, 0, lon + 1)
    left = jnp.where(lon == 0, 31, lon - 1)

    @pl.when(stencil)
    def _():
        lane = lax.broadcasted_iota(jnp.int32, (ROWS, 128), 1)
        high = [ref[0, :, 256:384] for ref in fields]
        low = [ref[0, :, 0:128] for ref in fields]
        packed[0] = jnp.where(
            lane >= 124, high[0], jnp.where(lane >= 120, pltpu.roll(high[1], 124, 1), pltpu.roll(high[2], 120, 1))
        )
        packed[1] = jnp.where(lane < 4, low[0], jnp.where(lane < 8, pltpu.roll(low[1], 4, 1), pltpu.roll(low[2], 8, 1)))
        remote(packed.at[0], sides.at[0], send_s.at[0], recv_s.at[0], (lat, right))
        remote(packed.at[1], sides.at[1], send_s.at[1], recv_s.at[1], (lat, left))

    def owner(row):
        late = jnp.logical_and(wide, row >= 28)
        return jnp.where(late, 28 + lax.div(row - 28, 2), row), jnp.where(late, lax.rem(row, 2), 0)

    for g in range(2):
        per = 3 * len(GROUPS[g])
        each_size(lambda size, g=g, per=per: landed(relay[g].at[pl.ds(0, size * per)], recv_a.at[g]))

        def spread(row, carry, g=g, per=per):
            to, slot = owner(row)
            send(
                relay[g].at[pl.ds(turned(row) * per, per)], recv[g].at[pl.ds((32 * slot + slab) * per, per)],
                send_b.at[g], recv_b.at[g, slot], member(line, lax.div(to, 2), lax.rem(to, 2)),
            )
            return carry

        lax.fori_loop(0, line_rows, spread, 0)

    @pl.when(stencil)
    def _():
        landed(sides.at[0], recv_s.at[0])
        landed(sides.at[1], recv_s.at[1])
        lane = lax.broadcasted_iota(jnp.int32, (ROWS, 128), 1)
        for f in range(3):
            ext[f, 8 : 8 + ROWS, 0:CELLS] = fields[f][0]
            after, before = sides[1], sides[0]
            if f:
                after, before = pltpu.roll(after, 128 - 4 * f, 1), pltpu.roll(before, 4 * f, 1)
            ext[f, 8 : 8 + ROWS, CELLS : CELLS + 128] = jnp.where(lane < 64, after, before)

        @pl.when(lat > 2)
        def _():
            remote(ext.at[:, 8:16, :], ext.at[:, 104:112, :], send_r.at[0], recv_r.at[0], (lat - 1, lon))

        @pl.when(lat < 13)
        def _():
            remote(ext.at[:, 96:104, :], ext.at[:, 0:8, :], send_r.at[1], recv_r.at[1], (lat + 1, lon))

        @pl.when(lat == 2)
        def _():
            ext[:, 0:8, :] = jnp.zeros((3, 8, 512), F32)

        @pl.when(lat == 13)
        def _():
            ext[:, 104:112, :] = jnp.zeros((3, 8, 512), F32)

    up_line, up_place = lax.div(chain - 1, 32), lax.rem(chain + 31, 32)
    up = member(up_line, lax.div(up_place, 2), lax.rem(up_place, 2))
    up_count = jnp.where(jnp.logical_and(up_line >= 6, up_place >= 28), 2, 1)
    down_place = lax.rem(chain + 1, 32)
    down = member(lax.div(chain + 1, 32), lax.div(down_place, 2), lax.rem(down_place, 2))
    speed = speed_ref[0]

    def each_slot(act):
        act(0)
        pl.when(double)(lambda: act(1))

    @pl.when(chain == 0)
    def _():
        for e in range(4):
            nb[e, 0] = jnp.zeros((2 * HALF, 128), F32)

    @pl.when(chain == 255)
    def _():
        for e in range(4):
            nb[e, 3] = jnp.zeros((2 * HALF, 128), F32)

    def trade(e):
        @pl.when(chain > 0)
        def _():
            remote(nb.at[e, 1], nb.at[e, up_count + 1], send_x.at[e, 0], recv_x.at[e, 1], up)

        @pl.when(chain < 255)
        def _():
            remote(nb.at[e, count], nb.at[e, 0], send_x.at[e, 1], recv_x.at[e, 0], down)

    def traded(e):
        @pl.when(chain > 0)
        def _():
            landed(nb.at[e, 0], recv_x.at[e, 0])

        @pl.when(chain < 255)
        def _():
            landed(nb.at[e, count + 1], recv_x.at[e, 1])

    def transform(g, slot):
        per = 3 * len(GROUPS[g])
        grids = []
        for pos in range(len(GROUPS[g])):
            start = 32 * per * slot + 3 * pos
            grids.append(jnp.concatenate([recv[g][pl.ds(start + s, 32, stride=per), :] for s in range(3)], axis=0))
        mixed = outer_step(first_ref[...], jnp.concatenate(grids, axis=1))
        cos, sin = grid_ref[0], grid_ref[1]
        turned_rows = []
        for pos in range(len(GROUPS[g])):
            real, imag = mixed[:HALF, 128 * pos : 128 * (pos + 1)], mixed[HALF:, 128 * pos : 128 * (pos + 1)]
            turned_rows.append(jnp.concatenate([real * cos + imag * sin, imag * cos - real * sin], axis=1))
        spectrum = inner_step(fore_ref, jnp.concatenate(turned_rows, axis=0))
        return [
            (spectrum[HALF * pos : HALF * (pos + 1), :128], spectrum[HALF * pos : HALF * (pos + 1), 128:])
            for pos in range(len(GROUPS[g]))
        ]

    def restore(g, slot, spectra):
        per = 3 * len(GROUPS[g])
        cos, sin = grid_ref[0], grid_ref[1]
        back = inner_step(back_ref, jnp.concatenate([jnp.concatenate(pair, axis=1) for pair in spectra], axis=0))
        spun = []
        for pos in range(len(GROUPS[g])):
            real, imag = back[HALF * pos : HALF * (pos + 1), :128], back[HALF * pos : HALF * (pos + 1), 128:]
            spun.append(jnp.concatenate([real * cos - imag * sin, imag * cos + real * sin], axis=0))
        rows = outer_step(last_ref[...], jnp.concatenate(spun, axis=1))
        for pos in range(len(GROUPS[g])):
            for s in range(3):
                snd[g][pl.ds(32 * per * slot + 3 * pos + s, 32, stride=per), :] = rows[
                    32 * s : 32 * (s + 1), 128 * pos : 128 * (pos + 1)
                ]

    def put(ref, index, pair):
        ref[(*index, slice(0, HALF))] = pair[0]
        ref[(*index, slice(HALF, 2 * HALF))] = pair[1]

    def get(ref, *index):
        return ref[(*index, slice(0, HALF))], ref[(*index, slice(HALF, 2 * HALF))]

    def factors(slot):
        cosine = ring_ref[0, row0 + slot + 1]
        share = 1.0 / jnp.maximum(grid_ref[3], cosine)
        return share, share * cosine, SPIN * ring_ref[1, row0 + slot + 1]

    def push_east(slot, height, east, north):
        share, keep, spin = factors(slot)
        slope, swirl = share * (COURANT * grid_ref[2]), keep * spin
        return (
            east[0] + slope * height[1] + swirl * north[0],
            east[1] - slope * height[0] + swirl * north[1],
        )

    def push_north(slot, above, below, east, north):
        _, keep, spin = factors(slot)
        return tuple(
            north[p] - keep * ((0.5 * NORTH) * (below[p] - above[p]) + spin * east[p]) for p in range(2)
        )

    def push_height(slot, above, below, east, height):
        share, _, _ = factors(slot)
        share = speed * share
        slope = share * (COURANT * grid_ref[2])
        fall = share * (0.5 * NORTH)
        higher, lower = ring_ref[0, row0 + slot], ring_ref[0, row0 + slot + 2]
        return (
            height[0] + slope * east[1] - fall * (lower * below[0] - higher * above[0]),
            height[1] - slope * east[0] - fall * (lower * below[1] - higher * above[1]),
        )

    def first_height(slot):
        landed(recv[0].at[pl.ds(96 * slot, 96)], recv_b.at[0, slot])
        put(nb, (0, slot + 1), transform(0, slot)[0])

    def first_winds(slot):
        landed(recv[1].at[pl.ds(192 * slot, 192)], recv_b.at[1, slot])
        east, north = transform(1, slot)
        put(state, (slot, 0), east)
        put(state, (slot, 1), (flip * north[0], flip * north[1]))

    def north_one(slot):
        put(
            nb, (1, slot + 1),
            push_north(slot, get(nb, 0, slot), get(nb, 0, slot + 2), get(state, slot, 0), get(state, slot, 1)),
        )

    def east_one(slot):
        put(state, (slot, 2), push_east(slot, get(nb, 0, slot + 1), get(state, slot, 0), get(state, slot, 1)))

    def height_one(slot):
        put(
            nb, (2, slot + 1),
            push_height(slot, get(nb, 1, slot), get(nb, 1, slot + 2), get(state, slot, 2), get(nb, 0, slot + 1)),
        )

    def east_two(slot):
        put(state, (slot, 3), push_east(slot, get(nb, 2, slot + 1), get(state, slot, 2), get(nb, 1, slot + 1)))

    def north_two(slot):
        put(
            nb, (3, slot + 1),
            push_north(slot, get(nb, 2, slot), get(nb, 2, slot + 2), get(state, slot, 2), get(nb, 1, slot + 1)),
        )

    def winds_back(slot):
        north = get(nb, 3, slot + 1)
        restore(1, slot, [get(state, slot, 3), (flip * north[0], flip * north[1])])

    def height_back(slot):
        height = push_height(slot, get(nb, 3, slot), get(nb, 3, slot + 2), get(state, slot, 3), get(nb, 2, slot + 1))
        restore(0, slot, [height])

    def return_pieces(g, slot):
        per = 3 * len(GROUPS[g])
        row = turned(line_row + slot)

        def piece(d, carry):
            send(
                snd[g].at[pl.ds((32 * slot + d) * per, per)], home[g].at[pl.ds(row * per, per)],
                send_c.at[g, slot], recv_c.at[g], member(line, lax.rem(d, 16), lax.div(d, 16)),
            )
            return carry

        lax.fori_loop(0, 32, piece, 0)

    each_slot(first_height)
    trade(0)
    each_slot(first_winds)
    traded(0)
    each_slot(north_one)
    trade(1)
    each_slot(east_one)
    traded(1)
    each_slot(height_one)
    trade(2)
    each_slot(east_two)
    traded(2)
    each_slot(north_two)
    trade(3)
    each_slot(winds_back)
    each_slot(lambda slot: return_pieces(1, slot))
    traded(3)
    each_slot(height_back)
    each_slot(lambda slot: return_pieces(0, slot))

    to_band = jnp.where(wide, 2, lax.div(line, 3))
    to_lat = jnp.where(south, 15 - to_band, to_band)
    nth = line - 3 * to_band
    for g in (1, 0):
        per = 3 * len(GROUPS[g])

        def deliver(size, g=g, per=per):
            landed(home[g].at[pl.ds(0, size * per)], recv_c.at[g])
            start = line_start(nth, size)
            send(
                home[g].at[pl.ds(0, size * per)], ret[g].at[pl.ds(start * per, size * per)],
                send_d.at[g], recv_d.at[g, nth], (to_lat, slab),
            )

        each_size(deliver)

    @pl.when(stencil)
    def _():
        @pl.when(lat > 2)
        def _():
            landed(ext.at[:, 0:8, :], recv_r.at[1])

        @pl.when(lat < 13)
        def _():
            landed(ext.at[:, 104:112, :], recv_r.at[0])

        row = lax.broadcasted_iota(jnp.int32, (ROWS + 16, 128), 0) + (ROWS * lat - 8)
        latitude = (row.astype(F32) + (0.5 - NLAT // 2)) * (math.pi / NLAT)
        wide_cos = jnp.concatenate([jnp.cos(latitude)] * 4, axis=1)
        spin = jnp.concatenate([SPIN * jnp.sin(latitude)] * 4, axis=1)
        inverse = 1.0 / wide_cos
        east_scale = (0.5 * COURANT) * inverse

        def across(value):
            return pltpu.roll(value, 511, 1) - pltpu.roll(value, 1, 1)

        def along(value):
            return pltpu.roll(value, ROWS + 15, 0) - pltpu.roll(value, 1, 0)

        height, east, north = ext[0], ext[1], ext[2]
        for _step in range(2):
            east_inc = spin * north - east_scale * across(height)
            north_inc = (-0.5 * NORTH) * along(height) - spin * east
            east, north = east + east_inc, north + north_inc
            spread_out = east_scale * across(east) + (0.5 * NORTH) * inverse * along(north * wide_cos)
            height = height - speed * spread_out
        for out, value in zip(outs, (height, east, north)):
            out[0] = value[8 : 8 + ROWS, 0:CELLS]

    def arrived(k, size):
        for g in range(2):
            per = 3 * len(GROUPS[g])
            landed(ret[g].at[pl.ds(line_start(k, size) * per, size * per)], recv_d.at[g, k])

    def back(f, s):
        g = 0 if f == 0 else 1
        per, pos = 3 * len(GROUPS[g]), GROUPS[g].index(f)
        return ret[g][pl.ds(3 * pos + s, ROWS, stride=per), :]

    @pl.when(band < 2)
    def _():
        for k in range(3):
            arrived(k, 32)
        for f in range(3):
            for s in range(3):
                outs[f][0, :, 128 * s : 128 * (s + 1)] = back(f, s)

    @pl.when(band == 2)
    def _():
        for k in range(2):
            arrived(k, 36)
        row = lax.broadcasted_iota(jnp.int32, (ROWS, 128), 0)
        from_pole = jnp.where(south, ROWS - 1 - row, row) + 2 * ROWS
        for f in range(3):
            for s in range(3):
                lanes = slice(128 * s, 128 * (s + 1))
                outs[f][0, :, lanes] = jnp.where(from_pole < FINAL, back(f, s), outs[f][0, :, lanes])

    for g in range(2):
        per = 3 * len(GROUPS[g])

        def left_lines(size, lines, g=g, per=per):
            for k in range(lines):
                to = member(3 * band + k, z, x_hi)

                @pl.when(jnp.logical_not(jnp.logical_and(to[0] == lat, to[1] == lon)))
                def _(k=k):
                    landed(src[g].at[pl.ds(0, size * per)], send_a.at[g, k])

        pl.when(band < 2)(lambda f=left_lines: f(32, 3))
        pl.when(band == 2)(lambda f=left_lines: f(36, 2))

        pl.when(jnp.logical_not(wide))(lambda g=g, per=per: landed(relay[g].at[pl.ds(0, 31 * per)], send_b.at[g]))
        pl.when(jnp.logical_and(wide, jnp.logical_not(double)))(
            lambda g=g, per=per: landed(relay[g].at[pl.ds(0, 35 * per)], send_b.at[g])
        )
        pl.when(double)(lambda g=g, per=per: landed(relay[g].at[pl.ds(0, 34 * per)], send_b.at[g]))
        each_slot(lambda slot, g=g, per=per: landed(snd[g].at[pl.ds(0, 31 * per)], send_c.at[g, slot]))

        @pl.when(jnp.logical_not(jnp.logical_and(to_lat == lat, slab == lon)))
        def _(g=g, per=per):
            each_size(lambda size: landed(home[g].at[pl.ds(0, size * per)], send_d.at[g]))

    @pl.when(stencil)
    def _():
        for side in range(2):
            landed(packed.at[side], send_s.at[side])

        @pl.when(lat > 2)
        def _():
            landed(ext.at[:, 8:16, :], send_r.at[0])

        @pl.when(lat < 13)
        def _():
            landed(ext.at[:, 96:104, :], send_r.at[1])

    for e in range(4):
        pl.when(chain > 0)(lambda e=e: landed(nb.at[e, 1], send_x.at[e, 0]))
        pl.when(chain < 255)(lambda e=e: landed(nb.at[e, 1], send_x.at[e, 1]))


def body(height, east_wind, north_wind, wave_speed_sq):
    first, last, fore, back, grid, ring = tables()
    vmem, smem = pl.BlockSpec(memory_space=pltpu.VMEM), pl.BlockSpec(memory_space=pltpu.SMEM)
    block = jax.ShapeDtypeStruct((1, ROWS, CELLS), F32)
    pairs = []
    for rows in (ROWS, 36, 64, 64, 36, ROWS):
        pairs += [pltpu.VMEM((rows * 3 * len(group), 128), F32) for group in GROUPS]
    dma = pltpu.SemaphoreType.DMA
    return pl.pallas_call(
        kernel,
        out_shape=[block] * 3,
        in_specs=[vmem] * 3 + [smem] * 2 + [vmem] * 5,
        out_specs=[vmem] * 3,
        scratch_shapes=[
            *pairs,
            pltpu.VMEM((4, 4, 2 * HALF, 128), F32),
            pltpu.VMEM((2, 4, 2 * HALF, 128), F32),
            pltpu.VMEM((2, ROWS, 128), F32),
            pltpu.VMEM((2, ROWS, 128), F32),
            pltpu.VMEM((3, ROWS + 16, 512), F32),
            dma((2, 3)), dma((2,)), dma((2,)), dma((2, 2)), dma((2, 2)), dma((2,)), dma((2,)), dma((2, 3)),
            dma((4, 2)), dma((4, 2)), dma((2,)), dma((2,)), dma((2,)), dma((2,)),
        ],
        compiler_params=pltpu.CompilerParams(has_side_effects=True, vmem_limit_bytes=32 * 1024 * 1024),
        name="substeps",
    )(height, east_wind, north_wind, wave_speed_sq, ring, first, last, fore, back, grid)


def solution(mesh):
    block = P(None, "lat", "lon")
    return jax.shard_map(
        lambda *args: tuple(body(*args)),
        mesh=mesh, in_specs=(block, block, block, P()), out_specs=(block, block, block), check_vma=False,
    )
```

```python
import math

import jax
import jax.numpy as jnp
import ml_dtypes
import numpy as np
from jax import lax
from jax.experimental import pallas as pl
from jax.experimental.pallas import tpu as pltpu
from jax.sharding import PartitionSpec as P

NLON, NLAT = 12288, 1536
ROWS, CELLS = 96, 384
OUTER, INNER = 96, 128
HALF = 56
COURANT, SPIN = 0.45, 0.3
NORTH = COURANT * 2.0 * NLAT / NLON
FINAL = 260
LAST = 264
MESH = pl.DeviceIdType.MESH
F32, BF16 = jnp.float32, jnp.bfloat16
GROUPS = ((0,), (1, 2))


def split(table):
    high = table.astype(ml_dtypes.bfloat16)
    low = (table - high.astype(np.float64)).astype(ml_dtypes.bfloat16)
    return high, low


def tables():
    a = np.array([3 * d + s for s in range(3) for d in range(32)])
    k1 = np.arange(HALF)
    live = (k1 <= OUTER // 2).astype(np.float64)
    angle = 2 * np.pi * ((k1[:, None] * a[None, :]) % OUTER) / OUTER
    first = np.concatenate([np.cos(angle) * live[:, None], -np.sin(angle) * live[:, None]], axis=0)
    weight = live * np.where((k1 == 0) | (k1 == OUTER // 2), 1.0, 2.0) / NLON
    last = np.concatenate([np.cos(angle) * weight[:, None], -np.sin(angle) * weight[:, None]], axis=0).T
    n = np.arange(INNER)
    turn = 2 * np.pi * (k1[:, None] * n[None, :]) / NLON
    inner = 2 * np.pi * ((n[:, None] * n[None, :]) % INNER) / INNER
    cos, sin = np.cos(inner), np.sin(inner)
    forward = np.block([[cos, -sin], [sin, cos]])
    backward = np.block([[cos, sin], [-sin, cos]])
    wave = k1[:, None] + OUTER * n[None, :]
    steep = np.sin(2 * np.pi * wave / NLON) * live[:, None]
    half_sine = np.where(live[:, None] > 0, 0.5 * np.abs(np.sin(np.pi * wave / NLON)), 1.0)
    first_high, first_low = split(first)
    last_high, last_low = split(last)
    forward_high, forward_low = split(forward)
    backward_high, backward_low = split(backward)
    grid = np.stack([np.cos(turn), np.sin(turn), steep, half_sine]).astype(np.float32)
    return (
        np.concatenate([first_high, first_low, first_high], axis=1),
        np.concatenate([last_high, last_low, last_high], axis=1),
        np.stack([forward_high, forward_low]),
        np.stack([backward_high, backward_low]),
        grid,
    )


def parts(value):
    high = value.astype(BF16)
    return high, (value - high.astype(F32)).astype(BF16)


def dot(left, right):
    return jnp.dot(left, right, preferred_element_type=F32)


def outer_step(table, value):
    high, low = parts(value)
    return dot(table.astype(BF16), jnp.concatenate([high, high, low], axis=0))


def inner_step(table, value):
    high, low = parts(value)
    table_high, table_low = table[0].astype(BF16), table[1].astype(BF16)
    return dot(high, table_high) + dot(low, table_high) + dot(high, table_low)


def kernel(
    speed_ref, h_hbm, u_hbm, v_hbm, first_hbm, last_hbm, fore_hbm, back_hbm, grid_hbm,
    h_out, u_out, v_out,
    h_ref, u_ref, v_ref, first_ref, last_ref, fore_ref, back_ref, grid_ref,
    src0, src1, relay0, relay1, recv0, recv1, snd0, snd1, home0, home1, ret0, ret1,
    nb, state, packed, sides, ext,
    loads, send_a, recv_a, send_b, recv_b, send_c, recv_c, send_d, recv_d,
    send_x, recv_x, send_s, recv_s, send_r, recv_r,
):
    fields, outs = (h_ref, u_ref, v_ref), (h_out, u_out, v_out)
    operands = (h_hbm, u_hbm, v_hbm, first_hbm, last_hbm, fore_hbm, back_hbm, grid_hbm)
    held = (h_ref, u_ref, v_ref, first_ref, last_ref, fore_ref, back_ref, grid_ref)
    src, relay, recv = (src0, src1), (relay0, relay1), (recv0, recv1)
    snd, home, ret = (snd0, snd1), (home0, home1), (ret0, ret1)
    lat, lon = lax.axis_index("lat"), lax.axis_index("lon")
    south = lat >= 8
    band = jnp.where(south, 15 - lat, lat)
    core = lax.rem(band, 2)
    x_hi, z = lax.div(lon, 16), lax.rem(lon, 16)
    x = 2 * x_hi + lax.rem(lax.div(band, 2), 2)
    line = jnp.where(band < 4, x, 7 - x)
    place = 2 * z + core
    slab = 16 * core + z
    wide = line >= 6
    double = jnp.logical_and(wide, place >= 28)
    count = jnp.where(double, 2, 1)
    chain = 32 * line + place
    line_rows = jnp.where(wide, 36, 32)
    line_row = place + jnp.where(double, place - 28, 0)
    row0 = 32 * line + jnp.where(line == 7, 4, 0) + line_row
    flip = jnp.where(south, -1.0, 1.0).astype(F32)
    source = band <= 2
    stencil = band >= 2

    def member(to_line, to_z, to_core):
        to_x = jnp.where(to_line < 4, to_line, 7 - to_line)
        to_band = 4 * lax.div(to_line, 4) + 2 * lax.rem(to_x, 2) + to_core
        return jnp.where(south, 15 - to_band, to_band), 16 * lax.div(to_x, 2) + to_z

    def mate(to_place):
        shift = lax.rem(to_place, 2) - core
        return jnp.where(south, lat - shift, lat + shift), 16 * x_hi + lax.div(to_place, 2)

    def around(k, here, total):
        step = lax.div(k + 1, 2)
        return lax.rem(here + total + jnp.where(lax.rem(k, 2) == 1, step, -step), total)

    def send(here, there, send_sem, recv_sem, target):
        same = jnp.logical_and(target[0] == lat, target[1] == lon)

        @pl.when(same)
        def _():
            pltpu.make_async_copy(here, there, recv_sem).start()

        @pl.when(jnp.logical_not(same))
        def _():
            pltpu.make_async_remote_copy(
                src_ref=here, dst_ref=there, send_sem=send_sem, recv_sem=recv_sem, device_id=target, device_id_type=MESH
            ).start()

    def remote(here, there, send_sem, recv_sem, target):
        pltpu.make_async_remote_copy(
            src_ref=here, dst_ref=there, send_sem=send_sem, recv_sem=recv_sem, device_id=target, device_id_type=MESH
        ).start()

    def landed(ref, sem):
        pltpu.make_async_copy(ref, ref, sem).wait()

    def each_size(act):
        pl.when(jnp.logical_not(wide))(lambda: act(32))
        pl.when(wide)(lambda: act(36))

    def line_start(k, size):
        return jnp.where(south, ROWS - size * (k + 1), size * k)

    def turned(row):
        return jnp.where(south, line_rows - 1 - row, row)

    right = jnp.where(lon == 31, 0, lon + 1)
    left = jnp.where(lon == 0, 31, lon - 1)
    up_line, up_place = lax.div(chain + 31, 32) - 1, lax.rem(chain + 31, 32)
    up = member(up_line, lax.div(up_place, 2), lax.rem(up_place, 2))
    up_count = jnp.where(jnp.logical_and(up_line >= 6, up_place >= 28), 2, 1)
    down_place = lax.rem(chain + 1, 32)
    down = member(lax.div(chain + 1, 32), lax.div(down_place, 2), lax.rem(down_place, 2))
    to_band = jnp.where(wide, 2, lax.div(line, 3))
    to_lat = jnp.where(south, 15 - to_band, to_band)
    nth = line - 3 * to_band

    barrier = pltpu.get_barrier_semaphore()

    def greet(target):
        pl.semaphore_signal(barrier, inc=1, device_id=target, device_id_type=MESH)

    def greet_other(target):
        other = jnp.logical_not(jnp.logical_and(target[0] == lat, target[1] == lon))
        pl.when(other)(lambda: greet(target))
        return other.astype(jnp.int32)

    def greet_mate(k, carry):
        greet(mate(lax.rem(place + k, 32)))
        return carry

    greeted = 31 + greet_other((to_lat, slab))
    for k in range(3):
        target = member(jnp.minimum(3 * band + k, 7), z, x_hi)
        other = jnp.logical_not(jnp.logical_and(target[0] == lat, target[1] == lon))
        meant = jnp.logical_and(other, jnp.logical_or(band < 2, jnp.logical_and(band == 2, k < 2)))
        pl.when(meant)(lambda target=target: greet(target))
        greeted += meant.astype(jnp.int32)
    for meant, target in (
        (chain > 0, up), (chain < 255, down), (stencil, (lat, left)), (stencil, (lat, right)),
        (jnp.logical_and(stencil, lat > 2), (lat - 1, lon)), (jnp.logical_and(stencil, lat < 13), (lat + 1, lon)),
    ):
        pl.when(meant)(lambda target=target: greet(target))
        greeted += meant.astype(jnp.int32)
    lax.fori_loop(1, 32, greet_mate, 0)

    for index, (there, here) in enumerate(zip(operands, held)):
        pltpu.make_async_copy(there, here, loads.at[index]).start()

    def loaded(*indices):
        for index in indices:
            pltpu.make_async_copy(operands[index], held[index], loads.at[index]).wait()

    def gather_lines(g):
        per = 3 * len(GROUPS[g])
        for pos, f in enumerate(GROUPS[g]):
            for s in range(3):
                src[g][pl.ds(3 * pos + s, ROWS, stride=per), :] = fields[f][0, :, 128 * s : 128 * (s + 1)]

    def send_lines(g):
        per = 3 * len(GROUPS[g])

        def to_line(k, size):
            start = line_start(k, size)
            send(
                src[g].at[pl.ds(start * per, size * per)], relay[g].at[pl.ds(0, size * per)],
                send_a.at[g, k], recv_a.at[g], member(3 * band + k, z, x_hi),
            )

        @pl.when(band < 2)
        def _():
            for k in range(3):
                to_line(k, 32)

        @pl.when(band == 2)
        def _():
            for k in range(2):
                to_line(k, 36)

    loaded(0)
    pl.when(source)(lambda: gather_lines(0))
    pl.semaphore_wait(barrier, greeted)
    pl.when(source)(lambda: send_lines(0))
    loaded(1, 2)

    @pl.when(source)
    def _():
        gather_lines(1)
        send_lines(1)

    @pl.when(stencil)
    def _():
        lane = lax.broadcasted_iota(jnp.int32, (ROWS, 128), 1)
        high = [ref[0, :, 256:384] for ref in fields]
        low = [ref[0, :, 0:128] for ref in fields]
        packed[0] = jnp.where(
            lane >= 124, high[0], jnp.where(lane >= 120, pltpu.roll(high[1], 124, 1), pltpu.roll(high[2], 120, 1))
        )
        packed[1] = jnp.where(lane < 4, low[0], jnp.where(lane < 8, pltpu.roll(low[1], 4, 1), pltpu.roll(low[2], 8, 1)))
        remote(packed.at[0], sides.at[0], send_s.at[0], recv_s.at[0], (lat, right))
        remote(packed.at[1], sides.at[1], send_s.at[1], recv_s.at[1], (lat, left))

    def owner(row):
        late = jnp.logical_and(wide, row >= 28)
        return jnp.where(late, 28 + lax.div(row - 28, 2), row), jnp.where(late, lax.rem(row, 2), 0)

    for g in range(2):
        per = 3 * len(GROUPS[g])
        each_size(lambda size, g=g, per=per: landed(relay[g].at[pl.ds(0, size * per)], recv_a.at[g]))

        def spread(k, carry, g=g, per=per):
            row = around(k, line_row, line_rows)
            to, slot = owner(row)
            send(
                relay[g].at[pl.ds(turned(row) * per, per)], recv[g].at[pl.ds((32 * slot + slab) * per, per)],
                send_b.at[g], recv_b.at[g, slot], mate(to),
            )
            return carry

        def spread_one(k, carry, g=g, per=per):
            to = around(k, place, 32)
            remote(
                relay[g].at[pl.ds(turned(to) * per, per)], recv[g].at[pl.ds(slab * per, per)],
                send_b.at[g], recv_b.at[g, 0], mate(to),
            )
            return carry

        @pl.when(wide)
        def _(spread=spread):
            lax.fori_loop(0, 36, spread, 0)

        @pl.when(jnp.logical_not(wide))
        def _(g=g, per=per, spread_one=spread_one):
            pltpu.make_async_copy(
                relay[g].at[pl.ds(turned(place) * per, per)], recv[g].at[pl.ds(slab * per, per)], recv_b.at[g, 0]
            ).start()
            lax.fori_loop(1, 32, spread_one, 0)

    @pl.when(stencil)
    def _():
        landed(sides.at[0], recv_s.at[0])
        landed(sides.at[1], recv_s.at[1])
        lane = lax.broadcasted_iota(jnp.int32, (ROWS, 128), 1)
        for f in range(3):
            ext[f, 8 : 8 + ROWS, 0:CELLS] = fields[f][0]
            after, before = sides[1], sides[0]
            if f:
                after, before = pltpu.roll(after, 128 - 4 * f, 1), pltpu.roll(before, 4 * f, 1)
            ext[f, 8 : 8 + ROWS, CELLS : CELLS + 128] = jnp.where(lane < 64, after, before)

        @pl.when(lat > 2)
        def _():
            remote(ext.at[:, 8:16, :], ext.at[:, 104:112, :], send_r.at[0], recv_r.at[0], (lat - 1, lon))

        @pl.when(lat < 13)
        def _():
            remote(ext.at[:, 96:104, :], ext.at[:, 0:8, :], send_r.at[1], recv_r.at[1], (lat + 1, lon))

        @pl.when(lat == 2)
        def _():
            ext[:, 0:8, :] = jnp.zeros((3, 8, 512), F32)

        @pl.when(lat == 13)
        def _():
            ext[:, 104:112, :] = jnp.zeros((3, 8, 512), F32)

    loaded(3, 4, 5, 6, 7)
    speed = speed_ref[0]

    def each_slot(act):
        act(0)
        pl.when(double)(lambda: act(1))

    @pl.when(chain == 0)
    def _():
        for e in range(4):
            nb[e, 0] = jnp.zeros((2 * HALF, 128), F32)

    @pl.when(chain == 255)
    def _():
        for e in range(4):
            nb[e, 3] = jnp.zeros((2 * HALF, 128), F32)

    def trade(e):
        @pl.when(chain > 0)
        def _():
            remote(nb.at[e, 1], nb.at[e, up_count + 1], send_x.at[e, 0], recv_x.at[e, 1], up)

        @pl.when(chain < 255)
        def _():
            remote(nb.at[e, count], nb.at[e, 0], send_x.at[e, 1], recv_x.at[e, 0], down)

    def traded(e):
        @pl.when(chain > 0)
        def _():
            landed(nb.at[e, 0], recv_x.at[e, 0])

        @pl.when(chain < 255)
        def _():
            landed(nb.at[e, count + 1], recv_x.at[e, 1])

    def transform(g, slot):
        per = 3 * len(GROUPS[g])
        grids = []
        for pos in range(len(GROUPS[g])):
            start = 32 * per * slot + 3 * pos
            grids.append(jnp.concatenate([recv[g][pl.ds(start + s, 32, stride=per), :] for s in range(3)], axis=0))
        mixed = outer_step(first_ref[...], jnp.concatenate(grids, axis=1))
        cos, sin = grid_ref[0], grid_ref[1]
        turned_rows = []
        for pos in range(len(GROUPS[g])):
            real, imag = mixed[:HALF, 128 * pos : 128 * (pos + 1)], mixed[HALF:, 128 * pos : 128 * (pos + 1)]
            turned_rows.append(jnp.concatenate([real * cos + imag * sin, imag * cos - real * sin], axis=1))
        spectrum = inner_step(fore_ref, jnp.concatenate(turned_rows, axis=0))
        return [
            (spectrum[HALF * pos : HALF * (pos + 1), :128], spectrum[HALF * pos : HALF * (pos + 1), 128:])
            for pos in range(len(GROUPS[g]))
        ]

    def restore(g, slot, spectra):
        per = 3 * len(GROUPS[g])
        cos, sin = grid_ref[0], grid_ref[1]
        back = inner_step(back_ref, jnp.concatenate([jnp.concatenate(pair, axis=1) for pair in spectra], axis=0))
        spun = []
        for pos in range(len(GROUPS[g])):
            real, imag = back[HALF * pos : HALF * (pos + 1), :128], back[HALF * pos : HALF * (pos + 1), 128:]
            spun.append(jnp.concatenate([real * cos - imag * sin, imag * cos + real * sin], axis=0))
        rows = outer_step(last_ref[...], jnp.concatenate(spun, axis=1))
        for pos in range(len(GROUPS[g])):
            for s in range(3):
                snd[g][pl.ds(32 * per * slot + 3 * pos + s, 32, stride=per), :] = rows[
                    32 * s : 32 * (s + 1), 128 * pos : 128 * (pos + 1)
                ]

    def put(ref, index, pair):
        ref[(*index, slice(0, HALF))] = pair[0]
        ref[(*index, slice(HALF, 2 * HALF))] = pair[1]

    def get(ref, *index):
        return ref[(*index, slice(0, HALF))], ref[(*index, slice(HALF, 2 * HALF))]

    def polar(row):
        return (jnp.full((1, 128), row, jnp.int32).astype(F32) + 0.5) * (math.pi / NLAT)

    def factors(slot):
        angle = polar(row0 + slot)
        cosine = jnp.sin(angle)
        share = 1.0 / jnp.maximum(grid_ref[3], cosine)
        return share, share * cosine, -SPIN * jnp.cos(angle)

    def push_east(slot, height, east, north):
        share, keep, spin = factors(slot)
        slope, swirl = share * (COURANT * grid_ref[2]), keep * spin
        return (
            east[0] + slope * height[1] + swirl * north[0],
            east[1] - slope * height[0] + swirl * north[1],
        )

    def push_north(slot, above, below, east, north):
        _, keep, spin = factors(slot)
        return tuple(
            north[p] - keep * ((0.5 * NORTH) * (below[p] - above[p]) + spin * east[p]) for p in range(2)
        )

    def push_height(slot, above, below, east, height):
        share, _, _ = factors(slot)
        share = speed * share
        slope = share * (COURANT * grid_ref[2])
        fall = share * (0.5 * NORTH)
        higher, lower = jnp.sin(polar(row0 + slot - 1)), jnp.sin(polar(row0 + slot + 1))
        return (
            height[0] + slope * east[1] - fall * (lower * below[0] - higher * above[0]),
            height[1] - slope * east[0] - fall * (lower * below[1] - higher * above[1]),
        )

    def first_height(slot):
        landed(recv[0].at[pl.ds(96 * slot, 96)], recv_b.at[0, slot])
        put(nb, (0, slot + 1), transform(0, slot)[0])

    def first_winds(slot):
        landed(recv[1].at[pl.ds(192 * slot, 192)], recv_b.at[1, slot])
        east, north = transform(1, slot)
        put(state, (slot, 0), east)
        put(state, (slot, 1), (flip * north[0], flip * north[1]))

    def north_one(slot):
        put(
            nb, (1, slot + 1),
            push_north(slot, get(nb, 0, slot), get(nb, 0, slot + 2), get(state, slot, 0), get(state, slot, 1)),
        )

    def east_one(slot):
        put(state, (slot, 2), push_east(slot, get(nb, 0, slot + 1), get(state, slot, 0), get(state, slot, 1)))

    def height_one(slot):
        put(
            nb, (2, slot + 1),
            push_height(slot, get(nb, 1, slot), get(nb, 1, slot + 2), get(state, slot, 2), get(nb, 0, slot + 1)),
        )

    def east_two(slot):
        put(state, (slot, 3), push_east(slot, get(nb, 2, slot + 1), get(state, slot, 2), get(nb, 1, slot + 1)))

    def north_two(slot):
        put(
            nb, (3, slot + 1),
            push_north(slot, get(nb, 2, slot), get(nb, 2, slot + 2), get(state, slot, 2), get(nb, 1, slot + 1)),
        )

    def winds_back(slot):
        north = get(nb, 3, slot + 1)
        restore(1, slot, [get(state, slot, 3), (flip * north[0], flip * north[1])])

    def height_back(slot):
        height = push_height(slot, get(nb, 3, slot), get(nb, 3, slot + 2), get(state, slot, 3), get(nb, 2, slot + 1))
        restore(0, slot, [height])

    def return_pieces(g, slot):
        per = 3 * len(GROUPS[g])
        row = turned(line_row + slot)

        def piece(k, carry):
            to = around(k, place, 32)
            d = 16 * lax.rem(to, 2) + lax.div(to, 2)
            remote(
                snd[g].at[pl.ds((32 * slot + d) * per, per)], home[g].at[pl.ds(row * per, per)],
                send_c.at[g, slot], recv_c.at[g], mate(to),
            )
            return carry

        pltpu.make_async_copy(
            snd[g].at[pl.ds((32 * slot + slab) * per, per)], home[g].at[pl.ds(row * per, per)], recv_c.at[g]
        ).start()
        lax.fori_loop(1, 32, piece, 0)

    each_slot(first_height)
    trade(0)
    each_slot(first_winds)
    traded(0)
    each_slot(north_one)
    trade(1)
    each_slot(east_one)
    traded(1)
    each_slot(height_one)
    trade(2)
    each_slot(east_two)
    traded(2)
    each_slot(north_two)
    trade(3)
    each_slot(winds_back)
    each_slot(lambda slot: return_pieces(1, slot))
    traded(3)
    each_slot(height_back)
    each_slot(lambda slot: return_pieces(0, slot))

    for g in (1, 0):
        per = 3 * len(GROUPS[g])

        def deliver(size, g=g, per=per):
            landed(home[g].at[pl.ds(0, size * per)], recv_c.at[g])
            start = line_start(nth, size)
            send(
                home[g].at[pl.ds(0, size * per)], ret[g].at[pl.ds(start * per, size * per)],
                send_d.at[g], recv_d.at[g, nth], (to_lat, slab),
            )

        each_size(deliver)

    @pl.when(stencil)
    def _():
        @pl.when(lat > 2)
        def _():
            landed(ext.at[:, 0:8, :], recv_r.at[1])

        @pl.when(lat < 13)
        def _():
            landed(ext.at[:, 104:112, :], recv_r.at[0])

        row = lax.broadcasted_iota(jnp.int32, (ROWS + 16, 128), 0) + (ROWS * lat - 8)
        latitude = (row.astype(F32) + (0.5 - NLAT // 2)) * (math.pi / NLAT)
        wide_cos = jnp.concatenate([jnp.cos(latitude)] * 4, axis=1)
        spin = jnp.concatenate([SPIN * jnp.sin(latitude)] * 4, axis=1)
        inverse = 1.0 / wide_cos
        east_scale = (0.5 * COURANT) * inverse

        def across(value):
            return pltpu.roll(value, 511, 1) - pltpu.roll(value, 1, 1)

        def along(value):
            return pltpu.roll(value, ROWS + 15, 0) - pltpu.roll(value, 1, 0)

        height, east, north = ext[0], ext[1], ext[2]
        for _step in range(2):
            east_inc = spin * north - east_scale * across(height)
            north_inc = (-0.5 * NORTH) * along(height) - spin * east
            east, north = east + east_inc, north + north_inc
            spread_out = east_scale * across(east) + (0.5 * NORTH) * inverse * along(north * wide_cos)
            height = height - speed * spread_out
        for out, value in zip(outs, (height, east, north)):
            out[0] = value[8 : 8 + ROWS, 0:CELLS]

    def arrived(k, size):
        for g in range(2):
            per = 3 * len(GROUPS[g])
            landed(ret[g].at[pl.ds(line_start(k, size) * per, size * per)], recv_d.at[g, k])

    def back(f, s):
        g = 0 if f == 0 else 1
        per, pos = 3 * len(GROUPS[g]), GROUPS[g].index(f)
        return ret[g][pl.ds(3 * pos + s, ROWS, stride=per), :]

    @pl.when(band < 2)
    def _():
        for k in range(3):
            arrived(k, 32)
        for f in range(3):
            for s in range(3):
                outs[f][0, :, 128 * s : 128 * (s + 1)] = back(f, s)

    @pl.when(band == 2)
    def _():
        for k in range(2):
            arrived(k, 36)
        row = lax.broadcasted_iota(jnp.int32, (ROWS, 128), 0)
        from_pole = jnp.where(south, ROWS - 1 - row, row) + 2 * ROWS
        for f in range(3):
            for s in range(3):
                lanes = slice(128 * s, 128 * (s + 1))
                outs[f][0, :, lanes] = jnp.where(from_pole < FINAL, back(f, s), outs[f][0, :, lanes])

    for g in range(2):
        per = 3 * len(GROUPS[g])

        def left_lines(size, lines, g=g, per=per):
            for k in range(lines):
                to = member(3 * band + k, z, x_hi)

                @pl.when(jnp.logical_not(jnp.logical_and(to[0] == lat, to[1] == lon)))
                def _(k=k):
                    landed(src[g].at[pl.ds(0, size * per)], send_a.at[g, k])

        pl.when(band < 2)(lambda f=left_lines: f(32, 3))
        pl.when(band == 2)(lambda f=left_lines: f(36, 2))

        pl.when(jnp.logical_not(wide))(lambda g=g, per=per: landed(relay[g].at[pl.ds(0, 31 * per)], send_b.at[g]))
        pl.when(jnp.logical_and(wide, jnp.logical_not(double)))(
            lambda g=g, per=per: landed(relay[g].at[pl.ds(0, 35 * per)], send_b.at[g])
        )
        pl.when(double)(lambda g=g, per=per: landed(relay[g].at[pl.ds(0, 34 * per)], send_b.at[g]))
        each_slot(lambda slot, g=g, per=per: landed(snd[g].at[pl.ds(0, 31 * per)], send_c.at[g, slot]))

        @pl.when(jnp.logical_not(jnp.logical_and(to_lat == lat, slab == lon)))
        def _(g=g, per=per):
            each_size(lambda size: landed(home[g].at[pl.ds(0, size * per)], send_d.at[g]))

    @pl.when(stencil)
    def _():
        for side in range(2):
            landed(packed.at[side], send_s.at[side])

        @pl.when(lat > 2)
        def _():
            landed(ext.at[:, 8:16, :], send_r.at[0])

        @pl.when(lat < 13)
        def _():
            landed(ext.at[:, 96:104, :], send_r.at[1])

    for e in range(4):
        pl.when(chain > 0)(lambda e=e: landed(nb.at[e, 1], send_x.at[e, 0]))
        pl.when(chain < 255)(lambda e=e: landed(nb.at[e, 1], send_x.at[e, 1]))


def body(height, east_wind, north_wind, wave_speed_sq):
    constants = [np.asarray(table, np.float32) for table in tables()]
    block = jax.ShapeDtypeStruct((1, ROWS, CELLS), F32)
    pairs = []
    for rows in (ROWS, 36, 64, 64, 36, ROWS):
        pairs += [pltpu.VMEM((rows * 3 * len(group), 128), F32) for group in GROUPS]
    dma = pltpu.SemaphoreType.DMA
    return pl.pallas_call(
        kernel,
        out_shape=[block] * 3,
        in_specs=[pl.BlockSpec(memory_space=pltpu.SMEM)] + [pl.BlockSpec(memory_space=pl.ANY)] * 8,
        out_specs=[pl.BlockSpec(memory_space=pltpu.VMEM)] * 3,
        scratch_shapes=[
            *[pltpu.VMEM((1, ROWS, CELLS), F32)] * 3,
            *[pltpu.VMEM(table.shape, table.dtype) for table in constants],
            *pairs,
            pltpu.VMEM((4, 4, 2 * HALF, 128), F32),
            pltpu.VMEM((2, 4, 2 * HALF, 128), F32),
            pltpu.VMEM((2, ROWS, 128), F32),
            pltpu.VMEM((2, ROWS, 128), F32),
            pltpu.VMEM((3, ROWS + 16, 512), F32),
            dma((8,)), dma((2, 3)), dma((2,)), dma((2,)), dma((2, 2)), dma((2, 2)), dma((2,)), dma((2,)), dma((2, 3)),
            dma((4, 2)), dma((4, 2)), dma((2,)), dma((2,)), dma((2,)), dma((2,)),
        ],
        compiler_params=pltpu.CompilerParams(
            collective_id=0, has_side_effects=True, vmem_limit_bytes=60 * 1024 * 1024
        ),
        name="substeps",
    )(wave_speed_sq, height, east_wind, north_wind, *constants)


def solution(mesh):
    block = P(None, "lat", "lon")
    return jax.shard_map(
        lambda *args: tuple(body(*args)),
        mesh=mesh, in_specs=(block, block, block, P()), out_specs=(block, block, block), check_vma=False,
    )
```

```python
import math

import jax
import jax.numpy as jnp
import ml_dtypes
import numpy as np
from jax import lax
from jax.experimental import pallas as pl
from jax.experimental.pallas import tpu as pltpu
from jax.sharding import PartitionSpec as P

NLON, NLAT = 12288, 1536
ROWS, CELLS = 96, 384
OUTER, INNER = 96, 128
HALF = 56
COURANT, SPIN = 0.45, 0.3
NORTH = COURANT * 2.0 * NLAT / NLON
FINAL = 260
HOLD = 3
OWNERS = 88
WINGS = HOLD + 2
MESH = pl.DeviceIdType.MESH
F32, BF16 = jnp.float32, jnp.bfloat16
GROUPS = ((0,), (1, 2))


def split(table):
    high = table.astype(ml_dtypes.bfloat16)
    low = (table - high.astype(np.float64)).astype(ml_dtypes.bfloat16)
    return high, low


def tables():
    a = np.array([3 * d + s for s in range(3) for d in range(32)])
    k1 = np.arange(HALF)
    live = (k1 <= OUTER // 2).astype(np.float64)
    angle = 2 * np.pi * ((k1[:, None] * a[None, :]) % OUTER) / OUTER
    first = np.concatenate([np.cos(angle) * live[:, None], -np.sin(angle) * live[:, None]], axis=0)
    weight = live * np.where((k1 == 0) | (k1 == OUTER // 2), 1.0, 2.0) / NLON
    last = np.concatenate([np.cos(angle) * weight[:, None], -np.sin(angle) * weight[:, None]], axis=0).T
    n = np.arange(INNER)
    turn = 2 * np.pi * (k1[:, None] * n[None, :]) / NLON
    inner = 2 * np.pi * ((n[:, None] * n[None, :]) % INNER) / INNER
    cos, sin = np.cos(inner), np.sin(inner)
    forward = np.block([[cos, -sin], [sin, cos]])
    backward = np.block([[cos, sin], [-sin, cos]])
    wave = k1[:, None] + OUTER * n[None, :]
    steep = np.sin(2 * np.pi * wave / NLON) * live[:, None]
    half_sine = np.where(live[:, None] > 0, 0.5 * np.abs(np.sin(np.pi * wave / NLON)), 1.0)
    first_high, first_low = split(first)
    last_high, last_low = split(last)
    forward_high, forward_low = split(forward)
    backward_high, backward_low = split(backward)
    grid = np.stack([np.cos(turn), np.sin(turn), steep, half_sine]).astype(np.float32)
    return (
        np.concatenate([first_high, first_low, first_high], axis=1),
        np.concatenate([last_high, last_low, last_high], axis=1),
        np.stack([forward_high, forward_low]),
        np.stack([backward_high, backward_low]),
        grid,
    )


def parts(value):
    high = value.astype(BF16)
    return high, (value - high.astype(F32)).astype(BF16)


def dot(left, right):
    return jnp.dot(left, right, preferred_element_type=F32)


def outer_step(table, value):
    high, low = parts(value)
    return dot(table.astype(BF16), jnp.concatenate([high, high, low], axis=0))


def inner_step(table, value):
    high, low = parts(value)
    table_high, table_low = table[0].astype(BF16), table[1].astype(BF16)
    return dot(high, table_high) + dot(low, table_high) + dot(high, table_low)


def kernel(
    speed_ref, h_hbm, u_hbm, v_hbm, first_hbm, last_hbm, fore_hbm, back_hbm, grid_hbm,
    h_out, u_out, v_out,
    h_ref, u_ref, v_ref, first_ref, last_ref, fore_ref, back_ref, grid_ref,
    src0, src1, recv0, recv1, snd0, snd1, ret0, ret1,
    tall, tall_new, wind, wind_new, wind_last, scale, packed, sides, ext,
    loads, send_a, recv_a, send_c, recv_c, send_x, recv_x, send_s, recv_s, send_r, recv_r,
):
    fields, outs = (h_ref, u_ref, v_ref), (h_out, u_out, v_out)
    operands = (h_hbm, u_hbm, v_hbm, first_hbm, last_hbm, fore_hbm, back_hbm, grid_hbm)
    held = (h_ref, u_ref, v_ref, first_ref, last_ref, fore_ref, back_ref, grid_ref)
    src, recv, snd, ret = (src0, src1), (recv0, recv1), (snd0, snd1), (ret0, ret1)
    lat, lon = lax.axis_index("lat"), lax.axis_index("lon")
    south = lat >= 8
    band = jnp.where(south, 15 - lat, lat)
    core = lax.rem(band, 2)
    z = lax.rem(lon, 16)
    x = 2 * lax.div(lon, 16) + lax.rem(lax.div(band, 2), 2)
    line = jnp.where(band < 4, x, 7 - x)
    step = lax.rem(z + line, 16) + jnp.where(lax.rem(z + line, 16) < lax.rem(10 * line + line, 16), 16, 0)
    nth = step - lax.rem(11 * line, 16)
    owner = jnp.logical_and(core == 1, nth < 11)
    chain = 11 * line + nth
    source = band <= 2
    stencil = band >= 2
    partners = jnp.where(band < 2, 32, 24)
    my_band = jnp.minimum(lax.div(chain, 32), 2)
    my_lat = jnp.where(south, 15 - my_band, my_band)

    def holder(n):
        to_line = lax.div(n, 11)
        to_x = jnp.where(to_line < 4, to_line, 7 - to_line)
        to_band = 4 * lax.div(to_line, 4) + 2 * lax.rem(to_x, 2) + 1
        return jnp.where(south, 15 - to_band, to_band), 16 * lax.div(to_x, 2) + lax.rem(n + 16 - to_line, 16)

    def same(target):
        return jnp.logical_and(target[0] == lat, target[1] == lon)

    def remote(here, there, send_sem, recv_sem, target):
        pltpu.make_async_remote_copy(
            src_ref=here, dst_ref=there, send_sem=send_sem, recv_sem=recv_sem, device_id=target, device_id_type=MESH
        ).start()

    def send(here, there, send_sem, recv_sem, target):
        own = same(target)

        @pl.when(own)
        def _():
            pltpu.make_async_copy(here, there, recv_sem).start()

        @pl.when(jnp.logical_not(own))
        def _():
            remote(here, there, send_sem, recv_sem, target)

    def landed(ref, sem):
        pltpu.make_async_copy(ref, ref, sem).wait()

    def first_row(i):
        return jnp.where(south, ROWS - HOLD - HOLD * i, HOLD * i)

    right = jnp.where(lon == 31, 0, lon + 1)
    left = jnp.where(lon == 0, 31, lon - 1)
    before = chain + jnp.where(south, 1, -1)
    after = chain + jnp.where(south, -1, 1)
    has_before = jnp.logical_and(owner, jnp.logical_and(before >= 0, before < OWNERS))
    has_after = jnp.logical_and(owner, jnp.logical_and(after >= 0, after < OWNERS))
    before_device, after_device = holder(jnp.maximum(before, 0)), holder(jnp.maximum(after, 0))

    barrier = pltpu.get_barrier_semaphore()

    def greet(target):
        pl.semaphore_signal(barrier, inc=1, device_id=target, device_id_type=MESH)

    def greet_other(target):
        pl.when(jnp.logical_not(same(target)))(lambda: greet(target))

    def target_of(k):
        return lax.rem(lon + k, partners)

    def greet_holder(k, carry):
        greet_other(holder(32 * band + k))
        return carry

    def greet_source(k, carry):
        greet_other((my_lat, k))
        return carry

    @pl.when(owner)
    def _():
        lax.fori_loop(0, 32, greet_source, 0)

    @pl.when(source)
    def _():
        lax.fori_loop(0, partners, greet_holder, 0)

    own_rows = jnp.logical_and(jnp.logical_and(owner, source), my_band == band)
    greeted = jnp.where(owner, 32, 0) + jnp.where(source, partners, 0) - jnp.where(own_rows, 2, 0)
    for meant, target in (
        (has_before, before_device), (has_after, after_device), (stencil, (lat, left)), (stencil, (lat, right)),
        (jnp.logical_and(stencil, lat > 2), (lat - 1, lon)), (jnp.logical_and(stencil, lat < 13), (lat + 1, lon)),
    ):
        pl.when(meant)(lambda target=target: greet(target))
        greeted += meant.astype(jnp.int32)

    def load(*indices):
        for index in indices:
            pltpu.make_async_copy(operands[index], held[index], loads.at[index]).start()

    def loaded(*indices):
        for index in indices:
            pltpu.make_async_copy(operands[index], held[index], loads.at[index]).wait()

    load(0, 1, 2)
    pl.when(owner)(lambda: load(3, 4, 5, 6, 7))

    def gather(g):
        per = 3 * len(GROUPS[g])
        for pos, f in enumerate(GROUPS[g]):
            for s in range(3):
                src[g][pl.ds(3 * pos + s, ROWS, stride=per), :] = fields[f][0, :, 128 * s : 128 * (s + 1)]

    def send_rows(g):
        size = HOLD * 3 * len(GROUPS[g])

        def one(k, carry):
            i = target_of(k)
            send(
                src[g].at[pl.ds(first_row(i) * (size // HOLD), size)], recv[g].at[pl.ds(lon * size, size)],
                send_a.at[g], recv_a.at[g], holder(32 * band + i),
            )
            return carry

        lax.fori_loop(0, partners, one, 0)

    loaded(0)
    pl.when(source)(lambda: gather(0))
    pl.semaphore_wait(barrier, greeted)
    pl.when(source)(lambda: send_rows(0))
    loaded(1, 2)

    @pl.when(source)
    def _():
        gather(1)
        send_rows(1)

    @pl.when(stencil)
    def _():
        lane = lax.broadcasted_iota(jnp.int32, (ROWS, 128), 1)
        high = [ref[0, :, 256:384] for ref in fields]
        low = [ref[0, :, 0:128] for ref in fields]
        packed[0] = jnp.where(
            lane >= 124, high[0], jnp.where(lane >= 120, pltpu.roll(high[1], 124, 1), pltpu.roll(high[2], 120, 1))
        )
        packed[1] = jnp.where(lane < 4, low[0], jnp.where(lane < 8, pltpu.roll(low[1], 4, 1), pltpu.roll(low[2], 8, 1)))
        remote(packed.at[0], sides.at[0], send_s.at[0], recv_s.at[0], (lat, right))
        remote(packed.at[1], sides.at[1], send_s.at[1], recv_s.at[1], (lat, left))

    @pl.when(stencil)
    def _():
        landed(sides.at[0], recv_s.at[0])
        landed(sides.at[1], recv_s.at[1])
        lane = lax.broadcasted_iota(jnp.int32, (ROWS, 128), 1)
        for f in range(3):
            ext[f, 8 : 8 + ROWS, 0:CELLS] = fields[f][0]
            east_side, west_side = sides[1], sides[0]
            if f:
                east_side, west_side = pltpu.roll(east_side, 128 - 4 * f, 1), pltpu.roll(west_side, 4 * f, 1)
            ext[f, 8 : 8 + ROWS, CELLS : CELLS + 128] = jnp.where(lane < 64, east_side, west_side)

        @pl.when(lat > 2)
        def _():
            remote(ext.at[:, 8:16, :], ext.at[:, 104:112, :], send_r.at[0], recv_r.at[0], (lat - 1, lon))

        @pl.when(lat < 13)
        def _():
            remote(ext.at[:, 96:104, :], ext.at[:, 0:8, :], send_r.at[1], recv_r.at[1], (lat + 1, lon))

        @pl.when(lat == 2)
        def _():
            ext[:, 0:8, :] = jnp.zeros((3, 8, 512), F32)

        @pl.when(lat == 13)
        def _():
            ext[:, 104:112, :] = jnp.zeros((3, 8, 512), F32)

    def transform(g):
        size = HOLD * 3 * len(GROUPS[g])
        order = [(row, pos) for row in range(HOLD) for pos in range(len(GROUPS[g]))]
        grids = [
            jnp.concatenate(
                [recv[g][pl.ds(row * (size // HOLD) + 3 * pos + s, 32, stride=size), :] for s in range(3)], axis=0
            )
            for row, pos in order
        ]
        mixed = outer_step(first_ref[...], jnp.concatenate(grids, axis=1))
        cos, sin = grid_ref[0], grid_ref[1]
        twisted = []
        for n in range(len(order)):
            real, imag = mixed[:HALF, 128 * n : 128 * (n + 1)], mixed[HALF:, 128 * n : 128 * (n + 1)]
            twisted.append(jnp.concatenate([real * cos + imag * sin, imag * cos - real * sin], axis=1))
        spectrum = inner_step(fore_ref, jnp.concatenate(twisted, axis=0))
        return {
            key: (spectrum[HALF * n : HALF * (n + 1), :128], spectrum[HALF * n : HALF * (n + 1), 128:])
            for n, key in enumerate(order)
        }

    def restore(g, spectra):
        size = HOLD * 3 * len(GROUPS[g])
        order = list(spectra)
        cos, sin = grid_ref[0], grid_ref[1]
        back = inner_step(
            back_ref, jnp.concatenate([jnp.concatenate(spectra[key], axis=1) for key in order], axis=0)
        )
        spun = []
        for n in range(len(order)):
            real, imag = back[HALF * n : HALF * (n + 1), :128], back[HALF * n : HALF * (n + 1), 128:]
            spun.append(jnp.concatenate([real * cos - imag * sin, imag * cos + real * sin], axis=0))
        cells = outer_step(last_ref[...], jnp.concatenate(spun, axis=1))
        for n, (row, pos) in enumerate(order):
            for s in range(3):
                snd[g][pl.ds(row * (size // HOLD) + 3 * pos + s, 32, stride=size), :] = cells[
                    32 * s : 32 * (s + 1), 128 * n : 128 * (n + 1)
                ]

    def put(ref, index, pair):
        ref[(*index, slice(0, HALF))] = pair[0]
        ref[(*index, slice(HALF, 2 * HALF))] = pair[1]

    def get(ref, *index):
        return ref[(*index, slice(0, HALF))], ref[(*index, slice(HALF, 2 * HALF))]

    row0 = jnp.where(south, NLAT - HOLD - HOLD * chain, HOLD * chain)

    def polar(row):
        steps = jnp.where(south, NLAT - 1 - row, row)
        return jnp.abs(jnp.full((1, 128), steps, jnp.int32).astype(F32) + 0.5) * (math.pi / NLAT)

    def cosine(w):
        return jnp.sin(polar(row0 + w - 1))

    def prepare():
        speed = speed_ref[0]
        share_of_pole = jnp.where(south, SPIN, -SPIN).astype(F32)
        for w in range(WINGS):
            there = 1.0
            if w == 0:
                there = jnp.where(has_before, 1.0, 0.0).astype(F32)
            if w == WINGS - 1:
                there = jnp.where(has_after, 1.0, 0.0).astype(F32)
            angle = polar(row0 + w - 1)
            share = 1.0 / jnp.maximum(grid_ref[3], jnp.sin(angle))
            keep = share * (jnp.sin(angle) * there)
            slope = share * (COURANT * grid_ref[2])
            scale[w, 0] = slope
            scale[w, 1] = keep * (share_of_pole * jnp.cos(angle))
            scale[w, 2] = keep * (0.5 * NORTH)
            if 0 < w < WINGS - 1:
                scale[w, 3] = speed * slope
                scale[w, 4] = share * (speed * (0.5 * NORTH) * cosine(w - 1))
                scale[w, 5] = share * (speed * (0.5 * NORTH) * cosine(w + 1))

    def push_winds(heights, old, new, w):
        low, mid, high = get(heights, w), get(heights, w + 1), get(heights, w + 2)
        east, north = get(old, w, 0), get(old, w, 1)
        slope, swirl, climb = scale[w, 0], scale[w, 1], scale[w, 2]
        put(new, (w, 0), (
            east[0] + slope * mid[1] + swirl * north[0],
            east[1] - slope * mid[0] + swirl * north[1],
        ))
        put(new, (w, 1), tuple(north[p] - climb * (high[p] - low[p]) - swirl * east[p] for p in range(2)))

    def pushed_height(heights, winds, w):
        mid, east = get(heights, w + 1), get(winds, w, 0)
        low, high = get(winds, w - 1, 1), get(winds, w + 1, 1)
        slope, below, above = scale[w, 3], scale[w, 4], scale[w, 5]
        return (
            mid[0] + slope * east[1] - (above * high[0] - below * low[0]),
            mid[1] - slope * east[0] - (above * high[1] - below * low[1]),
        )

    def trade(e, ref, wing):
        @pl.when(has_before)
        def _():
            remote(
                ref.at[pl.ds(wing, wing)], ref.at[pl.ds(wing + HOLD, wing)],
                send_x.at[e, 0], recv_x.at[e, 1], before_device,
            )

        @pl.when(has_after)
        def _():
            remote(ref.at[pl.ds(HOLD, wing)], ref.at[pl.ds(0, wing)], send_x.at[e, 1], recv_x.at[e, 0], after_device)

    def traded(e, ref, wing):
        pl.when(has_before)(lambda: landed(ref.at[pl.ds(0, wing)], recv_x.at[e, 0]))
        pl.when(has_after)(lambda: landed(ref.at[pl.ds(wing + HOLD, wing)], recv_x.at[e, 1]))

    def send_back(g):
        size = HOLD * 3 * len(GROUPS[g])
        start = first_row(chain - 32 * my_band) * (size // HOLD)

        def one(k, carry):
            to = lax.rem(chain + k, 32)
            send(
                snd[g].at[pl.ds(to * size, size)], ret[g].at[pl.ds(start, size)],
                send_c.at[g], recv_c.at[g], (my_lat, to),
            )
            return carry

        lax.fori_loop(0, 32, one, 0)

    @pl.when(owner)
    def _():
        loaded(3, 4, 5, 6, 7)
        prepare()

        @pl.when(jnp.logical_not(has_before))
        def _():
            tall[0:2] = jnp.zeros((2, 2 * HALF, 128), F32)
            tall_new[0:2] = jnp.zeros((2, 2 * HALF, 128), F32)
            wind[0] = jnp.zeros((2, 2 * HALF, 128), F32)

        @pl.when(jnp.logical_not(has_after))
        def _():
            tall[2 + HOLD : 4 + HOLD] = jnp.zeros((2, 2 * HALF, 128), F32)
            tall_new[2 + HOLD : 4 + HOLD] = jnp.zeros((2, 2 * HALF, 128), F32)
            wind[1 + HOLD] = jnp.zeros((2, 2 * HALF, 128), F32)

        landed(recv[0], recv_a.at[0])
        for (row, _), pair in transform(0).items():
            put(tall, (2 + row,), pair)
        trade(0, tall, 2)
        landed(recv[1], recv_a.at[1])
        for (row, which), pair in transform(1).items():
            put(wind, (1 + row, which), pair)
        trade(1, wind, 1)
        traded(0, tall, 2)
        traded(1, wind, 1)
        for w in range(WINGS):
            push_winds(tall, wind, wind_new, w)
        for w in range(1, 1 + HOLD):
            put(tall_new, (1 + w,), pushed_height(tall, wind_new, w))
        trade(2, tall_new, 2)
        traded(2, tall_new, 2)
        for w in range(WINGS):
            push_winds(tall_new, wind_new, wind_last, w)
        restore(1, {(row, which): get(wind_last, 1 + row, which) for row in range(HOLD) for which in range(2)})
        send_back(1)
        restore(0, {(row, 0): pushed_height(tall_new, wind_last, 1 + row) for row in range(HOLD)})
        send_back(0)

    @pl.when(stencil)
    def _():
        @pl.when(lat > 2)
        def _():
            landed(ext.at[:, 0:8, :], recv_r.at[1])

        @pl.when(lat < 13)
        def _():
            landed(ext.at[:, 104:112, :], recv_r.at[0])

        row = lax.broadcasted_iota(jnp.int32, (ROWS + 16, 128), 0) + (ROWS * lat - 8)
        latitude = (row.astype(F32) + (0.5 - NLAT // 2)) * (math.pi / NLAT)
        wide_cos = jnp.concatenate([jnp.cos(latitude)] * 4, axis=1)
        spin = jnp.concatenate([SPIN * jnp.sin(latitude)] * 4, axis=1)
        inverse = 1.0 / wide_cos
        east_scale = (0.5 * COURANT) * inverse
        speed = speed_ref[0]

        def across(value):
            return pltpu.roll(value, 511, 1) - pltpu.roll(value, 1, 1)

        def along(value):
            return pltpu.roll(value, ROWS + 15, 0) - pltpu.roll(value, 1, 0)

        height, east, north = ext[0], ext[1], ext[2]
        for _step in range(2):
            east_inc = spin * north - east_scale * across(height)
            north_inc = (-0.5 * NORTH) * along(height) - spin * east
            east, north = east + east_inc, north + north_inc
            spread_out = east_scale * across(east) + (0.5 * NORTH) * inverse * along(north * wide_cos)
            height = height - speed * spread_out
        for out, value in zip(outs, (height, east, north)):
            out[0] = value[8 : 8 + ROWS, 0:CELLS]

    def back(f, s):
        g = 0 if f == 0 else 1
        return ret[g][pl.ds(3 * GROUPS[g].index(f) + s, ROWS, stride=3 * len(GROUPS[g])), :]

    @pl.when(band < 2)
    def _():
        for g in (1, 0):
            landed(ret[g], recv_c.at[g])
            for f in GROUPS[g]:
                for s in range(3):
                    outs[f][0, :, 128 * s : 128 * (s + 1)] = back(f, s)

    @pl.when(band == 2)
    def _():
        row = lax.broadcasted_iota(jnp.int32, (ROWS, 128), 0)
        from_pole = jnp.where(south, ROWS - 1 - row, row) + 2 * ROWS
        for g in (1, 0):
            landed(ret[g].at[pl.ds(0, 24 * HOLD * 3 * len(GROUPS[g]))], recv_c.at[g])
            for f in GROUPS[g]:
                for s in range(3):
                    lanes = slice(128 * s, 128 * (s + 1))
                    outs[f][0, :, lanes] = jnp.where(from_pole < FINAL, back(f, s), outs[f][0, :, lanes])

    for g in range(2):
        size = HOLD * 3 * len(GROUPS[g])
        for case, count in (
            (jnp.logical_and(band < 2, jnp.logical_not(own_rows)), 32), (jnp.logical_and(band < 2, own_rows), 31),
            (jnp.logical_and(band == 2, jnp.logical_not(own_rows)), 24), (jnp.logical_and(band == 2, own_rows), 23),
        ):
            pl.when(case)(lambda g=g, size=size, count=count: landed(src[g].at[pl.ds(0, count * size)], send_a.at[g]))
        for case, count in (
            (jnp.logical_and(owner, jnp.logical_not(own_rows)), 32), (jnp.logical_and(owner, own_rows), 31),
        ):
            pl.when(case)(lambda g=g, size=size, count=count: landed(snd[g].at[pl.ds(0, count * size)], send_c.at[g]))

    @pl.when(stencil)
    def _():
        for side in range(2):
            landed(packed.at[side], send_s.at[side])

        @pl.when(lat > 2)
        def _():
            landed(ext.at[:, 8:16, :], send_r.at[0])

        @pl.when(lat < 13)
        def _():
            landed(ext.at[:, 96:104, :], send_r.at[1])

    for e, (ref, wing) in enumerate(((tall, 2), (wind, 1), (tall_new, 2))):
        pl.when(has_before)(lambda e=e, ref=ref, wing=wing: landed(ref.at[pl.ds(0, wing)], send_x.at[e, 0]))
        pl.when(has_after)(lambda e=e, ref=ref, wing=wing: landed(ref.at[pl.ds(0, wing)], send_x.at[e, 1]))


def body(height, east_wind, north_wind, wave_speed_sq):
    constants = [np.asarray(table, np.float32) for table in tables()]
    block = jax.ShapeDtypeStruct((1, ROWS, CELLS), F32)
    pairs = []
    for rows in (ROWS, 32 * HOLD, 32 * HOLD, ROWS):
        pairs += [pltpu.VMEM((rows * 3 * len(group), 128), F32) for group in GROUPS]
    dma = pltpu.SemaphoreType.DMA
    return pl.pallas_call(
        kernel,
        out_shape=[block] * 3,
        in_specs=[pl.BlockSpec(memory_space=pltpu.SMEM)] + [pl.BlockSpec(memory_space=pl.ANY)] * 8,
        out_specs=[pl.BlockSpec(memory_space=pltpu.VMEM)] * 3,
        scratch_shapes=[
            *[pltpu.VMEM((1, ROWS, CELLS), F32)] * 3,
            *[pltpu.VMEM(table.shape, table.dtype) for table in constants],
            *pairs,
            *[pltpu.VMEM((HOLD + 4, 2 * HALF, 128), F32)] * 2,
            *[pltpu.VMEM((WINGS, 2, 2 * HALF, 128), F32)] * 3,
            pltpu.VMEM((WINGS, 6, HALF, 128), F32),
            pltpu.VMEM((2, ROWS, 128), F32),
            pltpu.VMEM((2, ROWS, 128), F32),
            pltpu.VMEM((3, ROWS + 16, 512), F32),
            dma((8,)), dma((2,)), dma((2,)), dma((2,)), dma((2,)),
            dma((3, 2)), dma((3, 2)), dma((2,)), dma((2,)), dma((2,)), dma((2,)),
        ],
        compiler_params=pltpu.CompilerParams(
            collective_id=0, has_side_effects=True, vmem_limit_bytes=60 * 1024 * 1024
        ),
        name="substeps",
    )(wave_speed_sq, height, east_wind, north_wind, *constants)


def solution(mesh):
    block = P(None, "lat", "lon")
    return jax.shard_map(
        lambda *args: tuple(body(*args)),
        mesh=mesh, in_specs=(block, block, block, P()), out_specs=(block, block, block), check_vma=False,
    )
```

```python
import math

import jax
import jax.numpy as jnp
import ml_dtypes
import numpy as np
from jax import lax
from jax.experimental import pallas as pl
from jax.experimental.pallas import tpu as pltpu
from jax.sharding import PartitionSpec as P

NLON, NLAT = 12288, 1536
ROWS, CELLS = 96, 384
OUTER, INNER = 96, 128
HALF = 56
COURANT, SPIN = 0.45, 0.3
NORTH = COURANT * 2.0 * NLAT / NLON
FINAL = 260
HOLD = 2
OWNERS = 132
WINGS = HOLD + 2
MESH = pl.DeviceIdType.MESH
F32, BF16 = jnp.float32, jnp.bfloat16
GROUPS = ((0,), (1, 2))


def split(table):
    high = table.astype(ml_dtypes.bfloat16)
    low = (table - high.astype(np.float64)).astype(ml_dtypes.bfloat16)
    return high, low


def tables():
    a = np.array([3 * d + s for s in range(3) for d in range(32)])
    k1 = np.arange(HALF)
    live = (k1 <= OUTER // 2).astype(np.float64)
    angle = 2 * np.pi * ((k1[:, None] * a[None, :]) % OUTER) / OUTER
    first = np.concatenate([np.cos(angle) * live[:, None], -np.sin(angle) * live[:, None]], axis=0)
    weight = live * np.where((k1 == 0) | (k1 == OUTER // 2), 1.0, 2.0) / NLON
    last = np.concatenate([np.cos(angle) * weight[:, None], -np.sin(angle) * weight[:, None]], axis=0).T
    n = np.arange(INNER)
    turn = 2 * np.pi * (k1[:, None] * n[None, :]) / NLON
    inner = 2 * np.pi * ((n[:, None] * n[None, :]) % INNER) / INNER
    cos, sin = np.cos(inner), np.sin(inner)
    forward = np.block([[cos, -sin], [sin, cos]])
    backward = np.block([[cos, sin], [-sin, cos]])
    wave = k1[:, None] + OUTER * n[None, :]
    steep = np.sin(2 * np.pi * wave / NLON) * live[:, None]
    half_sine = np.where(live[:, None] > 0, 0.5 * np.abs(np.sin(np.pi * wave / NLON)), 1.0)
    first_high, first_low = split(first)
    last_high, last_low = split(last)
    forward_high, forward_low = split(forward)
    backward_high, backward_low = split(backward)
    grid = np.stack([np.cos(turn), np.sin(turn), steep, half_sine]).astype(np.float32)
    return (
        np.concatenate([first_high, first_low, first_high], axis=1),
        np.concatenate([last_high, last_low, last_high], axis=1),
        np.stack([forward_high, forward_low]),
        np.stack([backward_high, backward_low]),
        grid,
    )


def parts(value):
    high = value.astype(BF16)
    return high, (value - high.astype(F32)).astype(BF16)


def dot(left, right):
    return jnp.dot(left, right, preferred_element_type=F32)


def outer_step(table, value):
    high, low = parts(value)
    return dot(table.astype(BF16), jnp.concatenate([high, high, low], axis=0))


def inner_step(table, value):
    high, low = parts(value)
    table_high, table_low = table[0].astype(BF16), table[1].astype(BF16)
    return dot(high, table_high) + dot(low, table_high) + dot(high, table_low)


def kernel(
    speed_ref, h_hbm, u_hbm, v_hbm, first_hbm, last_hbm, fore_hbm, back_hbm, grid_hbm,
    h_out, u_out, v_out,
    h_ref, u_ref, v_ref, first_ref, last_ref, fore_ref, back_ref, grid_ref,
    src0, src1, relay0, relay1, recv0, recv1, snd0, snd1, home0, home1, ret0, ret1,
    tall, tall_new, wind, wind_new, wind_last, scale, packed, sides, ext,
    loads, send_a, recv_a, send_b, recv_b, send_c, recv_c, send_d, recv_d, send_x, recv_x, send_s, recv_s, send_r, recv_r,
):
    fields, outs = (h_ref, u_ref, v_ref), (h_out, u_out, v_out)
    operands = (h_hbm, u_hbm, v_hbm, first_hbm, last_hbm, fore_hbm, back_hbm, grid_hbm)
    held = (h_ref, u_ref, v_ref, first_ref, last_ref, fore_ref, back_ref, grid_ref)
    src, relay, recv = (src0, src1), (relay0, relay1), (recv0, recv1)
    snd, home, ret = (snd0, snd1), (home0, home1), (ret0, ret1)
    lat, lon = lax.axis_index("lat"), lax.axis_index("lon")
    south = lat >= 8
    band = jnp.where(south, 15 - lat, lat)
    core = lax.rem(band, 2)
    z = lax.rem(lon, 16)
    x = 2 * lax.div(lon, 16) + lax.rem(lax.div(band, 2), 2)
    line = jnp.where(band < 4, x, 7 - x)
    wide = line >= 6
    near = lax.rem(z + line, 16)
    slab = 16 * core + z
    extra = jnp.logical_and(wide, jnp.logical_and(core == 0, jnp.logical_or(near == 0, near == 15)))
    owner = jnp.logical_or(core == 1, extra)
    owners = jnp.where(wide, 18, 16)
    nth = jnp.where(wide, jnp.where(core == 1, near + 1, jnp.where(near == 0, 0, 17)), near)
    chain = 16 * line + 2 * jnp.where(line == 7, 1, 0) + nth
    source = band <= 2
    stencil = band >= 2
    my_band = jnp.where(wide, 2, lax.div(line, 3))
    my_lat = jnp.where(south, 15 - my_band, my_band)
    my_part = line - 3 * my_band

    def member(to_line, to_z, to_core):
        to_x = jnp.where(to_line < 4, to_line, 7 - to_line)
        to_band = 4 * lax.div(to_line, 4) + 2 * lax.rem(to_x, 2) + to_core
        return jnp.where(south, 15 - to_band, to_band), 16 * lax.div(to_x, 2) + to_z

    def mate(to_z, to_core):
        shift = to_core - core
        return jnp.where(south, lat - shift, lat + shift), lon - z + to_z

    def holder(n):
        to_line = jnp.where(n < 96, lax.div(n, 16), 6 + lax.div(jnp.maximum(n - 96, 0), 18))
        to_nth = n - 16 * to_line - 2 * jnp.where(to_line == 7, 1, 0)
        broad = to_line >= 6
        to_near = jnp.where(broad, jnp.clip(to_nth - 1, 0, 15), to_nth)
        to_core = jnp.where(jnp.logical_and(broad, jnp.logical_or(to_nth == 0, to_nth == 17)), 0, 1)
        return member(to_line, lax.rem(to_near + 16 - to_line, 16), to_core)

    def chip(k):
        away = 8 - lax.div(k + 1, 2)
        return lax.rem(z + 16 + jnp.where(lax.rem(k, 2) == 1, away, -away), 16)

    def same(target):
        return jnp.logical_and(target[0] == lat, target[1] == lon)

    def remote(here, there, send_sem, recv_sem, target):
        pltpu.make_async_remote_copy(
            src_ref=here, dst_ref=there, send_sem=send_sem, recv_sem=recv_sem, device_id=target, device_id_type=MESH
        ).start()

    def send(here, there, send_sem, recv_sem, target):
        own = same(target)

        @pl.when(own)
        def _():
            pltpu.make_async_copy(here, there, recv_sem).start()

        @pl.when(jnp.logical_not(own))
        def _():
            remote(here, there, send_sem, recv_sem, target)

    def landed(ref, sem):
        pltpu.make_async_copy(ref, ref, sem).wait()

    def part_start(k, size):
        return jnp.where(south, ROWS - size * (k + 1), size * k)

    def owner_start(i):
        return HOLD * jnp.where(south, owners - 1 - i, i)

    def each_size(act):
        pl.when(jnp.logical_not(wide))(lambda: act(32))
        pl.when(wide)(lambda: act(36))

    right = jnp.where(lon == 31, 0, lon + 1)
    left = jnp.where(lon == 0, 31, lon - 1)
    before = chain + jnp.where(south, 1, -1)
    after = chain + jnp.where(south, -1, 1)
    has_before = jnp.logical_and(owner, jnp.logical_and(before >= 0, before < OWNERS))
    has_after = jnp.logical_and(owner, jnp.logical_and(after >= 0, after < OWNERS))
    before_device, after_device = holder(jnp.clip(before, 0, OWNERS - 1)), holder(jnp.clip(after, 0, OWNERS - 1))

    barrier = pltpu.get_barrier_semaphore()

    def greet(target):
        pl.semaphore_signal(barrier, inc=1, device_id=target, device_id_type=MESH)

    def greet_other(target):
        pl.when(jnp.logical_not(same(target)))(lambda: greet(target))

    def greet_chip(k, carry):
        to = lax.rem(z + k, 16)
        greet(mate(to, 1))
        pl.when(owner)(lambda: greet(mate(to, 0)))
        return carry

    lax.fori_loop(1, 16, greet_chip, 0)
    greeted = jnp.where(owner, 30, 15)
    own_chip = jnp.logical_or(core == 0, owner)
    pl.when(own_chip)(lambda: greet(mate(z, 1 - core)))
    greeted += own_chip.astype(jnp.int32)
    for end in (0, 15):
        there = lax.rem(end + 16 - line, 16)
        meant = jnp.logical_and(wide, jnp.logical_not(jnp.logical_or(owner, there == z)))
        pl.when(meant)(lambda there=there: greet(mate(there, 0)))
        greeted += meant.astype(jnp.int32)
    meant = jnp.logical_not(same((my_lat, slab)))
    pl.when(meant)(lambda: greet((my_lat, slab)))
    greeted += meant.astype(jnp.int32)
    for k in range(3):
        target = member(jnp.minimum(3 * band + k, 7), z, lax.div(lon, 16))
        meant = jnp.logical_or(band < 2, jnp.logical_and(band == 2, k < 2))
        meant = jnp.logical_and(meant, jnp.logical_not(same(target)))
        pl.when(meant)(lambda target=target: greet(target))
        greeted += meant.astype(jnp.int32)
    for meant, target in (
        (has_before, before_device), (has_after, after_device), (stencil, (lat, left)), (stencil, (lat, right)),
        (jnp.logical_and(stencil, lat > 2), (lat - 1, lon)), (jnp.logical_and(stencil, lat < 13), (lat + 1, lon)),
    ):
        pl.when(meant)(lambda target=target: greet(target))
        greeted += meant.astype(jnp.int32)

    def load(*indices):
        for index in indices:
            pltpu.make_async_copy(operands[index], held[index], loads.at[index]).start()

    def loaded(*indices):
        for index in indices:
            pltpu.make_async_copy(operands[index], held[index], loads.at[index]).wait()

    load(0, 1, 2)
    pl.when(owner)(lambda: load(3, 4, 5, 6, 7))

    def gather(g):
        per = 3 * len(GROUPS[g])
        for pos, f in enumerate(GROUPS[g]):
            for s in range(3):
                src[g][pl.ds(3 * pos + s, ROWS, stride=per), :] = fields[f][0, :, 128 * s : 128 * (s + 1)]

    def send_rows(g):
        per = 3 * len(GROUPS[g])

        def one(k, size):
            send(
                src[g].at[pl.ds(part_start(k, size) * per, size * per)], relay[g].at[pl.ds(0, size * per)],
                send_a.at[g, k], recv_a.at[g], member(3 * band + k, z, lax.div(lon, 16)),
            )

        @pl.when(band < 2)
        def _():
            for k in range(3):
                one(k, 32)

        @pl.when(band == 2)
        def _():
            for k in range(2):
                one(k, 36)

    loaded(0)
    pl.when(source)(lambda: gather(0))
    pl.semaphore_wait(barrier, greeted)
    pl.when(source)(lambda: send_rows(0))
    loaded(1, 2)

    @pl.when(source)
    def _():
        gather(1)
        send_rows(1)

    @pl.when(stencil)
    def _():
        lane = lax.broadcasted_iota(jnp.int32, (ROWS, 128), 1)
        high = [ref[0, :, 256:384] for ref in fields]
        low = [ref[0, :, 0:128] for ref in fields]
        packed[0] = jnp.where(
            lane >= 124, high[0], jnp.where(lane >= 120, pltpu.roll(high[1], 124, 1), pltpu.roll(high[2], 120, 1))
        )
        packed[1] = jnp.where(lane < 4, low[0], jnp.where(lane < 8, pltpu.roll(low[1], 4, 1), pltpu.roll(low[2], 8, 1)))
        remote(packed.at[0], sides.at[0], send_s.at[0], recv_s.at[0], (lat, right))
        remote(packed.at[1], sides.at[1], send_s.at[1], recv_s.at[1], (lat, left))

    for g in range(2):
        per = 3 * len(GROUPS[g])
        each_size(lambda size, g=g, per=per: landed(relay[g].at[pl.ds(0, size * per)], recv_a.at[g]))

        def to_owner(how, i, target, g=g, per=per):
            how(
                relay[g].at[pl.ds(owner_start(i) * per, HOLD * per)],
                recv[g].at[pl.ds(slab * (HOLD * per), HOLD * per)],
                send_b.at[g], recv_b.at[g], target,
            )

        def spread(k, carry, to_owner=to_owner):
            to = chip(k)
            to_owner(remote, lax.rem(to + line, 16) + jnp.where(wide, 1, 0), mate(to, 1))
            return carry

        @pl.when(wide)
        def _(to_owner=to_owner):
            for i in (0, 17):
                to_owner(send, i, mate(lax.rem(min(i, 15) + 16 - line, 16), 0))

        lax.fori_loop(0, 15, spread, 0)
        to_owner(send, near + jnp.where(wide, 1, 0), mate(z, 1))

    @pl.when(stencil)
    def _():
        landed(sides.at[0], recv_s.at[0])
        landed(sides.at[1], recv_s.at[1])
        lane = lax.broadcasted_iota(jnp.int32, (ROWS, 128), 1)
        for f in range(3):
            ext[f, 8 : 8 + ROWS, 0:CELLS] = fields[f][0]
            east_side, west_side = sides[1], sides[0]
            if f:
                east_side, west_side = pltpu.roll(east_side, 128 - 4 * f, 1), pltpu.roll(west_side, 4 * f, 1)
            ext[f, 8 : 8 + ROWS, CELLS : CELLS + 128] = jnp.where(lane < 64, east_side, west_side)

        @pl.when(lat > 2)
        def _():
            remote(ext.at[:, 8:16, :], ext.at[:, 104:112, :], send_r.at[0], recv_r.at[0], (lat - 1, lon))

        @pl.when(lat < 13)
        def _():
            remote(ext.at[:, 96:104, :], ext.at[:, 0:8, :], send_r.at[1], recv_r.at[1], (lat + 1, lon))

        @pl.when(lat == 2)
        def _():
            ext[:, 0:8, :] = jnp.zeros((3, 8, 512), F32)

        @pl.when(lat == 13)
        def _():
            ext[:, 104:112, :] = jnp.zeros((3, 8, 512), F32)

    def transform(g):
        size = HOLD * 3 * len(GROUPS[g])
        order = [(row, pos) for row in range(HOLD) for pos in range(len(GROUPS[g]))]
        grids = [
            jnp.concatenate(
                [recv[g][pl.ds(row * (size // HOLD) + 3 * pos + s, 32, stride=size), :] for s in range(3)], axis=0
            )
            for row, pos in order
        ]
        mixed = outer_step(first_ref[...], jnp.concatenate(grids, axis=1))
        cos, sin = grid_ref[0], grid_ref[1]
        twisted = []
        for n in range(len(order)):
            real, imag = mixed[:HALF, 128 * n : 128 * (n + 1)], mixed[HALF:, 128 * n : 128 * (n + 1)]
            twisted.append(jnp.concatenate([real * cos + imag * sin, imag * cos - real * sin], axis=1))
        spectrum = inner_step(fore_ref, jnp.concatenate(twisted, axis=0))
        return {
            key: (spectrum[HALF * n : HALF * (n + 1), :128], spectrum[HALF * n : HALF * (n + 1), 128:])
            for n, key in enumerate(order)
        }

    def restore(g, spectra):
        size = HOLD * 3 * len(GROUPS[g])
        order = list(spectra)
        cos, sin = grid_ref[0], grid_ref[1]
        back = inner_step(
            back_ref, jnp.concatenate([jnp.concatenate(spectra[key], axis=1) for key in order], axis=0)
        )
        spun = []
        for n in range(len(order)):
            real, imag = back[HALF * n : HALF * (n + 1), :128], back[HALF * n : HALF * (n + 1), 128:]
            spun.append(jnp.concatenate([real * cos - imag * sin, imag * cos + real * sin], axis=0))
        cells = outer_step(last_ref[...], jnp.concatenate(spun, axis=1))
        for n, (row, pos) in enumerate(order):
            for s in range(3):
                snd[g][pl.ds(row * (size // HOLD) + 3 * pos + s, 32, stride=size), :] = cells[
                    32 * s : 32 * (s + 1), 128 * n : 128 * (n + 1)
                ]

    def put(ref, index, pair):
        ref[(*index, slice(0, HALF))] = pair[0]
        ref[(*index, slice(HALF, 2 * HALF))] = pair[1]

    def get(ref, *index):
        return ref[(*index, slice(0, HALF))], ref[(*index, slice(HALF, 2 * HALF))]

    row0 = jnp.where(south, NLAT - HOLD - HOLD * chain, HOLD * chain)

    def polar(row):
        steps = jnp.where(south, NLAT - 1 - row, row)
        return jnp.abs(jnp.full((1, 128), steps, jnp.int32).astype(F32) + 0.5) * (math.pi / NLAT)

    def cosine(w):
        return jnp.sin(polar(row0 + w - 1))

    def prepare():
        speed = speed_ref[0]
        share_of_pole = jnp.where(south, SPIN, -SPIN).astype(F32)
        for w in range(WINGS):
            there = 1.0
            if w == 0:
                there = jnp.where(has_before, 1.0, 0.0).astype(F32)
            if w == WINGS - 1:
                there = jnp.where(has_after, 1.0, 0.0).astype(F32)
            angle = polar(row0 + w - 1)
            share = 1.0 / jnp.maximum(grid_ref[3], jnp.sin(angle))
            keep = share * (jnp.sin(angle) * there)
            slope = share * (COURANT * grid_ref[2])
            scale[w, 0] = slope
            scale[w, 1] = keep * (share_of_pole * jnp.cos(angle))
            scale[w, 2] = keep * (0.5 * NORTH)
            if 0 < w < WINGS - 1:
                scale[w, 3] = speed * slope
                scale[w, 4] = share * (speed * (0.5 * NORTH) * cosine(w - 1))
                scale[w, 5] = share * (speed * (0.5 * NORTH) * cosine(w + 1))

    def push_winds(heights, old, new, w):
        low, mid, high = get(heights, w), get(heights, w + 1), get(heights, w + 2)
        east, north = get(old, w, 0), get(old, w, 1)
        slope, swirl, climb = scale[w, 0], scale[w, 1], scale[w, 2]
        put(new, (w, 0), (
            east[0] + slope * mid[1] + swirl * north[0],
            east[1] - slope * mid[0] + swirl * north[1],
        ))
        put(new, (w, 1), tuple(north[p] - climb * (high[p] - low[p]) - swirl * east[p] for p in range(2)))

    def pushed_height(heights, winds, w):
        mid, east = get(heights, w + 1), get(winds, w, 0)
        low, high = get(winds, w - 1, 1), get(winds, w + 1, 1)
        slope, below, above = scale[w, 3], scale[w, 4], scale[w, 5]
        return (
            mid[0] + slope * east[1] - (above * high[0] - below * low[0]),
            mid[1] - slope * east[0] - (above * high[1] - below * low[1]),
        )

    def trade(e, ref, wing):
        @pl.when(has_before)
        def _():
            remote(
                ref.at[pl.ds(wing, wing)], ref.at[pl.ds(wing + HOLD, wing)],
                send_x.at[e, 0], recv_x.at[e, 1], before_device,
            )

        @pl.when(has_after)
        def _():
            remote(ref.at[pl.ds(HOLD, wing)], ref.at[pl.ds(0, wing)], send_x.at[e, 1], recv_x.at[e, 0], after_device)

    def traded(e, ref, wing):
        pl.when(has_before)(lambda: landed(ref.at[pl.ds(0, wing)], recv_x.at[e, 0]))
        pl.when(has_after)(lambda: landed(ref.at[pl.ds(wing + HOLD, wing)], recv_x.at[e, 1]))

    def send_back(g):
        size = HOLD * 3 * len(GROUPS[g])
        start = owner_start(nth) * (size // HOLD)

        def one(how, to_z, to_core):
            how(
                snd[g].at[pl.ds((16 * to_core + to_z) * size, size)], home[g].at[pl.ds(start, size)],
                send_c.at[g], recv_c.at[g], mate(to_z, to_core),
            )

        def both(k, carry):
            to = chip(k)
            one(remote, to, 0)
            one(remote, to, 1)
            return carry

        lax.fori_loop(0, 15, both, 0)
        one(send, z, 0)
        one(send, z, 1)

    @pl.when(owner)
    def _():
        loaded(3, 4, 5, 6, 7)
        prepare()

        @pl.when(jnp.logical_not(has_before))
        def _():
            tall[0:2] = jnp.zeros((2, 2 * HALF, 128), F32)
            tall_new[0:2] = jnp.zeros((2, 2 * HALF, 128), F32)
            wind[0] = jnp.zeros((2, 2 * HALF, 128), F32)

        @pl.when(jnp.logical_not(has_after))
        def _():
            tall[2 + HOLD : 4 + HOLD] = jnp.zeros((2, 2 * HALF, 128), F32)
            tall_new[2 + HOLD : 4 + HOLD] = jnp.zeros((2, 2 * HALF, 128), F32)
            wind[1 + HOLD] = jnp.zeros((2, 2 * HALF, 128), F32)

        landed(recv[0], recv_b.at[0])
        for (row, _), pair in transform(0).items():
            put(tall, (2 + row,), pair)
        trade(0, tall, 2)
        landed(recv[1], recv_b.at[1])
        for (row, which), pair in transform(1).items():
            put(wind, (1 + row, which), pair)
        trade(1, wind, 1)
        traded(0, tall, 2)
        traded(1, wind, 1)
        for w in range(WINGS):
            push_winds(tall, wind, wind_new, w)
        for w in range(1, 1 + HOLD):
            put(tall_new, (1 + w,), pushed_height(tall, wind_new, w))
        trade(2, tall_new, 2)
        traded(2, tall_new, 2)
        for w in range(WINGS):
            push_winds(tall_new, wind_new, wind_last, w)
        restore(1, {(row, which): get(wind_last, 1 + row, which) for row in range(HOLD) for which in range(2)})
        send_back(1)
        restore(0, {(row, 0): pushed_height(tall_new, wind_last, 1 + row) for row in range(HOLD)})
        send_back(0)

    for g in (1, 0):
        per = 3 * len(GROUPS[g])

        def deliver(size, g=g, per=per):
            landed(home[g].at[pl.ds(0, size * per)], recv_c.at[g])
            send(
                home[g].at[pl.ds(0, size * per)], ret[g].at[pl.ds(part_start(my_part, size) * per, size * per)],
                send_d.at[g], recv_d.at[g, my_part], (my_lat, slab),
            )

        each_size(deliver)

    @pl.when(stencil)
    def _():
        @pl.when(lat > 2)
        def _():
            landed(ext.at[:, 0:8, :], recv_r.at[1])

        @pl.when(lat < 13)
        def _():
            landed(ext.at[:, 104:112, :], recv_r.at[0])

        row = lax.broadcasted_iota(jnp.int32, (ROWS + 16, 128), 0) + (ROWS * lat - 8)
        latitude = (row.astype(F32) + (0.5 - NLAT // 2)) * (math.pi / NLAT)
        wide_cos = jnp.concatenate([jnp.cos(latitude)] * 4, axis=1)
        spin = jnp.concatenate([SPIN * jnp.sin(latitude)] * 4, axis=1)
        inverse = 1.0 / wide_cos
        east_scale = (0.5 * COURANT) * inverse
        speed = speed_ref[0]

        def across(value):
            return pltpu.roll(value, 511, 1) - pltpu.roll(value, 1, 1)

        def along(value):
            return pltpu.roll(value, ROWS + 15, 0) - pltpu.roll(value, 1, 0)

        height, east, north = ext[0], ext[1], ext[2]
        for _step in range(2):
            east_inc = spin * north - east_scale * across(height)
            north_inc = (-0.5 * NORTH) * along(height) - spin * east
            east, north = east + east_inc, north + north_inc
            spread_out = east_scale * across(east) + (0.5 * NORTH) * inverse * along(north * wide_cos)
            height = height - speed * spread_out
        for out, value in zip(outs, (height, east, north)):
            out[0] = value[8 : 8 + ROWS, 0:CELLS]

    def back(f, s):
        g = 0 if f == 0 else 1
        return ret[g][pl.ds(3 * GROUPS[g].index(f) + s, ROWS, stride=3 * len(GROUPS[g])), :]

    @pl.when(band < 2)
    def _():
        for g in (1, 0):
            per = 3 * len(GROUPS[g])
            for k in range(3):
                landed(ret[g].at[pl.ds(part_start(k, 32) * per, 32 * per)], recv_d.at[g, k])
            for f in GROUPS[g]:
                for s in range(3):
                    outs[f][0, :, 128 * s : 128 * (s + 1)] = back(f, s)

    @pl.when(band == 2)
    def _():
        row = lax.broadcasted_iota(jnp.int32, (ROWS, 128), 0)
        from_pole = jnp.where(south, ROWS - 1 - row, row) + 2 * ROWS
        for g in (1, 0):
            per = 3 * len(GROUPS[g])
            for k in range(2):
                landed(ret[g].at[pl.ds(part_start(k, 36) * per, 36 * per)], recv_d.at[g, k])
            for f in GROUPS[g]:
                for s in range(3):
                    lanes = slice(128 * s, 128 * (s + 1))
                    outs[f][0, :, lanes] = jnp.where(from_pole < FINAL, back(f, s), outs[f][0, :, lanes])

    for g in range(2):
        per = 3 * len(GROUPS[g])

        def left_parts(size, parts, g=g, per=per):
            for k in range(parts):
                other = jnp.logical_not(same(member(3 * band + k, z, lax.div(lon, 16))))
                pl.when(other)(lambda k=k: landed(src[g].at[pl.ds(0, size * per)], send_a.at[g, k]))

        pl.when(band < 2)(lambda f=left_parts: f(32, 3))
        pl.when(band == 2)(lambda f=left_parts: f(36, 2))
        for case, count in (
            (jnp.logical_and(jnp.logical_not(wide), owner), 15),
            (jnp.logical_and(jnp.logical_not(wide), jnp.logical_not(owner)), 16),
            (jnp.logical_and(wide, owner), 17),
            (jnp.logical_and(wide, jnp.logical_not(owner)), 18),
        ):
            pl.when(case)(
                lambda g=g, n=count * HOLD * per: landed(relay[g].at[pl.ds(0, n)], send_b.at[g])
            )
        pl.when(owner)(lambda g=g, per=per: landed(snd[g].at[pl.ds(0, 31 * HOLD * per)], send_c.at[g]))

        @pl.when(jnp.logical_not(same((my_lat, slab))))
        def _(g=g, per=per):
            each_size(lambda size: landed(home[g].at[pl.ds(0, size * per)], send_d.at[g]))

    @pl.when(stencil)
    def _():
        for side in range(2):
            landed(packed.at[side], send_s.at[side])

        @pl.when(lat > 2)
        def _():
            landed(ext.at[:, 8:16, :], send_r.at[0])

        @pl.when(lat < 13)
        def _():
            landed(ext.at[:, 96:104, :], send_r.at[1])

    for e, (ref, wing) in enumerate(((tall, 2), (wind, 1), (tall_new, 2))):
        pl.when(has_before)(lambda e=e, ref=ref, wing=wing: landed(ref.at[pl.ds(0, wing)], send_x.at[e, 0]))
        pl.when(has_after)(lambda e=e, ref=ref, wing=wing: landed(ref.at[pl.ds(0, wing)], send_x.at[e, 1]))


def body(height, east_wind, north_wind, wave_speed_sq):
    constants = [np.asarray(table, np.float32) for table in tables()]
    block = jax.ShapeDtypeStruct((1, ROWS, CELLS), F32)
    pairs = []
    for rows in (ROWS, 36, 32 * HOLD, 32 * HOLD, 36, ROWS):
        pairs += [pltpu.VMEM((rows * 3 * len(group), 128), F32) for group in GROUPS]
    dma = pltpu.SemaphoreType.DMA
    return pl.pallas_call(
        kernel,
        out_shape=[block] * 3,
        in_specs=[pl.BlockSpec(memory_space=pltpu.SMEM)] + [pl.BlockSpec(memory_space=pl.ANY)] * 8,
        out_specs=[pl.BlockSpec(memory_space=pltpu.VMEM)] * 3,
        scratch_shapes=[
            *[pltpu.VMEM((1, ROWS, CELLS), F32)] * 3,
            *[pltpu.VMEM(table.shape, table.dtype) for table in constants],
            *pairs,
            *[pltpu.VMEM((HOLD + 4, 2 * HALF, 128), F32)] * 2,
            *[pltpu.VMEM((WINGS, 2, 2 * HALF, 128), F32)] * 3,
            pltpu.VMEM((WINGS, 6, HALF, 128), F32),
            pltpu.VMEM((2, ROWS, 128), F32),
            pltpu.VMEM((2, ROWS, 128), F32),
            pltpu.VMEM((3, ROWS + 16, 512), F32),
            dma((8,)), dma((2, 3)), dma((2,)), dma((2,)), dma((2,)), dma((2,)), dma((2,)), dma((2,)), dma((2, 3)),
            dma((3, 2)), dma((3, 2)), dma((2,)), dma((2,)), dma((2,)), dma((2,)),
        ],
        compiler_params=pltpu.CompilerParams(
            collective_id=0, has_side_effects=True, vmem_limit_bytes=60 * 1024 * 1024
        ),
        name="substeps",
    )(wave_speed_sq, height, east_wind, north_wind, *constants)


def solution(mesh):
    block = P(None, "lat", "lon")
    return jax.shard_map(
        lambda *args: tuple(body(*args)),
        mesh=mesh, in_specs=(block, block, block, P()), out_specs=(block, block, block), check_vma=False,
    )
```

```python
import math

import jax
import jax.numpy as jnp
import ml_dtypes
import numpy as np
from jax import lax
from jax.experimental import pallas as pl
from jax.experimental.pallas import tpu as pltpu
from jax.sharding import PartitionSpec as P

NLON, NLAT = 12288, 1536
ROWS, CELLS = 96, 384
OUTER, INNER = 96, 128
HALF = 56
COURANT, SPIN = 0.45, 0.3
NORTH = COURANT * 2.0 * NLAT / NLON
FINAL = 260
HOLD = 2
OWNERS = 132
WINGS = HOLD + 2
MESH = pl.DeviceIdType.MESH
F32, BF16 = jnp.float32, jnp.bfloat16
GROUPS = ((0,), (1, 2))
BACK = ((1,), (2, 0))


def split(table):
    high = table.astype(ml_dtypes.bfloat16)
    low = (table - high.astype(np.float64)).astype(ml_dtypes.bfloat16)
    return high, low


def tables():
    a = np.array([3 * d + s for s in range(3) for d in range(32)])
    k1 = np.arange(HALF)
    live = (k1 <= OUTER // 2).astype(np.float64)
    angle = 2 * np.pi * ((k1[:, None] * a[None, :]) % OUTER) / OUTER
    first = np.concatenate([np.cos(angle) * live[:, None], -np.sin(angle) * live[:, None]], axis=0)
    weight = live * np.where((k1 == 0) | (k1 == OUTER // 2), 1.0, 2.0) / NLON
    last = np.concatenate([np.cos(angle) * weight[:, None], -np.sin(angle) * weight[:, None]], axis=0).T
    n = np.arange(INNER)
    turn = 2 * np.pi * (k1[:, None] * n[None, :]) / NLON
    inner = 2 * np.pi * ((n[:, None] * n[None, :]) % INNER) / INNER
    cos, sin = np.cos(inner), np.sin(inner)
    forward = np.block([[cos, -sin], [sin, cos]])
    backward = np.block([[cos, sin], [-sin, cos]])
    wave = k1[:, None] + OUTER * n[None, :]
    steep = np.sin(2 * np.pi * wave / NLON) * live[:, None]
    half_sine = np.where(live[:, None] > 0, 0.5 * np.abs(np.sin(np.pi * wave / NLON)), 1.0)
    first_high, first_low = split(first)
    last_high, last_low = split(last)
    forward_high, forward_low = split(forward)
    backward_high, backward_low = split(backward)
    grid = np.stack([np.cos(turn), np.sin(turn), steep, half_sine]).astype(np.float32)
    return (
        np.concatenate([first_high, first_low, first_high], axis=1),
        np.concatenate([last_high, last_low, last_high], axis=1),
        np.stack([forward_high, forward_low]),
        np.stack([backward_high, backward_low]),
        grid,
    )


def parts(value):
    high = value.astype(BF16)
    return high, (value - high.astype(F32)).astype(BF16)


def dot(left, right):
    return jnp.dot(left, right, preferred_element_type=F32)


def outer_step(table, value):
    high, low = parts(value)
    return dot(table.astype(BF16), jnp.concatenate([high, high, low], axis=0))


def inner_step(table, value):
    high, low = parts(value)
    table_high, table_low = table[0].astype(BF16), table[1].astype(BF16)
    return dot(high, table_high) + dot(low, table_high) + dot(high, table_low)


def kernel(
    speed_ref, h_hbm, u_hbm, v_hbm, first_hbm, last_hbm, fore_hbm, back_hbm, grid_hbm,
    h_out, u_out, v_out,
    h_ref, u_ref, v_ref, first_ref, last_ref, fore_ref, back_ref, grid_ref,
    src0, src1, relay0, relay1, recv0, recv1, snd0, snd1, home0, home1, ret0, ret1,
    tall, tall_new, wind, wind_new, wind_last, scale, packed, sides, ext,
    loads, send_a, recv_a, send_b, recv_b, send_c, recv_c, send_d, recv_d, send_x, recv_x, send_s, recv_s, send_r, recv_r,
):
    fields, outs = (h_ref, u_ref, v_ref), (h_out, u_out, v_out)
    operands = (h_hbm, u_hbm, v_hbm, first_hbm, last_hbm, fore_hbm, back_hbm, grid_hbm)
    held = (h_ref, u_ref, v_ref, first_ref, last_ref, fore_ref, back_ref, grid_ref)
    src, relay, recv = (src0, src1), (relay0, relay1), (recv0, recv1)
    snd, home, ret = (snd0, snd1), (home0, home1), (ret0, ret1)
    lat, lon = lax.axis_index("lat"), lax.axis_index("lon")
    south = lat >= 8
    band = jnp.where(south, 15 - lat, lat)
    core = lax.rem(band, 2)
    z = lax.rem(lon, 16)
    x = 2 * lax.div(lon, 16) + lax.rem(lax.div(band, 2), 2)
    line = jnp.where(band < 4, x, 7 - x)
    wide = line >= 6
    near = lax.rem(z + line, 16)
    slab = 16 * core + z
    extra = jnp.logical_and(wide, jnp.logical_and(core == 0, jnp.logical_or(near == 0, near == 15)))
    owner = jnp.logical_or(core == 1, extra)
    owners = jnp.where(wide, 18, 16)
    nth = jnp.where(wide, jnp.where(core == 1, near + 1, jnp.where(near == 0, 0, 17)), near)
    chain = 16 * line + 2 * jnp.where(line == 7, 1, 0) + nth
    source = band <= 2
    stencil = band >= 2
    my_band = jnp.where(wide, 2, lax.div(line, 3))
    my_lat = jnp.where(south, 15 - my_band, my_band)
    my_part = line - 3 * my_band

    def member(to_line, to_z, to_core):
        to_x = jnp.where(to_line < 4, to_line, 7 - to_line)
        to_band = 4 * lax.div(to_line, 4) + 2 * lax.rem(to_x, 2) + to_core
        return jnp.where(south, 15 - to_band, to_band), 16 * lax.div(to_x, 2) + to_z

    def mate(to_z, to_core):
        shift = to_core - core
        return jnp.where(south, lat - shift, lat + shift), lon - z + to_z

    def holder(n):
        to_line = jnp.where(n < 96, lax.div(n, 16), 6 + lax.div(jnp.maximum(n - 96, 0), 18))
        to_nth = n - 16 * to_line - 2 * jnp.where(to_line == 7, 1, 0)
        broad = to_line >= 6
        to_near = jnp.where(broad, jnp.clip(to_nth - 1, 0, 15), to_nth)
        to_core = jnp.where(jnp.logical_and(broad, jnp.logical_or(to_nth == 0, to_nth == 17)), 0, 1)
        return member(to_line, lax.rem(to_near + 16 - to_line, 16), to_core)

    def chip(k):
        away = 8 - lax.div(k + 1, 2)
        return lax.rem(z + 16 + jnp.where(lax.rem(k, 2) == 1, away, -away), 16)

    def same(target):
        return jnp.logical_and(target[0] == lat, target[1] == lon)

    def remote(here, there, send_sem, recv_sem, target):
        pltpu.make_async_remote_copy(
            src_ref=here, dst_ref=there, send_sem=send_sem, recv_sem=recv_sem, device_id=target, device_id_type=MESH
        ).start()

    def send(here, there, send_sem, recv_sem, target):
        own = same(target)

        @pl.when(own)
        def _():
            pltpu.make_async_copy(here, there, recv_sem).start()

        @pl.when(jnp.logical_not(own))
        def _():
            remote(here, there, send_sem, recv_sem, target)

    def landed(ref, sem):
        pltpu.make_async_copy(ref, ref, sem).wait()

    def part_start(k, size):
        return jnp.where(south, ROWS - size * (k + 1), size * k)

    def owner_start(i):
        return HOLD * jnp.where(south, owners - 1 - i, i)

    def each_size(act):
        pl.when(jnp.logical_not(wide))(lambda: act(32))
        pl.when(wide)(lambda: act(36))

    right = jnp.where(lon == 31, 0, lon + 1)
    left = jnp.where(lon == 0, 31, lon - 1)
    before = chain + jnp.where(south, 1, -1)
    after = chain + jnp.where(south, -1, 1)
    has_before = jnp.logical_and(owner, jnp.logical_and(before >= 0, before < OWNERS))
    has_after = jnp.logical_and(owner, jnp.logical_and(after >= 0, after < OWNERS))
    before_device, after_device = holder(jnp.clip(before, 0, OWNERS - 1)), holder(jnp.clip(after, 0, OWNERS - 1))

    barrier = pltpu.get_barrier_semaphore()

    def greet(target):
        pl.semaphore_signal(barrier, inc=1, device_id=target, device_id_type=MESH)

    def greet_other(target):
        pl.when(jnp.logical_not(same(target)))(lambda: greet(target))

    def greet_chip(k, carry):
        to = lax.rem(z + k, 16)
        greet(mate(to, 1))
        pl.when(owner)(lambda: greet(mate(to, 0)))
        return carry

    lax.fori_loop(1, 16, greet_chip, 0)
    greeted = jnp.where(owner, 30, 15)
    own_chip = jnp.logical_or(core == 0, owner)
    pl.when(own_chip)(lambda: greet(mate(z, 1 - core)))
    greeted += own_chip.astype(jnp.int32)
    for end in (0, 15):
        there = lax.rem(end + 16 - line, 16)
        meant = jnp.logical_and(wide, jnp.logical_not(jnp.logical_or(owner, there == z)))
        pl.when(meant)(lambda there=there: greet(mate(there, 0)))
        greeted += meant.astype(jnp.int32)
    meant = jnp.logical_not(same((my_lat, slab)))
    pl.when(meant)(lambda: greet((my_lat, slab)))
    greeted += meant.astype(jnp.int32)
    for k in range(3):
        target = member(jnp.minimum(3 * band + k, 7), z, lax.div(lon, 16))
        meant = jnp.logical_or(band < 2, jnp.logical_and(band == 2, k < 2))
        meant = jnp.logical_and(meant, jnp.logical_not(same(target)))
        pl.when(meant)(lambda target=target: greet(target))
        greeted += meant.astype(jnp.int32)
    for meant, target in (
        (has_before, before_device), (has_after, after_device), (stencil, (lat, left)), (stencil, (lat, right)),
        (jnp.logical_and(stencil, lat > 2), (lat - 1, lon)), (jnp.logical_and(stencil, lat < 13), (lat + 1, lon)),
    ):
        pl.when(meant)(lambda target=target: greet(target))
        greeted += meant.astype(jnp.int32)

    def load(*indices):
        for index in indices:
            pltpu.make_async_copy(operands[index], held[index], loads.at[index]).start()

    def loaded(*indices):
        for index in indices:
            pltpu.make_async_copy(operands[index], held[index], loads.at[index]).wait()

    load(0, 1, 2)
    pl.when(owner)(lambda: load(3, 4, 5, 6, 7))

    def gather(g):
        per = 3 * len(GROUPS[g])
        for pos, f in enumerate(GROUPS[g]):
            for s in range(3):
                src[g][pl.ds(3 * pos + s, ROWS, stride=per), :] = fields[f][0, :, 128 * s : 128 * (s + 1)]

    def send_rows(g):
        per = 3 * len(GROUPS[g])

        def one(k, size):
            send(
                src[g].at[pl.ds(part_start(k, size) * per, size * per)], relay[g].at[pl.ds(0, size * per)],
                send_a.at[g, k], recv_a.at[g], member(3 * band + k, z, lax.div(lon, 16)),
            )

        @pl.when(band < 2)
        def _():
            for k in range(3):
                one(k, 32)

        @pl.when(band == 2)
        def _():
            for k in range(2):
                one(k, 36)

    loaded(0)
    pl.when(source)(lambda: gather(0))
    pl.semaphore_wait(barrier, greeted)
    pl.when(source)(lambda: send_rows(0))
    loaded(1, 2)

    @pl.when(source)
    def _():
        gather(1)
        send_rows(1)

    @pl.when(stencil)
    def _():
        lane = lax.broadcasted_iota(jnp.int32, (ROWS, 128), 1)
        high = [ref[0, :, 256:384] for ref in fields]
        low = [ref[0, :, 0:128] for ref in fields]
        packed[0] = jnp.where(
            lane >= 124, high[0], jnp.where(lane >= 120, pltpu.roll(high[1], 124, 1), pltpu.roll(high[2], 120, 1))
        )
        packed[1] = jnp.where(lane < 4, low[0], jnp.where(lane < 8, pltpu.roll(low[1], 4, 1), pltpu.roll(low[2], 8, 1)))
        remote(packed.at[0], sides.at[0], send_s.at[0], recv_s.at[0], (lat, right))
        remote(packed.at[1], sides.at[1], send_s.at[1], recv_s.at[1], (lat, left))

    for g in range(2):
        per = 3 * len(GROUPS[g])
        each_size(lambda size, g=g, per=per: landed(relay[g].at[pl.ds(0, size * per)], recv_a.at[g]))

        def to_owner(how, i, target, g=g, per=per):
            how(
                relay[g].at[pl.ds(owner_start(i) * per, HOLD * per)],
                recv[g].at[pl.ds(slab * (HOLD * per), HOLD * per)],
                send_b.at[g], recv_b.at[g], target,
            )

        def spread(k, carry, to_owner=to_owner):
            to = chip(k)
            to_owner(remote, lax.rem(to + line, 16) + jnp.where(wide, 1, 0), mate(to, 1))
            return carry

        @pl.when(wide)
        def _(to_owner=to_owner):
            for i in (0, 17):
                to_owner(send, i, mate(lax.rem(min(i, 15) + 16 - line, 16), 0))

        lax.fori_loop(0, 15, spread, 0)
        to_owner(send, near + jnp.where(wide, 1, 0), mate(z, 1))

    @pl.when(stencil)
    def _():
        landed(sides.at[0], recv_s.at[0])
        landed(sides.at[1], recv_s.at[1])
        lane = lax.broadcasted_iota(jnp.int32, (ROWS, 128), 1)
        for f in range(3):
            ext[f, 8 : 8 + ROWS, 0:CELLS] = fields[f][0]
            east_side, west_side = sides[1], sides[0]
            if f:
                east_side, west_side = pltpu.roll(east_side, 128 - 4 * f, 1), pltpu.roll(west_side, 4 * f, 1)
            ext[f, 8 : 8 + ROWS, CELLS : CELLS + 128] = jnp.where(lane < 64, east_side, west_side)

        @pl.when(lat > 2)
        def _():
            remote(ext.at[:, 8:16, :], ext.at[:, 104:112, :], send_r.at[0], recv_r.at[0], (lat - 1, lon))

        @pl.when(lat < 13)
        def _():
            remote(ext.at[:, 96:104, :], ext.at[:, 0:8, :], send_r.at[1], recv_r.at[1], (lat + 1, lon))

        @pl.when(lat == 2)
        def _():
            ext[:, 0:8, :] = jnp.zeros((3, 8, 512), F32)

        @pl.when(lat == 13)
        def _():
            ext[:, 104:112, :] = jnp.zeros((3, 8, 512), F32)

    def transform(g):
        size = HOLD * 3 * len(GROUPS[g])
        order = [(row, pos) for row in range(HOLD) for pos in range(len(GROUPS[g]))]
        grids = [
            jnp.concatenate(
                [recv[g][pl.ds(row * (size // HOLD) + 3 * pos + s, 32, stride=size), :] for s in range(3)], axis=0
            )
            for row, pos in order
        ]
        mixed = outer_step(first_ref[...], jnp.concatenate(grids, axis=1))
        cos, sin = grid_ref[0], grid_ref[1]
        twisted = []
        for n in range(len(order)):
            real, imag = mixed[:HALF, 128 * n : 128 * (n + 1)], mixed[HALF:, 128 * n : 128 * (n + 1)]
            twisted.append(jnp.concatenate([real * cos + imag * sin, imag * cos - real * sin], axis=1))
        spectrum = inner_step(fore_ref, jnp.concatenate(twisted, axis=0))
        return {
            key: (spectrum[HALF * n : HALF * (n + 1), :128], spectrum[HALF * n : HALF * (n + 1), 128:])
            for n, key in enumerate(order)
        }

    def restore(g, spectra):
        size = HOLD * 3 * len(BACK[g])
        order = list(spectra)
        cos, sin = grid_ref[0], grid_ref[1]
        back = inner_step(
            back_ref, jnp.concatenate([jnp.concatenate(spectra[key], axis=1) for key in order], axis=0)
        )
        spun = []
        for n in range(len(order)):
            real, imag = back[HALF * n : HALF * (n + 1), :128], back[HALF * n : HALF * (n + 1), 128:]
            spun.append(jnp.concatenate([real * cos - imag * sin, imag * cos + real * sin], axis=0))
        cells = outer_step(last_ref[...], jnp.concatenate(spun, axis=1))
        for n, (row, pos) in enumerate(order):
            for s in range(3):
                snd[g][pl.ds(row * (size // HOLD) + 3 * pos + s, 32, stride=size), :] = cells[
                    32 * s : 32 * (s + 1), 128 * n : 128 * (n + 1)
                ]

    def put(ref, index, pair):
        ref[(*index, slice(0, HALF))] = pair[0]
        ref[(*index, slice(HALF, 2 * HALF))] = pair[1]

    def get(ref, *index):
        return ref[(*index, slice(0, HALF))], ref[(*index, slice(HALF, 2 * HALF))]

    row0 = jnp.where(south, NLAT - HOLD - HOLD * chain, HOLD * chain)

    def polar(row):
        steps = jnp.where(south, NLAT - 1 - row, row)
        return jnp.abs(jnp.full((1, 128), steps, jnp.int32).astype(F32) + 0.5) * (math.pi / NLAT)

    def cosine(w):
        return jnp.sin(polar(row0 + w - 1))

    def prepare():
        speed = speed_ref[0]
        share_of_pole = jnp.where(south, SPIN, -SPIN).astype(F32)
        for w in range(WINGS):
            there = 1.0
            if w == 0:
                there = jnp.where(has_before, 1.0, 0.0).astype(F32)
            if w == WINGS - 1:
                there = jnp.where(has_after, 1.0, 0.0).astype(F32)
            angle = polar(row0 + w - 1)
            share = 1.0 / jnp.maximum(grid_ref[3], jnp.sin(angle))
            keep = share * (jnp.sin(angle) * there)
            slope = share * (COURANT * grid_ref[2])
            scale[w, 0] = slope
            scale[w, 1] = keep * (share_of_pole * jnp.cos(angle))
            scale[w, 2] = keep * (0.5 * NORTH)
            if 0 < w < WINGS - 1:
                scale[w, 3] = speed * slope
                scale[w, 4] = share * (speed * (0.5 * NORTH) * cosine(w - 1))
                scale[w, 5] = share * (speed * (0.5 * NORTH) * cosine(w + 1))

    def push_east(heights, old, new, w):
        mid, east, north = get(heights, w + 1), get(old, w, 0), get(old, w, 1)
        slope, swirl = scale[w, 0], scale[w, 1]
        put(new, (w, 0), (
            east[0] + slope * mid[1] + swirl * north[0],
            east[1] - slope * mid[0] + swirl * north[1],
        ))

    def push_north(heights, old, new, w):
        low, high = get(heights, w), get(heights, w + 2)
        east, north = get(old, w, 0), get(old, w, 1)
        swirl, climb = scale[w, 1], scale[w, 2]
        put(new, (w, 1), tuple(north[p] - climb * (high[p] - low[p]) - swirl * east[p] for p in range(2)))

    def pushed_height(heights, winds, w):
        mid, east = get(heights, w + 1), get(winds, w, 0)
        low, high = get(winds, w - 1, 1), get(winds, w + 1, 1)
        slope, below, above = scale[w, 3], scale[w, 4], scale[w, 5]
        return (
            mid[0] + slope * east[1] - (above * high[0] - below * low[0]),
            mid[1] - slope * east[0] - (above * high[1] - below * low[1]),
        )

    def trade(e, ref, wing):
        @pl.when(has_before)
        def _():
            remote(
                ref.at[pl.ds(wing, wing)], ref.at[pl.ds(wing + HOLD, wing)],
                send_x.at[e, 0], recv_x.at[e, 1], before_device,
            )

        @pl.when(has_after)
        def _():
            remote(ref.at[pl.ds(HOLD, wing)], ref.at[pl.ds(0, wing)], send_x.at[e, 1], recv_x.at[e, 0], after_device)

    def traded(e, ref, wing):
        pl.when(has_before)(lambda: landed(ref.at[pl.ds(0, wing)], recv_x.at[e, 0]))
        pl.when(has_after)(lambda: landed(ref.at[pl.ds(wing + HOLD, wing)], recv_x.at[e, 1]))

    def send_back(g):
        size = HOLD * 3 * len(BACK[g])
        start = owner_start(nth) * (size // HOLD)

        def one(how, to_z, to_core):
            how(
                snd[g].at[pl.ds((16 * to_core + to_z) * size, size)], home[g].at[pl.ds(start, size)],
                send_c.at[g], recv_c.at[g], mate(to_z, to_core),
            )

        def both(k, carry):
            to = chip(k)
            one(remote, to, 0)
            one(remote, to, 1)
            return carry

        lax.fori_loop(0, 15, both, 0)
        one(send, z, 0)
        one(send, z, 1)

    @pl.when(owner)
    def _():
        loaded(3, 4, 5, 6, 7)
        prepare()

        @pl.when(jnp.logical_not(has_before))
        def _():
            tall[0:2] = jnp.zeros((2, 2 * HALF, 128), F32)
            tall_new[0:2] = jnp.zeros((2, 2 * HALF, 128), F32)
            wind[0] = jnp.zeros((2, 2 * HALF, 128), F32)

        @pl.when(jnp.logical_not(has_after))
        def _():
            tall[2 + HOLD : 4 + HOLD] = jnp.zeros((2, 2 * HALF, 128), F32)
            tall_new[2 + HOLD : 4 + HOLD] = jnp.zeros((2, 2 * HALF, 128), F32)
            wind[1 + HOLD] = jnp.zeros((2, 2 * HALF, 128), F32)

        landed(recv[0], recv_b.at[0])
        for (row, _), pair in transform(0).items():
            put(tall, (2 + row,), pair)
        trade(0, tall, 2)
        landed(recv[1], recv_b.at[1])
        for (row, which), pair in transform(1).items():
            put(wind, (1 + row, which), pair)
        trade(1, wind, 1)
        traded(0, tall, 2)
        traded(1, wind, 1)
        for w in range(WINGS):
            push_east(tall, wind, wind_new, w)
            push_north(tall, wind, wind_new, w)
        for w in range(1, 1 + HOLD):
            put(tall_new, (1 + w,), pushed_height(tall, wind_new, w))
        trade(2, tall_new, 2)
        for w in range(1, 1 + HOLD):
            push_east(tall_new, wind_new, wind_last, w)
        restore(0, {(row, 0): get(wind_last, 1 + row, 0) for row in range(HOLD)})
        send_back(0)
        traded(2, tall_new, 2)
        for w in range(WINGS):
            push_north(tall_new, wind_new, wind_last, w)
        last = {(row, 0): get(wind_last, 1 + row, 1) for row in range(HOLD)}
        last.update({(row, 1): pushed_height(tall_new, wind_last, 1 + row) for row in range(HOLD)})
        restore(1, last)
        send_back(1)

    for g in range(2):
        per = 3 * len(BACK[g])

        def deliver(size, g=g, per=per):
            landed(home[g].at[pl.ds(0, size * per)], recv_c.at[g])
            send(
                home[g].at[pl.ds(0, size * per)], ret[g].at[pl.ds(part_start(my_part, size) * per, size * per)],
                send_d.at[g], recv_d.at[g, my_part], (my_lat, slab),
            )

        each_size(deliver)

    @pl.when(stencil)
    def _():
        @pl.when(lat > 2)
        def _():
            landed(ext.at[:, 0:8, :], recv_r.at[1])

        @pl.when(lat < 13)
        def _():
            landed(ext.at[:, 104:112, :], recv_r.at[0])

        row = lax.broadcasted_iota(jnp.int32, (ROWS + 16, 128), 0) + (ROWS * lat - 8)
        latitude = (row.astype(F32) + (0.5 - NLAT // 2)) * (math.pi / NLAT)
        wide_cos = jnp.concatenate([jnp.cos(latitude)] * 4, axis=1)
        spin = jnp.concatenate([SPIN * jnp.sin(latitude)] * 4, axis=1)
        inverse = 1.0 / wide_cos
        east_scale = (0.5 * COURANT) * inverse
        speed = speed_ref[0]

        def across(value):
            return pltpu.roll(value, 511, 1) - pltpu.roll(value, 1, 1)

        def along(value):
            return pltpu.roll(value, ROWS + 15, 0) - pltpu.roll(value, 1, 0)

        height, east, north = ext[0], ext[1], ext[2]
        for _step in range(2):
            east_inc = spin * north - east_scale * across(height)
            north_inc = (-0.5 * NORTH) * along(height) - spin * east
            east, north = east + east_inc, north + north_inc
            spread_out = east_scale * across(east) + (0.5 * NORTH) * inverse * along(north * wide_cos)
            height = height - speed * spread_out
        for out, value in zip(outs, (height, east, north)):
            out[0] = value[8 : 8 + ROWS, 0:CELLS]

    def back(f, s):
        g = 0 if f in BACK[0] else 1
        return ret[g][pl.ds(3 * BACK[g].index(f) + s, ROWS, stride=3 * len(BACK[g])), :]

    @pl.when(band < 2)
    def _():
        for g in range(2):
            per = 3 * len(BACK[g])
            for k in range(3):
                landed(ret[g].at[pl.ds(part_start(k, 32) * per, 32 * per)], recv_d.at[g, k])
            for f in BACK[g]:
                for s in range(3):
                    outs[f][0, :, 128 * s : 128 * (s + 1)] = back(f, s)

    @pl.when(band == 2)
    def _():
        row = lax.broadcasted_iota(jnp.int32, (ROWS, 128), 0)
        from_pole = jnp.where(south, ROWS - 1 - row, row) + 2 * ROWS
        for g in range(2):
            per = 3 * len(BACK[g])
            for k in range(2):
                landed(ret[g].at[pl.ds(part_start(k, 36) * per, 36 * per)], recv_d.at[g, k])
            for f in BACK[g]:
                for s in range(3):
                    lanes = slice(128 * s, 128 * (s + 1))
                    outs[f][0, :, lanes] = jnp.where(from_pole < FINAL, back(f, s), outs[f][0, :, lanes])

    for g in range(2):
        per = 3 * len(GROUPS[g])

        def left_parts(size, parts, g=g, per=per):
            for k in range(parts):
                other = jnp.logical_not(same(member(3 * band + k, z, lax.div(lon, 16))))
                pl.when(other)(lambda k=k: landed(src[g].at[pl.ds(0, size * per)], send_a.at[g, k]))

        pl.when(band < 2)(lambda f=left_parts: f(32, 3))
        pl.when(band == 2)(lambda f=left_parts: f(36, 2))
        for case, count in (
            (jnp.logical_and(jnp.logical_not(wide), owner), 15),
            (jnp.logical_and(jnp.logical_not(wide), jnp.logical_not(owner)), 16),
            (jnp.logical_and(wide, owner), 17),
            (jnp.logical_and(wide, jnp.logical_not(owner)), 18),
        ):
            pl.when(case)(
                lambda g=g, n=count * HOLD * per: landed(relay[g].at[pl.ds(0, n)], send_b.at[g])
            )
        ret_per = 3 * len(BACK[g])
        pl.when(owner)(lambda g=g, per=ret_per: landed(snd[g].at[pl.ds(0, 31 * HOLD * per)], send_c.at[g]))

        @pl.when(jnp.logical_not(same((my_lat, slab))))
        def _(g=g, per=ret_per):
            each_size(lambda size: landed(home[g].at[pl.ds(0, size * per)], send_d.at[g]))

    @pl.when(stencil)
    def _():
        for side in range(2):
            landed(packed.at[side], send_s.at[side])

        @pl.when(lat > 2)
        def _():
            landed(ext.at[:, 8:16, :], send_r.at[0])

        @pl.when(lat < 13)
        def _():
            landed(ext.at[:, 96:104, :], send_r.at[1])

    for e, (ref, wing) in enumerate(((tall, 2), (wind, 1), (tall_new, 2))):
        pl.when(has_before)(lambda e=e, ref=ref, wing=wing: landed(ref.at[pl.ds(0, wing)], send_x.at[e, 0]))
        pl.when(has_after)(lambda e=e, ref=ref, wing=wing: landed(ref.at[pl.ds(0, wing)], send_x.at[e, 1]))


def write(h_ref, u_ref, v_ref, h_out, u_out, v_out, sems):
    copies = [
        pltpu.make_async_copy(here, there, sems.at[n])
        for n, (here, there) in enumerate(((h_ref, h_out), (u_ref, u_out), (v_ref, v_out)))
    ]
    for copy in copies:
        copy.start()
    for copy in copies:
        copy.wait()


def body(height, east_wind, north_wind, wave_speed_sq):
    constants = [np.asarray(table, np.float32) for table in tables()]
    block = jax.ShapeDtypeStruct((1, ROWS, CELLS), F32)
    pairs = []
    for groups, rows in ((GROUPS, ROWS), (GROUPS, 36), (GROUPS, 32 * HOLD), (BACK, 32 * HOLD), (BACK, 36), (BACK, ROWS)):
        pairs += [pltpu.VMEM((rows * 3 * len(group), 128), F32) for group in groups]
    dma = pltpu.SemaphoreType.DMA
    vmem = pl.BlockSpec(memory_space=pltpu.VMEM)
    results = pl.pallas_call(
        kernel,
        out_shape=[pltpu.VMEM(block.shape, F32)] * 3,
        in_specs=[pl.BlockSpec(memory_space=pltpu.SMEM)] + [pl.BlockSpec(memory_space=pl.ANY)] * 8,
        out_specs=[vmem] * 3,
        scratch_shapes=[
            *[pltpu.VMEM((1, ROWS, CELLS), F32)] * 3,
            *[pltpu.VMEM(table.shape, table.dtype) for table in constants],
            *pairs,
            *[pltpu.VMEM((HOLD + 4, 2 * HALF, 128), F32)] * 2,
            *[pltpu.VMEM((WINGS, 2, 2 * HALF, 128), F32)] * 3,
            pltpu.VMEM((WINGS, 6, HALF, 128), F32),
            pltpu.VMEM((2, ROWS, 128), F32),
            pltpu.VMEM((2, ROWS, 128), F32),
            pltpu.VMEM((3, ROWS + 16, 512), F32),
            dma((8,)), dma((2, 3)), dma((2,)), dma((2,)), dma((2,)), dma((2,)), dma((2,)), dma((2,)), dma((2, 3)),
            dma((3, 2)), dma((3, 2)), dma((2,)), dma((2,)), dma((2,)), dma((2,)),
        ],
        compiler_params=pltpu.CompilerParams(
            collective_id=0, has_side_effects=True, vmem_limit_bytes=60 * 1024 * 1024
        ),
        name="substeps",
    )(wave_speed_sq, height, east_wind, north_wind, *constants)
    return pl.pallas_call(
        write,
        out_shape=[block] * 3,
        in_specs=[vmem] * 3,
        out_specs=[pl.BlockSpec(memory_space=pl.ANY)] * 3,
        scratch_shapes=[dma((3,))],
        compiler_params=pltpu.CompilerParams(vmem_limit_bytes=16 * 1024 * 1024),
        name="write",
    )(*results)


def solution(mesh):
    block = P(None, "lat", "lon")
    return jax.shard_map(
        lambda *args: tuple(body(*args)),
        mesh=mesh, in_specs=(block, block, block, P()), out_specs=(block, block, block), check_vma=False,
    )
```

```python
import math

import jax
import jax.numpy as jnp
import ml_dtypes
import numpy as np
from jax import lax
from jax.experimental import pallas as pl
from jax.experimental.pallas import tpu as pltpu
from jax.sharding import PartitionSpec as P

NLON, NLAT = 12288, 1536
ROWS, CELLS = 96, 384
OUTER, INNER = 96, 128
HALF = 56
COURANT, SPIN = 0.45, 0.3
NORTH = COURANT * 2.0 * NLAT / NLON
FINAL = 260
HOLD = 2
OWNERS = 132
WINGS = HOLD + 2
MESH = pl.DeviceIdType.MESH
F32, BF16 = jnp.float32, jnp.bfloat16
GROUPS = ((0,), (1, 2))
BACK = ((1,), (2, 0))


def split(table):
    high = table.astype(ml_dtypes.bfloat16)
    low = (table - high.astype(np.float64)).astype(ml_dtypes.bfloat16)
    return high, low


def tables():
    a = np.array([3 * d + s for s in range(3) for d in range(32)])
    k1 = np.arange(HALF)
    live = (k1 <= OUTER // 2).astype(np.float64)
    angle = 2 * np.pi * ((k1[:, None] * a[None, :]) % OUTER) / OUTER
    first = np.concatenate([np.cos(angle) * live[:, None], -np.sin(angle) * live[:, None]], axis=0)
    weight = live * np.where((k1 == 0) | (k1 == OUTER // 2), 1.0, 2.0) / NLON
    last = np.concatenate([np.cos(angle) * weight[:, None], -np.sin(angle) * weight[:, None]], axis=0).T
    n = np.arange(INNER)
    turn = 2 * np.pi * (k1[:, None] * n[None, :]) / NLON
    inner = 2 * np.pi * ((n[:, None] * n[None, :]) % INNER) / INNER
    cos, sin = np.cos(inner), np.sin(inner)
    forward = np.block([[cos, -sin], [sin, cos]])
    backward = np.block([[cos, sin], [-sin, cos]])
    wave = k1[:, None] + OUTER * n[None, :]
    steep = np.sin(2 * np.pi * wave / NLON) * live[:, None]
    half_sine = np.where(live[:, None] > 0, 0.5 * np.abs(np.sin(np.pi * wave / NLON)), 1.0)
    first_high, first_low = split(first)
    last_high, last_low = split(last)
    forward_high, forward_low = split(forward)
    backward_high, backward_low = split(backward)
    grid = np.stack([np.cos(turn), np.sin(turn), steep, half_sine]).astype(np.float32)
    return (
        np.concatenate([first_high, first_low, first_high], axis=1),
        np.concatenate([last_high, last_low, last_high], axis=1),
        np.stack([forward_high, forward_low]),
        np.stack([backward_high, backward_low]),
        grid,
    )


def parts(value):
    high = value.astype(BF16)
    return high, (value - high.astype(F32)).astype(BF16)


def dot(left, right):
    return jnp.dot(left, right, preferred_element_type=F32)


def outer_step(table, value):
    high, low = parts(value)
    return dot(table.astype(BF16), jnp.concatenate([high, high, low], axis=0))


def inner_step(table, value):
    high, low = parts(value)
    table_high, table_low = table[0].astype(BF16), table[1].astype(BF16)
    return dot(high, table_high) + dot(low, table_high) + dot(high, table_low)


def kernel(
    speed_ref, h_hbm, u_hbm, v_hbm, first_hbm, last_hbm, fore_hbm, back_hbm, grid_hbm,
    h_out, u_out, v_out,
    h_ref, u_ref, v_ref, first_ref, last_ref, fore_ref, back_ref, grid_ref,
    src0, src1, relay0, relay1, recv0, recv1, snd0, snd1, home0, home1, ret0, ret1,
    tall, tall_new, wind, wind_new, wind_last, scale, packed, sides, ext,
    go, loads, send_a, recv_a, send_b, recv_b, send_c, recv_c, send_d, recv_d, send_x, recv_x, send_s, recv_s, send_r, recv_r,
):
    fields, outs = (h_ref, u_ref, v_ref), (h_out, u_out, v_out)
    operands = (h_hbm, u_hbm, v_hbm, first_hbm, last_hbm, fore_hbm, back_hbm, grid_hbm)
    held = (h_ref, u_ref, v_ref, first_ref, last_ref, fore_ref, back_ref, grid_ref)
    src, relay, recv = (src0, src1), (relay0, relay1), (recv0, recv1)
    snd, home, ret = (snd0, snd1), (home0, home1), (ret0, ret1)
    lat, lon = lax.axis_index("lat"), lax.axis_index("lon")
    south = lat >= 8
    band = jnp.where(south, 15 - lat, lat)
    core = lax.rem(band, 2)
    z = lax.rem(lon, 16)
    x = 2 * lax.div(lon, 16) + lax.rem(lax.div(band, 2), 2)
    line = jnp.where(band < 4, x, 7 - x)
    wide = line >= 6
    near = lax.rem(z + line, 16)
    slab = 16 * core + z
    extra = jnp.logical_and(wide, jnp.logical_and(core == 0, jnp.logical_or(near == 0, near == 15)))
    owner = jnp.logical_or(core == 1, extra)
    owners = jnp.where(wide, 18, 16)
    nth = jnp.where(wide, jnp.where(core == 1, near + 1, jnp.where(near == 0, 0, 17)), near)
    chain = 16 * line + 2 * jnp.where(line == 7, 1, 0) + nth
    source = band <= 2
    stencil = band >= 2
    my_band = jnp.where(wide, 2, lax.div(line, 3))
    my_lat = jnp.where(south, 15 - my_band, my_band)
    my_part = line - 3 * my_band

    def member(to_line, to_z, to_core):
        to_x = jnp.where(to_line < 4, to_line, 7 - to_line)
        to_band = 4 * lax.div(to_line, 4) + 2 * lax.rem(to_x, 2) + to_core
        return jnp.where(south, 15 - to_band, to_band), 16 * lax.div(to_x, 2) + to_z

    def mate(to_z, to_core):
        shift = to_core - core
        return jnp.where(south, lat - shift, lat + shift), lon - z + to_z

    def holder(n):
        to_line = jnp.where(n < 96, lax.div(n, 16), 6 + lax.div(jnp.maximum(n - 96, 0), 18))
        to_nth = n - 16 * to_line - 2 * jnp.where(to_line == 7, 1, 0)
        broad = to_line >= 6
        to_near = jnp.where(broad, jnp.clip(to_nth - 1, 0, 15), to_nth)
        to_core = jnp.where(jnp.logical_and(broad, jnp.logical_or(to_nth == 0, to_nth == 17)), 0, 1)
        return member(to_line, lax.rem(to_near + 16 - to_line, 16), to_core)

    def chip(k):
        away = 8 - lax.div(k + 1, 2)
        return lax.rem(z + 16 + jnp.where(lax.rem(k, 2) == 1, away, -away), 16)

    def same(target):
        return jnp.logical_and(target[0] == lat, target[1] == lon)

    def remote(here, there, send_sem, recv_sem, target):
        pltpu.make_async_remote_copy(
            src_ref=here, dst_ref=there, send_sem=send_sem, recv_sem=recv_sem, device_id=target, device_id_type=MESH
        ).start()

    def send(here, there, send_sem, recv_sem, target):
        own = same(target)

        @pl.when(own)
        def _():
            pltpu.make_async_copy(here, there, recv_sem).start()

        @pl.when(jnp.logical_not(own))
        def _():
            remote(here, there, send_sem, recv_sem, target)

    def landed(ref, sem):
        pltpu.make_async_copy(ref, ref, sem).wait()

    def part_start(k, size):
        return jnp.where(south, ROWS - size * (k + 1), size * k)

    def owner_start(i):
        return HOLD * jnp.where(south, owners - 1 - i, i)

    def each_size(act):
        pl.when(jnp.logical_not(wide))(lambda: act(32))
        pl.when(wide)(lambda: act(36))

    right = jnp.where(lon == 31, 0, lon + 1)
    left = jnp.where(lon == 0, 31, lon - 1)
    before = chain + jnp.where(south, 1, -1)
    after = chain + jnp.where(south, -1, 1)
    has_before = jnp.logical_and(owner, jnp.logical_and(before >= 0, before < OWNERS))
    has_after = jnp.logical_and(owner, jnp.logical_and(after >= 0, after < OWNERS))
    before_device, after_device = holder(jnp.clip(before, 0, OWNERS - 1)), holder(jnp.clip(after, 0, OWNERS - 1))

    barrier = pltpu.get_barrier_semaphore()

    def greet(target):
        pl.semaphore_signal(barrier, inc=1, device_id=target, device_id_type=MESH)

    def greet_other(target):
        pl.when(jnp.logical_not(same(target)))(lambda: greet(target))

    def helper(of_line, to_z):
        of_x = jnp.where(of_line < 4, of_line, 7 - of_line)
        return member(7 - of_x, to_z, lax.div(of_line, 4))

    helps = band >= 4
    helped = jnp.where(core == 1, 7 - x, x)

    def greet_helper(k, carry):
        greet(helper(line, lax.rem(z + k, 16)))
        return carry

    my_helper = helper(line, z)
    helped_from_afar = jnp.logical_not(same(my_helper))

    @pl.when(owner)
    def _():
        lax.fori_loop(1, 16, greet_helper, 0)

    pl.when(jnp.logical_and(owner, helped_from_afar))(lambda: greet(my_helper))
    pl.when(helped_from_afar)(lambda: greet(my_helper))
    greeted = jnp.where(helps, jnp.where(helped >= 6, 18, 16) + 2 - 2 * core, 0)
    pl.when(jnp.logical_not(same((my_lat, slab))))(lambda: greet((my_lat, slab)))
    for k in range(3):
        target = member(jnp.minimum(3 * band + k, 7), z, lax.div(lon, 16))
        meant = jnp.logical_or(band < 2, jnp.logical_and(band == 2, k < 2))
        meant = jnp.logical_and(meant, jnp.logical_not(same(target)))
        greeted += meant.astype(jnp.int32)
    for meant, target in (
        (has_before, before_device), (has_after, after_device), (stencil, (lat, left)), (stencil, (lat, right)),
        (jnp.logical_and(stencil, lat > 2), (lat - 1, lon)), (jnp.logical_and(stencil, lat < 13), (lat + 1, lon)),
    ):
        pl.when(meant)(lambda target=target: greet(target))
        greeted += meant.astype(jnp.int32)

    def load(*indices):
        for index in indices:
            pltpu.make_async_copy(operands[index], held[index], loads.at[index]).start()

    def loaded(*indices):
        for index in indices:
            pltpu.make_async_copy(operands[index], held[index], loads.at[index]).wait()

    load(0, 1, 2)
    pl.when(owner)(lambda: load(3, 4, 5, 6, 7))

    def gather(g):
        per = 3 * len(GROUPS[g])
        for pos, f in enumerate(GROUPS[g]):
            for s in range(3):
                src[g][pl.ds(3 * pos + s, ROWS, stride=per), :] = fields[f][0, :, 128 * s : 128 * (s + 1)]

    def send_rows(g):
        per = 3 * len(GROUPS[g])

        def one(k, size):
            send(
                src[g].at[pl.ds(part_start(k, size) * per, size * per)], relay[g].at[pl.ds(0, size * per)],
                send_a.at[g, k], recv_a.at[g], member(3 * band + k, z, lax.div(lon, 16)),
            )

        @pl.when(band < 2)
        def _():
            for k in range(3):
                one(k, 32)

        @pl.when(band == 2)
        def _():
            for k in range(2):
                one(k, 36)

    loaded(0)
    pl.when(source)(lambda: gather(0))
    pl.semaphore_wait(barrier, greeted)

    @pl.when(helps)
    def _():
        for to_core in range(2):
            target = member(helped, z, to_core)
            pl.when(jnp.logical_not(same(target)))(
                lambda target=target: pl.semaphore_signal(go, inc=1, device_id=target, device_id_type=MESH)
            )

    pl.when(source)(lambda: send_rows(0))
    loaded(1, 2)

    @pl.when(source)
    def _():
        gather(1)
        send_rows(1)

    @pl.when(stencil)
    def _():
        lane = lax.broadcasted_iota(jnp.int32, (ROWS, 128), 1)
        high = [ref[0, :, 256:384] for ref in fields]
        low = [ref[0, :, 0:128] for ref in fields]
        packed[0] = jnp.where(
            lane >= 124, high[0], jnp.where(lane >= 120, pltpu.roll(high[1], 124, 1), pltpu.roll(high[2], 120, 1))
        )
        packed[1] = jnp.where(lane < 4, low[0], jnp.where(lane < 8, pltpu.roll(low[1], 4, 1), pltpu.roll(low[2], 8, 1)))
        remote(packed.at[0], sides.at[0], send_s.at[0], recv_s.at[0], (lat, right))
        remote(packed.at[1], sides.at[1], send_s.at[1], recv_s.at[1], (lat, left))

    pl.when(helped_from_afar)(lambda: pl.semaphore_wait(go, 1))
    for g in range(2):
        per = 3 * len(GROUPS[g])
        each_size(lambda size, g=g, per=per: landed(relay[g].at[pl.ds(0, size * per)], recv_a.at[g]))

        def to_owner(how, i, target, g=g, per=per):
            how(
                relay[g].at[pl.ds(owner_start(i) * per, HOLD * per)],
                recv[g].at[pl.ds(slab * (HOLD * per), HOLD * per)],
                send_b.at[g], recv_b.at[g], target,
            )

        def spread(k, carry, to_owner=to_owner):
            to = chip(k)
            to_owner(remote, lax.rem(to + line, 16) + jnp.where(wide, 1, 0), mate(to, 1))
            return carry

        @pl.when(wide)
        def _(to_owner=to_owner):
            for i in (0, 17):
                to_owner(send, i, mate(lax.rem(min(i, 15) + 16 - line, 16), 0))

        lax.fori_loop(0, 15, spread, 0)
        to_owner(send, near + jnp.where(wide, 1, 0), mate(z, 1))

    @pl.when(stencil)
    def _():
        landed(sides.at[0], recv_s.at[0])
        landed(sides.at[1], recv_s.at[1])
        lane = lax.broadcasted_iota(jnp.int32, (ROWS, 128), 1)
        for f in range(3):
            ext[f, 8 : 8 + ROWS, 0:CELLS] = fields[f][0]
            east_side, west_side = sides[1], sides[0]
            if f:
                east_side, west_side = pltpu.roll(east_side, 128 - 4 * f, 1), pltpu.roll(west_side, 4 * f, 1)
            ext[f, 8 : 8 + ROWS, CELLS : CELLS + 128] = jnp.where(lane < 64, east_side, west_side)

        @pl.when(lat > 2)
        def _():
            remote(ext.at[:, 8:16, :], ext.at[:, 104:112, :], send_r.at[0], recv_r.at[0], (lat - 1, lon))

        @pl.when(lat < 13)
        def _():
            remote(ext.at[:, 96:104, :], ext.at[:, 0:8, :], send_r.at[1], recv_r.at[1], (lat + 1, lon))

        @pl.when(lat == 2)
        def _():
            ext[:, 0:8, :] = jnp.zeros((3, 8, 512), F32)

        @pl.when(lat == 13)
        def _():
            ext[:, 104:112, :] = jnp.zeros((3, 8, 512), F32)

    def transform(g):
        size = HOLD * 3 * len(GROUPS[g])
        order = [(row, pos) for row in range(HOLD) for pos in range(len(GROUPS[g]))]
        grids = [
            jnp.concatenate(
                [recv[g][pl.ds(row * (size // HOLD) + 3 * pos + s, 32, stride=size), :] for s in range(3)], axis=0
            )
            for row, pos in order
        ]
        mixed = outer_step(first_ref[...], jnp.concatenate(grids, axis=1))
        cos, sin = grid_ref[0], grid_ref[1]
        twisted = []
        for n in range(len(order)):
            real, imag = mixed[:HALF, 128 * n : 128 * (n + 1)], mixed[HALF:, 128 * n : 128 * (n + 1)]
            twisted.append(jnp.concatenate([real * cos + imag * sin, imag * cos - real * sin], axis=1))
        spectrum = inner_step(fore_ref, jnp.concatenate(twisted, axis=0))
        return {
            key: (spectrum[HALF * n : HALF * (n + 1), :128], spectrum[HALF * n : HALF * (n + 1), 128:])
            for n, key in enumerate(order)
        }

    def restore(g, spectra):
        size = HOLD * 3 * len(BACK[g])
        order = list(spectra)
        cos, sin = grid_ref[0], grid_ref[1]
        back = inner_step(
            back_ref, jnp.concatenate([jnp.concatenate(spectra[key], axis=1) for key in order], axis=0)
        )
        spun = []
        for n in range(len(order)):
            real, imag = back[HALF * n : HALF * (n + 1), :128], back[HALF * n : HALF * (n + 1), 128:]
            spun.append(jnp.concatenate([real * cos - imag * sin, imag * cos + real * sin], axis=0))
        cells = outer_step(last_ref[...], jnp.concatenate(spun, axis=1))
        for n, (row, pos) in enumerate(order):
            for s in range(3):
                snd[g][pl.ds(row * (size // HOLD) + 3 * pos + s, 32, stride=size), :] = cells[
                    32 * s : 32 * (s + 1), 128 * n : 128 * (n + 1)
                ]

    def put(ref, index, pair):
        ref[(*index, slice(0, HALF))] = pair[0]
        ref[(*index, slice(HALF, 2 * HALF))] = pair[1]

    def get(ref, *index):
        return ref[(*index, slice(0, HALF))], ref[(*index, slice(HALF, 2 * HALF))]

    row0 = jnp.where(south, NLAT - HOLD - HOLD * chain, HOLD * chain)

    def polar(row):
        steps = jnp.where(south, NLAT - 1 - row, row)
        return jnp.abs(jnp.full((1, 128), steps, jnp.int32).astype(F32) + 0.5) * (math.pi / NLAT)

    def cosine(w):
        return jnp.sin(polar(row0 + w - 1))

    def prepare():
        speed = speed_ref[0]
        share_of_pole = jnp.where(south, SPIN, -SPIN).astype(F32)
        for w in range(WINGS):
            there = 1.0
            if w == 0:
                there = jnp.where(has_before, 1.0, 0.0).astype(F32)
            if w == WINGS - 1:
                there = jnp.where(has_after, 1.0, 0.0).astype(F32)
            angle = polar(row0 + w - 1)
            share = 1.0 / jnp.maximum(grid_ref[3], jnp.sin(angle))
            keep = share * (jnp.sin(angle) * there)
            slope = share * (COURANT * grid_ref[2])
            scale[w, 0] = slope
            scale[w, 1] = keep * (share_of_pole * jnp.cos(angle))
            scale[w, 2] = keep * (0.5 * NORTH)
            if 0 < w < WINGS - 1:
                scale[w, 3] = speed * slope
                scale[w, 4] = share * (speed * (0.5 * NORTH) * cosine(w - 1))
                scale[w, 5] = share * (speed * (0.5 * NORTH) * cosine(w + 1))

    def push_east(heights, old, new, w):
        mid, east, north = get(heights, w + 1), get(old, w, 0), get(old, w, 1)
        slope, swirl = scale[w, 0], scale[w, 1]
        put(new, (w, 0), (
            east[0] + slope * mid[1] + swirl * north[0],
            east[1] - slope * mid[0] + swirl * north[1],
        ))

    def push_north(heights, old, new, w):
        low, high = get(heights, w), get(heights, w + 2)
        east, north = get(old, w, 0), get(old, w, 1)
        swirl, climb = scale[w, 1], scale[w, 2]
        put(new, (w, 1), tuple(north[p] - climb * (high[p] - low[p]) - swirl * east[p] for p in range(2)))

    def pushed_height(heights, winds, w):
        mid, east = get(heights, w + 1), get(winds, w, 0)
        low, high = get(winds, w - 1, 1), get(winds, w + 1, 1)
        slope, below, above = scale[w, 3], scale[w, 4], scale[w, 5]
        return (
            mid[0] + slope * east[1] - (above * high[0] - below * low[0]),
            mid[1] - slope * east[0] - (above * high[1] - below * low[1]),
        )

    def trade(e, ref, wing):
        @pl.when(has_before)
        def _():
            remote(
                ref.at[pl.ds(wing, wing)], ref.at[pl.ds(wing + HOLD, wing)],
                send_x.at[e, 0], recv_x.at[e, 1], before_device,
            )

        @pl.when(has_after)
        def _():
            remote(ref.at[pl.ds(HOLD, wing)], ref.at[pl.ds(0, wing)], send_x.at[e, 1], recv_x.at[e, 0], after_device)

    def traded(e, ref, wing):
        pl.when(has_before)(lambda: landed(ref.at[pl.ds(0, wing)], recv_x.at[e, 0]))
        pl.when(has_after)(lambda: landed(ref.at[pl.ds(wing + HOLD, wing)], recv_x.at[e, 1]))

    def send_back(g):
        size = HOLD * 3 * len(BACK[g])
        start = owner_start(nth) * (size // HOLD)

        def one(how, to_z, to_core):
            how(
                snd[g].at[pl.ds((16 * to_core + to_z) * size, size)], home[g].at[pl.ds(start, size)],
                send_c.at[g], recv_c.at[g], mate(to_z, to_core),
            )

        def both(k, carry):
            to = chip(k)
            one(remote, to, 0)
            one(remote, to, 1)
            return carry

        lax.fori_loop(0, 15, both, 0)
        one(send, z, 0)
        one(send, z, 1)

    @pl.when(owner)
    def _():
        loaded(3, 4, 5, 6, 7)
        prepare()

        @pl.when(jnp.logical_not(has_before))
        def _():
            tall[0:2] = jnp.zeros((2, 2 * HALF, 128), F32)
            tall_new[0:2] = jnp.zeros((2, 2 * HALF, 128), F32)
            wind[0] = jnp.zeros((2, 2 * HALF, 128), F32)

        @pl.when(jnp.logical_not(has_after))
        def _():
            tall[2 + HOLD : 4 + HOLD] = jnp.zeros((2, 2 * HALF, 128), F32)
            tall_new[2 + HOLD : 4 + HOLD] = jnp.zeros((2, 2 * HALF, 128), F32)
            wind[1 + HOLD] = jnp.zeros((2, 2 * HALF, 128), F32)

        landed(recv[0], recv_b.at[0])
        for (row, _), pair in transform(0).items():
            put(tall, (2 + row,), pair)
        trade(0, tall, 2)
        landed(recv[1], recv_b.at[1])
        for (row, which), pair in transform(1).items():
            put(wind, (1 + row, which), pair)
        trade(1, wind, 1)
        traded(0, tall, 2)
        traded(1, wind, 1)
        for w in range(WINGS):
            push_east(tall, wind, wind_new, w)
            push_north(tall, wind, wind_new, w)
        for w in range(1, 1 + HOLD):
            put(tall_new, (1 + w,), pushed_height(tall, wind_new, w))
        trade(2, tall_new, 2)
        for w in range(1, 1 + HOLD):
            push_east(tall_new, wind_new, wind_last, w)
        restore(0, {(row, 0): get(wind_last, 1 + row, 0) for row in range(HOLD)})
        send_back(0)
        traded(2, tall_new, 2)
        for w in range(WINGS):
            push_north(tall_new, wind_new, wind_last, w)
        last = {(row, 0): get(wind_last, 1 + row, 1) for row in range(HOLD)}
        last.update({(row, 1): pushed_height(tall_new, wind_last, 1 + row) for row in range(HOLD)})
        restore(1, last)
        send_back(1)

    for g in range(2):
        per = 3 * len(BACK[g])

        def deliver(size, g=g, per=per):
            landed(home[g].at[pl.ds(0, size * per)], recv_c.at[g])
            send(
                home[g].at[pl.ds(0, size * per)], ret[g].at[pl.ds(part_start(my_part, size) * per, size * per)],
                send_d.at[g], recv_d.at[g, my_part], (my_lat, slab),
            )

        each_size(deliver)

    @pl.when(stencil)
    def _():
        @pl.when(lat > 2)
        def _():
            landed(ext.at[:, 0:8, :], recv_r.at[1])

        @pl.when(lat < 13)
        def _():
            landed(ext.at[:, 104:112, :], recv_r.at[0])

        row = lax.broadcasted_iota(jnp.int32, (ROWS + 16, 128), 0) + (ROWS * lat - 8)
        latitude = (row.astype(F32) + (0.5 - NLAT // 2)) * (math.pi / NLAT)
        wide_cos = jnp.concatenate([jnp.cos(latitude)] * 4, axis=1)
        spin = jnp.concatenate([SPIN * jnp.sin(latitude)] * 4, axis=1)
        inverse = 1.0 / wide_cos
        east_scale = (0.5 * COURANT) * inverse
        speed = speed_ref[0]

        def across(value):
            return pltpu.roll(value, 511, 1) - pltpu.roll(value, 1, 1)

        def along(value):
            return pltpu.roll(value, ROWS + 15, 0) - pltpu.roll(value, 1, 0)

        height, east, north = ext[0], ext[1], ext[2]
        for _step in range(2):
            east_inc = spin * north - east_scale * across(height)
            north_inc = (-0.5 * NORTH) * along(height) - spin * east
            east, north = east + east_inc, north + north_inc
            spread_out = east_scale * across(east) + (0.5 * NORTH) * inverse * along(north * wide_cos)
            height = height - speed * spread_out
        for out, value in zip(outs, (height, east, north)):
            out[0] = value[8 : 8 + ROWS, 0:CELLS]

    def back(f, s):
        g = 0 if f in BACK[0] else 1
        return ret[g][pl.ds(3 * BACK[g].index(f) + s, ROWS, stride=3 * len(BACK[g])), :]

    @pl.when(band < 2)
    def _():
        for g in range(2):
            per = 3 * len(BACK[g])
            for k in range(3):
                landed(ret[g].at[pl.ds(part_start(k, 32) * per, 32 * per)], recv_d.at[g, k])
            for f in BACK[g]:
                for s in range(3):
                    outs[f][0, :, 128 * s : 128 * (s + 1)] = back(f, s)

    @pl.when(band == 2)
    def _():
        row = lax.broadcasted_iota(jnp.int32, (ROWS, 128), 0)
        from_pole = jnp.where(south, ROWS - 1 - row, row) + 2 * ROWS
        for g in range(2):
            per = 3 * len(BACK[g])
            for k in range(2):
                landed(ret[g].at[pl.ds(part_start(k, 36) * per, 36 * per)], recv_d.at[g, k])
            for f in BACK[g]:
                for s in range(3):
                    lanes = slice(128 * s, 128 * (s + 1))
                    outs[f][0, :, lanes] = jnp.where(from_pole < FINAL, back(f, s), outs[f][0, :, lanes])

    for g in range(2):
        per = 3 * len(GROUPS[g])

        def left_parts(size, parts, g=g, per=per):
            for k in range(parts):
                other = jnp.logical_not(same(member(3 * band + k, z, lax.div(lon, 16))))
                pl.when(other)(lambda k=k: landed(src[g].at[pl.ds(0, size * per)], send_a.at[g, k]))

        pl.when(band < 2)(lambda f=left_parts: f(32, 3))
        pl.when(band == 2)(lambda f=left_parts: f(36, 2))
        for case, count in (
            (jnp.logical_and(jnp.logical_not(wide), owner), 15),
            (jnp.logical_and(jnp.logical_not(wide), jnp.logical_not(owner)), 16),
            (jnp.logical_and(wide, owner), 17),
            (jnp.logical_and(wide, jnp.logical_not(owner)), 18),
        ):
            pl.when(case)(
                lambda g=g, n=count * HOLD * per: landed(relay[g].at[pl.ds(0, n)], send_b.at[g])
            )
        ret_per = 3 * len(BACK[g])
        pl.when(owner)(lambda g=g, per=ret_per: landed(snd[g].at[pl.ds(0, 31 * HOLD * per)], send_c.at[g]))

        @pl.when(jnp.logical_not(same((my_lat, slab))))
        def _(g=g, per=ret_per):
            each_size(lambda size: landed(home[g].at[pl.ds(0, size * per)], send_d.at[g]))

    @pl.when(stencil)
    def _():
        for side in range(2):
            landed(packed.at[side], send_s.at[side])

        @pl.when(lat > 2)
        def _():
            landed(ext.at[:, 8:16, :], send_r.at[0])

        @pl.when(lat < 13)
        def _():
            landed(ext.at[:, 96:104, :], send_r.at[1])

    for e, (ref, wing) in enumerate(((tall, 2), (wind, 1), (tall_new, 2))):
        pl.when(has_before)(lambda e=e, ref=ref, wing=wing: landed(ref.at[pl.ds(0, wing)], send_x.at[e, 0]))
        pl.when(has_after)(lambda e=e, ref=ref, wing=wing: landed(ref.at[pl.ds(0, wing)], send_x.at[e, 1]))


def write(h_ref, u_ref, v_ref, h_out, u_out, v_out, sems):
    copies = [
        pltpu.make_async_copy(here, there, sems.at[n])
        for n, (here, there) in enumerate(((h_ref, h_out), (u_ref, u_out), (v_ref, v_out)))
    ]
    for copy in copies:
        copy.start()
    for copy in copies:
        copy.wait()


def body(height, east_wind, north_wind, wave_speed_sq):
    constants = [np.asarray(table, np.float32) for table in tables()]
    block = jax.ShapeDtypeStruct((1, ROWS, CELLS), F32)
    pairs = []
    for groups, rows in ((GROUPS, ROWS), (GROUPS, 36), (GROUPS, 32 * HOLD), (BACK, 32 * HOLD), (BACK, 36), (BACK, ROWS)):
        pairs += [pltpu.VMEM((rows * 3 * len(group), 128), F32) for group in groups]
    dma = pltpu.SemaphoreType.DMA
    vmem = pl.BlockSpec(memory_space=pltpu.VMEM)
    results = pl.pallas_call(
        kernel,
        out_shape=[pltpu.VMEM(block.shape, F32)] * 3,
        in_specs=[pl.BlockSpec(memory_space=pltpu.SMEM)] + [pl.BlockSpec(memory_space=pl.ANY)] * 8,
        out_specs=[vmem] * 3,
        scratch_shapes=[
            *[pltpu.VMEM((1, ROWS, CELLS), F32)] * 3,
            *[pltpu.VMEM(table.shape, table.dtype) for table in constants],
            *pairs,
            *[pltpu.VMEM((HOLD + 4, 2 * HALF, 128), F32)] * 2,
            *[pltpu.VMEM((WINGS, 2, 2 * HALF, 128), F32)] * 3,
            pltpu.VMEM((WINGS, 6, HALF, 128), F32),
            pltpu.VMEM((2, ROWS, 128), F32),
            pltpu.VMEM((2, ROWS, 128), F32),
            pltpu.VMEM((3, ROWS + 16, 512), F32),
            pltpu.SemaphoreType.REGULAR,
            dma((8,)), dma((2, 3)), dma((2,)), dma((2,)), dma((2,)), dma((2,)), dma((2,)), dma((2,)), dma((2, 3)),
            dma((3, 2)), dma((3, 2)), dma((2,)), dma((2,)), dma((2,)), dma((2,)),
        ],
        compiler_params=pltpu.CompilerParams(
            collective_id=0, has_side_effects=True, vmem_limit_bytes=60 * 1024 * 1024
        ),
        name="substeps",
    )(wave_speed_sq, height, east_wind, north_wind, *constants)
    return pl.pallas_call(
        write,
        out_shape=[block] * 3,
        in_specs=[vmem] * 3,
        out_specs=[pl.BlockSpec(memory_space=pl.ANY)] * 3,
        scratch_shapes=[dma((3,))],
        compiler_params=pltpu.CompilerParams(vmem_limit_bytes=16 * 1024 * 1024),
        name="write",
    )(*results)


def solution(mesh):
    block = P(None, "lat", "lon")
    return jax.shard_map(
        lambda *args: tuple(body(*args)),
        mesh=mesh, in_specs=(block, block, block, P()), out_specs=(block, block, block), check_vma=False,
    )
```

```python
import math

import jax
import jax.numpy as jnp
import ml_dtypes
import numpy as np
from jax import lax
from jax.experimental import pallas as pl
from jax.experimental.pallas import tpu as pltpu
from jax.sharding import PartitionSpec as P

NLON, NLAT = 12288, 1536
ROWS, CELLS = 96, 384
OUTER, INNER = 96, 128
HALF = 56
COURANT, SPIN = 0.45, 0.3
NORTH = COURANT * 2.0 * NLAT / NLON
FINAL = 260
HOLD = 2
OWNERS = 132
WINGS = HOLD + 2
MESH = pl.DeviceIdType.MESH
F32, BF16 = jnp.float32, jnp.bfloat16
GROUPS = ((0,), (1, 2))
BACK = ((1,), (2, 0))


def split(table):
    high = table.astype(ml_dtypes.bfloat16)
    low = (table - high.astype(np.float64)).astype(ml_dtypes.bfloat16)
    return high, low


def tables():
    a = np.array([3 * d + s for s in range(3) for d in range(32)])
    k1 = np.arange(HALF)
    live = (k1 <= OUTER // 2).astype(np.float64)
    angle = 2 * np.pi * ((k1[:, None] * a[None, :]) % OUTER) / OUTER
    first = np.concatenate([np.cos(angle) * live[:, None], -np.sin(angle) * live[:, None]], axis=0)
    weight = live * np.where((k1 == 0) | (k1 == OUTER // 2), 1.0, 2.0) / NLON
    last = np.concatenate([np.cos(angle) * weight[:, None], -np.sin(angle) * weight[:, None]], axis=0).T
    n = np.arange(INNER)
    turn = 2 * np.pi * (k1[:, None] * n[None, :]) / NLON
    inner = 2 * np.pi * ((n[:, None] * n[None, :]) % INNER) / INNER
    cos, sin = np.cos(inner), np.sin(inner)
    forward = np.block([[cos, -sin], [sin, cos]])
    backward = np.block([[cos, sin], [-sin, cos]])
    wave = k1[:, None] + OUTER * n[None, :]
    steep = np.sin(2 * np.pi * wave / NLON) * live[:, None]
    half_sine = np.where(live[:, None] > 0, 0.5 * np.abs(np.sin(np.pi * wave / NLON)), 1.0)
    first_high, first_low = split(first)
    last_high, last_low = split(last)
    forward_high, forward_low = split(forward)
    backward_high, backward_low = split(backward)
    grid = np.stack([np.cos(turn), np.sin(turn), steep, half_sine]).astype(np.float32)
    return (
        np.concatenate([first_high, first_low, first_high], axis=1),
        np.concatenate([last_high, last_low, last_high], axis=1),
        np.stack([forward_high, forward_low]),
        np.stack([backward_high, backward_low]),
        grid,
    )


def parts(value):
    high = value.astype(BF16)
    return high, (value - high.astype(F32)).astype(BF16)


def dot(left, right):
    return jnp.dot(left, right, preferred_element_type=F32)


def outer_step(table, value):
    high, low = parts(value)
    return dot(table.astype(BF16), jnp.concatenate([high, high, low], axis=0))


def inner_step(table, value):
    high, low = parts(value)
    table_high, table_low = table[0].astype(BF16), table[1].astype(BF16)
    return dot(high, table_high) + dot(low, table_high) + dot(high, table_low)


def kernel(
    speed_ref, h_hbm, u_hbm, v_hbm, first_hbm, last_hbm, fore_hbm, back_hbm, grid_hbm,
    h_out, u_out, v_out,
    h_ref, u_ref, v_ref, first_ref, last_ref, fore_ref, back_ref, grid_ref,
    src0, src1, relay0, relay1, recv0, recv1, snd0, snd1, home0, home1, ret0, ret1,
    tall, tall_new, wind, wind_new, wind_last, scale, packed, sides, ext,
    go, loads, send_a, recv_a, send_b, recv_b, send_c, recv_c, send_d, recv_d, send_x, recv_x, send_s, recv_s, send_r, recv_r,
):
    fields, outs = (h_ref, u_ref, v_ref), (h_out, u_out, v_out)
    operands = (h_hbm, u_hbm, v_hbm, first_hbm, last_hbm, fore_hbm, back_hbm, grid_hbm)
    held = (h_ref, u_ref, v_ref, first_ref, last_ref, fore_ref, back_ref, grid_ref)
    src, relay, recv = (src0, src1), (relay0, relay1), (recv0, recv1)
    snd, home, ret = (snd0, snd1), (home0, home1), (ret0, ret1)
    lat, lon = lax.axis_index("lat"), lax.axis_index("lon")
    south = lat >= 8
    band = jnp.where(south, 15 - lat, lat)
    core = lax.rem(band, 2)
    z = lax.rem(lon, 16)
    x = 2 * lax.div(lon, 16) + lax.rem(lax.div(band, 2), 2)
    line = jnp.where(band < 4, x, 7 - x)
    wide = line >= 6
    near = lax.rem(z + line, 16)
    slab = 16 * core + z
    extra = jnp.logical_and(wide, jnp.logical_and(core == 0, jnp.logical_or(near == 0, near == 15)))
    owner = jnp.logical_or(core == 1, extra)
    owners = jnp.where(wide, 18, 16)
    nth = jnp.where(wide, jnp.where(core == 1, near + 1, jnp.where(near == 0, 0, 17)), near)
    chain = 16 * line + 2 * jnp.where(line == 7, 1, 0) + nth
    source = band <= 2
    stencil = band >= 2
    my_band = jnp.where(wide, 2, lax.div(line, 3))
    my_lat = jnp.where(south, 15 - my_band, my_band)
    my_part = line - 3 * my_band

    def member(to_line, to_z, to_core):
        to_x = jnp.where(to_line < 4, to_line, 7 - to_line)
        to_band = 4 * lax.div(to_line, 4) + 2 * lax.rem(to_x, 2) + to_core
        return jnp.where(south, 15 - to_band, to_band), 16 * lax.div(to_x, 2) + to_z

    def mate(to_z, to_core):
        shift = to_core - core
        return jnp.where(south, lat - shift, lat + shift), lon - z + to_z

    def holder(n):
        to_line = jnp.where(n < 96, lax.div(n, 16), 6 + lax.div(jnp.maximum(n - 96, 0), 18))
        to_nth = n - 16 * to_line - 2 * jnp.where(to_line == 7, 1, 0)
        broad = to_line >= 6
        to_near = jnp.where(broad, jnp.clip(to_nth - 1, 0, 15), to_nth)
        to_core = jnp.where(jnp.logical_and(broad, jnp.logical_or(to_nth == 0, to_nth == 17)), 0, 1)
        return member(to_line, lax.rem(to_near + 16 - to_line, 16), to_core)

    def chip(k):
        away = 8 - lax.div(k + 1, 2)
        return lax.rem(z + 16 + jnp.where(lax.rem(k, 2) == 1, away, -away), 16)

    def same(target):
        return jnp.logical_and(target[0] == lat, target[1] == lon)

    def remote(here, there, send_sem, recv_sem, target):
        pltpu.make_async_remote_copy(
            src_ref=here, dst_ref=there, send_sem=send_sem, recv_sem=recv_sem, device_id=target, device_id_type=MESH
        ).start()

    def send(here, there, send_sem, recv_sem, target):
        own = same(target)

        @pl.when(own)
        def _():
            pltpu.make_async_copy(here, there, recv_sem).start()

        @pl.when(jnp.logical_not(own))
        def _():
            remote(here, there, send_sem, recv_sem, target)

    def landed(ref, sem):
        pltpu.make_async_copy(ref, ref, sem).wait()

    def part_start(k, size):
        return jnp.where(south, ROWS - size * (k + 1), size * k)

    def owner_start(i):
        return HOLD * jnp.where(south, owners - 1 - i, i)

    def each_size(act):
        pl.when(jnp.logical_not(wide))(lambda: act(32))
        pl.when(wide)(lambda: act(36))

    right = jnp.where(lon == 31, 0, lon + 1)
    left = jnp.where(lon == 0, 31, lon - 1)
    before = chain + jnp.where(south, 1, -1)
    after = chain + jnp.where(south, -1, 1)
    has_before = jnp.logical_and(owner, jnp.logical_and(before >= 0, before < OWNERS))
    has_after = jnp.logical_and(owner, jnp.logical_and(after >= 0, after < OWNERS))
    before_device, after_device = holder(jnp.clip(before, 0, OWNERS - 1)), holder(jnp.clip(after, 0, OWNERS - 1))

    barrier = pltpu.get_barrier_semaphore()

    def greet(target):
        pl.semaphore_signal(barrier, inc=1, device_id=target, device_id_type=MESH)

    def greet_other(target):
        pl.when(jnp.logical_not(same(target)))(lambda: greet(target))

    def helper(of_line, to_z):
        of_x = jnp.where(of_line < 4, of_line, 7 - of_line)
        return member(7 - of_x, to_z, lax.div(of_line, 4))

    helps = band >= 4
    helped = jnp.where(core == 1, 7 - x, x)

    def greet_helper(k, carry):
        greet(helper(line, lax.rem(z + k, 16)))
        return carry

    my_helper = helper(line, z)
    helped_from_afar = jnp.logical_not(same(my_helper))

    @pl.when(owner)
    def _():
        lax.fori_loop(1, 16, greet_helper, 0)

    pl.when(jnp.logical_and(owner, helped_from_afar))(lambda: greet(my_helper))
    pl.when(helped_from_afar)(lambda: greet(my_helper))
    greeted = jnp.where(helps, jnp.where(helped >= 6, 18, 16) + 2 - 2 * core, 0)
    pl.when(jnp.logical_not(same((my_lat, slab))))(lambda: greet((my_lat, slab)))
    for k in range(3):
        target = member(jnp.minimum(3 * band + k, 7), z, lax.div(lon, 16))
        meant = jnp.logical_or(band < 2, jnp.logical_and(band == 2, k < 2))
        meant = jnp.logical_and(meant, jnp.logical_not(same(target)))
        greeted += meant.astype(jnp.int32)
    for meant, target in (
        (has_before, before_device), (has_after, after_device), (stencil, (lat, left)), (stencil, (lat, right)),
        (jnp.logical_and(stencil, lat > 2), (lat - 1, lon)), (jnp.logical_and(stencil, lat < 13), (lat + 1, lon)),
    ):
        pl.when(meant)(lambda target=target: greet(target))
        greeted += meant.astype(jnp.int32)

    def load(*indices):
        for index in indices:
            pltpu.make_async_copy(operands[index], held[index], loads.at[index]).start()

    def loaded(*indices):
        for index in indices:
            pltpu.make_async_copy(operands[index], held[index], loads.at[index]).wait()

    load(0, 1, 2)
    pl.when(owner)(lambda: load(3, 4, 5, 6, 7))

    def gather(g):
        per = 3 * len(GROUPS[g])
        for pos, f in enumerate(GROUPS[g]):
            for s in range(3):
                src[g][pl.ds(3 * pos + s, ROWS, stride=per), :] = fields[f][0, :, 128 * s : 128 * (s + 1)]

    def send_rows(g):
        per = 3 * len(GROUPS[g])

        def one(k, size):
            send(
                src[g].at[pl.ds(part_start(k, size) * per, size * per)], relay[g].at[pl.ds(0, size * per)],
                send_a.at[g, k], recv_a.at[g], member(3 * band + k, z, lax.div(lon, 16)),
            )

        @pl.when(band < 2)
        def _():
            for k in range(3):
                one(k, 32)

        @pl.when(band == 2)
        def _():
            for k in range(2):
                one(k, 36)

    loaded(0)
    pl.when(source)(lambda: gather(0))
    pl.semaphore_wait(barrier, greeted)

    @pl.when(helps)
    def _():
        for to_core in range(2):
            target = member(helped, z, to_core)
            pl.when(jnp.logical_not(same(target)))(
                lambda target=target: pl.semaphore_signal(go, inc=1, device_id=target, device_id_type=MESH)
            )

    pl.when(source)(lambda: send_rows(0))
    loaded(1, 2)

    @pl.when(source)
    def _():
        gather(1)
        send_rows(1)

    @pl.when(stencil)
    def _():
        lane = lax.broadcasted_iota(jnp.int32, (ROWS, 128), 1)
        high = [ref[0, :, 256:384] for ref in fields]
        low = [ref[0, :, 0:128] for ref in fields]
        packed[0] = jnp.where(
            lane >= 124, high[0], jnp.where(lane >= 120, pltpu.roll(high[1], 124, 1), pltpu.roll(high[2], 120, 1))
        )
        packed[1] = jnp.where(lane < 4, low[0], jnp.where(lane < 8, pltpu.roll(low[1], 4, 1), pltpu.roll(low[2], 8, 1)))
        remote(packed.at[0], sides.at[0], send_s.at[0], recv_s.at[0], (lat, right))
        remote(packed.at[1], sides.at[1], send_s.at[1], recv_s.at[1], (lat, left))

    pl.when(helped_from_afar)(lambda: pl.semaphore_wait(go, 1))
    for g in range(2):
        per = 3 * len(GROUPS[g])
        each_size(lambda size, g=g, per=per: landed(relay[g].at[pl.ds(0, size * per)], recv_a.at[g]))

        def to_owner(how, i, target, g=g, per=per):
            how(
                relay[g].at[pl.ds(owner_start(i) * per, HOLD * per)],
                recv[g].at[pl.ds(slab * (HOLD * per), HOLD * per)],
                send_b.at[g], recv_b.at[g], target,
            )

        def spread(k, carry, to_owner=to_owner):
            to = chip(k)
            to_owner(remote, lax.rem(to + line, 16) + jnp.where(wide, 1, 0), mate(to, 1))
            return carry

        @pl.when(wide)
        def _(to_owner=to_owner):
            for i in (0, 17):
                to_owner(send, i, mate(lax.rem(min(i, 15) + 16 - line, 16), 0))

        lax.fori_loop(0, 15, spread, 0)
        to_owner(send, near + jnp.where(wide, 1, 0), mate(z, 1))

    @pl.when(stencil)
    def _():
        landed(sides.at[0], recv_s.at[0])
        landed(sides.at[1], recv_s.at[1])
        lane = lax.broadcasted_iota(jnp.int32, (ROWS, 128), 1)
        for f in range(3):
            ext[f, 8 : 8 + ROWS, 0:CELLS] = fields[f][0]
            east_side, west_side = sides[1], sides[0]
            if f:
                east_side, west_side = pltpu.roll(east_side, 128 - 4 * f, 1), pltpu.roll(west_side, 4 * f, 1)
            ext[f, 8 : 8 + ROWS, CELLS : CELLS + 128] = jnp.where(lane < 64, east_side, west_side)

        @pl.when(lat > 2)
        def _():
            remote(ext.at[:, 8:16, :], ext.at[:, 104:112, :], send_r.at[0], recv_r.at[0], (lat - 1, lon))

        @pl.when(lat < 13)
        def _():
            remote(ext.at[:, 96:104, :], ext.at[:, 0:8, :], send_r.at[1], recv_r.at[1], (lat + 1, lon))

        @pl.when(lat == 2)
        def _():
            ext[:, 0:8, :] = jnp.zeros((3, 8, 512), F32)

        @pl.when(lat == 13)
        def _():
            ext[:, 104:112, :] = jnp.zeros((3, 8, 512), F32)

    def transform(g):
        size = HOLD * 3 * len(GROUPS[g])
        order = [(row, pos) for row in range(HOLD) for pos in range(len(GROUPS[g]))]
        grids = [
            jnp.concatenate(
                [recv[g][pl.ds(row * (size // HOLD) + 3 * pos + s, 32, stride=size), :] for s in range(3)], axis=0
            )
            for row, pos in order
        ]
        mixed = outer_step(first_ref[...], jnp.concatenate(grids, axis=1))
        cos, sin = grid_ref[0], grid_ref[1]
        twisted = []
        for n in range(len(order)):
            real, imag = mixed[:HALF, 128 * n : 128 * (n + 1)], mixed[HALF:, 128 * n : 128 * (n + 1)]
            twisted.append(jnp.concatenate([real * cos + imag * sin, imag * cos - real * sin], axis=1))
        spectrum = inner_step(fore_ref, jnp.concatenate(twisted, axis=0))
        return {
            key: (spectrum[HALF * n : HALF * (n + 1), :128], spectrum[HALF * n : HALF * (n + 1), 128:])
            for n, key in enumerate(order)
        }

    def restore(g, spectra):
        size = HOLD * 3 * len(BACK[g])
        order = list(spectra)
        cos, sin = grid_ref[0], grid_ref[1]
        back = inner_step(
            back_ref, jnp.concatenate([jnp.concatenate(spectra[key], axis=1) for key in order], axis=0)
        )
        spun = []
        for n in range(len(order)):
            real, imag = back[HALF * n : HALF * (n + 1), :128], back[HALF * n : HALF * (n + 1), 128:]
            spun.append(jnp.concatenate([real * cos - imag * sin, imag * cos + real * sin], axis=0))
        cells = outer_step(last_ref[...], jnp.concatenate(spun, axis=1))
        for n, (row, pos) in enumerate(order):
            for s in range(3):
                snd[g][pl.ds(row * (size // HOLD) + 3 * pos + s, 32, stride=size), :] = cells[
                    32 * s : 32 * (s + 1), 128 * n : 128 * (n + 1)
                ]

    def put(ref, index, pair):
        ref[(*index, slice(0, HALF))] = pair[0]
        ref[(*index, slice(HALF, 2 * HALF))] = pair[1]

    def get(ref, *index):
        return ref[(*index, slice(0, HALF))], ref[(*index, slice(HALF, 2 * HALF))]

    row0 = jnp.where(south, NLAT - HOLD - HOLD * chain, HOLD * chain)

    def polar(row):
        steps = jnp.where(south, NLAT - 1 - row, row)
        return jnp.abs(jnp.full((1, 128), steps, jnp.int32).astype(F32) + 0.5) * (math.pi / NLAT)

    def cosine(w):
        return jnp.sin(polar(row0 + w - 1))

    def prepare():
        speed = speed_ref[0]
        share_of_pole = jnp.where(south, SPIN, -SPIN).astype(F32)
        for w in range(WINGS):
            there = 1.0
            if w == 0:
                there = jnp.where(has_before, 1.0, 0.0).astype(F32)
            if w == WINGS - 1:
                there = jnp.where(has_after, 1.0, 0.0).astype(F32)
            angle = polar(row0 + w - 1)
            share = 1.0 / jnp.maximum(grid_ref[3], jnp.sin(angle))
            keep = share * (jnp.sin(angle) * there)
            slope = share * (COURANT * grid_ref[2])
            scale[w, 0] = slope
            scale[w, 1] = keep * (share_of_pole * jnp.cos(angle))
            scale[w, 2] = keep * (0.5 * NORTH)
            if 0 < w < WINGS - 1:
                scale[w, 3] = speed * slope
                scale[w, 4] = share * (speed * (0.5 * NORTH) * cosine(w - 1))
                scale[w, 5] = share * (speed * (0.5 * NORTH) * cosine(w + 1))

    def push_east(heights, old, new, w):
        mid, east, north = get(heights, w + 1), get(old, w, 0), get(old, w, 1)
        slope, swirl = scale[w, 0], scale[w, 1]
        put(new, (w, 0), (
            east[0] + slope * mid[1] + swirl * north[0],
            east[1] - slope * mid[0] + swirl * north[1],
        ))

    def push_north(heights, old, new, w):
        low, high = get(heights, w), get(heights, w + 2)
        east, north = get(old, w, 0), get(old, w, 1)
        swirl, climb = scale[w, 1], scale[w, 2]
        put(new, (w, 1), tuple(north[p] - climb * (high[p] - low[p]) - swirl * east[p] for p in range(2)))

    def pushed_height(heights, winds, w):
        mid, east = get(heights, w + 1), get(winds, w, 0)
        low, high = get(winds, w - 1, 1), get(winds, w + 1, 1)
        slope, below, above = scale[w, 3], scale[w, 4], scale[w, 5]
        return (
            mid[0] + slope * east[1] - (above * high[0] - below * low[0]),
            mid[1] - slope * east[0] - (above * high[1] - below * low[1]),
        )

    def trade(e, ref, wing):
        @pl.when(has_before)
        def _():
            remote(
                ref.at[pl.ds(wing, wing)], ref.at[pl.ds(wing + HOLD, wing)],
                send_x.at[e, 0], recv_x.at[e, 1], before_device,
            )

        @pl.when(has_after)
        def _():
            remote(ref.at[pl.ds(HOLD, wing)], ref.at[pl.ds(0, wing)], send_x.at[e, 1], recv_x.at[e, 0], after_device)

    def traded(e, ref, wing):
        pl.when(has_before)(lambda: landed(ref.at[pl.ds(0, wing)], recv_x.at[e, 0]))
        pl.when(has_after)(lambda: landed(ref.at[pl.ds(wing + HOLD, wing)], recv_x.at[e, 1]))

    def send_back(g):
        size = HOLD * 3 * len(BACK[g])
        start = owner_start(nth) * (size // HOLD)

        def one(how, to_z, to_core):
            how(
                snd[g].at[pl.ds((16 * to_core + to_z) * size, size)], home[g].at[pl.ds(start, size)],
                send_c.at[g], recv_c.at[g], mate(to_z, to_core),
            )

        def both(k, carry):
            to = jnp.where(k < 5, lax.rem(z + k, 5), 5 + lax.rem(z + k, 11))
            one(send, to, 0)
            one(send, to, 1)
            return carry

        lax.fori_loop(0, 16, both, 0)

    @pl.when(owner)
    def _():
        loaded(3, 4, 5, 6, 7)
        prepare()

        @pl.when(jnp.logical_not(has_before))
        def _():
            tall[0:2] = jnp.zeros((2, 2 * HALF, 128), F32)
            tall_new[0:2] = jnp.zeros((2, 2 * HALF, 128), F32)
            wind[0] = jnp.zeros((2, 2 * HALF, 128), F32)

        @pl.when(jnp.logical_not(has_after))
        def _():
            tall[2 + HOLD : 4 + HOLD] = jnp.zeros((2, 2 * HALF, 128), F32)
            tall_new[2 + HOLD : 4 + HOLD] = jnp.zeros((2, 2 * HALF, 128), F32)
            wind[1 + HOLD] = jnp.zeros((2, 2 * HALF, 128), F32)

        landed(recv[0], recv_b.at[0])
        for (row, _), pair in transform(0).items():
            put(tall, (2 + row,), pair)
        trade(0, tall, 2)
        landed(recv[1], recv_b.at[1])
        for (row, which), pair in transform(1).items():
            put(wind, (1 + row, which), pair)
        trade(1, wind, 1)
        traded(0, tall, 2)
        traded(1, wind, 1)
        for w in range(WINGS):
            push_east(tall, wind, wind_new, w)
            push_north(tall, wind, wind_new, w)
        for w in range(1, 1 + HOLD):
            put(tall_new, (1 + w,), pushed_height(tall, wind_new, w))
        trade(2, tall_new, 2)
        for w in range(1, 1 + HOLD):
            push_east(tall_new, wind_new, wind_last, w)
        restore(0, {(row, 0): get(wind_last, 1 + row, 0) for row in range(HOLD)})
        send_back(0)
        traded(2, tall_new, 2)
        for w in range(WINGS):
            push_north(tall_new, wind_new, wind_last, w)
        last = {(row, 0): get(wind_last, 1 + row, 1) for row in range(HOLD)}
        last.update({(row, 1): pushed_height(tall_new, wind_last, 1 + row) for row in range(HOLD)})
        restore(1, last)
        send_back(1)

    @pl.when(stencil)
    def _():
        @pl.when(lat > 2)
        def _():
            landed(ext.at[:, 0:8, :], recv_r.at[1])

        @pl.when(lat < 13)
        def _():
            landed(ext.at[:, 104:112, :], recv_r.at[0])

        row = lax.broadcasted_iota(jnp.int32, (ROWS + 16, 128), 0) + (ROWS * lat - 8)
        latitude = (row.astype(F32) + (0.5 - NLAT // 2)) * (math.pi / NLAT)
        wide_cos = jnp.concatenate([jnp.cos(latitude)] * 4, axis=1)
        spin = jnp.concatenate([SPIN * jnp.sin(latitude)] * 4, axis=1)
        inverse = 1.0 / wide_cos
        east_scale = (0.5 * COURANT) * inverse
        speed = speed_ref[0]

        def across(value):
            return pltpu.roll(value, 511, 1) - pltpu.roll(value, 1, 1)

        def along(value):
            return pltpu.roll(value, ROWS + 15, 0) - pltpu.roll(value, 1, 0)

        height, east, north = ext[0], ext[1], ext[2]
        for _step in range(2):
            east_inc = spin * north - east_scale * across(height)
            north_inc = (-0.5 * NORTH) * along(height) - spin * east
            east, north = east + east_inc, north + north_inc
            spread_out = east_scale * across(east) + (0.5 * NORTH) * inverse * along(north * wide_cos)
            height = height - speed * spread_out
        for out, value in zip(outs, (height, east, north)):
            out[0] = value[8 : 8 + ROWS, 0:CELLS]

    for g in range(2):
        per = 3 * len(BACK[g])

        def deliver(size, g=g, per=per):
            landed(home[g].at[pl.ds(0, size * per)], recv_c.at[g])
            send(
                home[g].at[pl.ds(0, size * per)], ret[g].at[pl.ds(part_start(my_part, size) * per, size * per)],
                send_d.at[g], recv_d.at[g, my_part], (my_lat, slab),
            )

        each_size(deliver)

    def back(f, s):
        g = 0 if f in BACK[0] else 1
        return ret[g][pl.ds(3 * BACK[g].index(f) + s, ROWS, stride=3 * len(BACK[g])), :]

    @pl.when(band < 2)
    def _():
        for g in range(2):
            per = 3 * len(BACK[g])
            for k in range(3):
                landed(ret[g].at[pl.ds(part_start(k, 32) * per, 32 * per)], recv_d.at[g, k])
            for f in BACK[g]:
                for s in range(3):
                    outs[f][0, :, 128 * s : 128 * (s + 1)] = back(f, s)

    @pl.when(band == 2)
    def _():
        row = lax.broadcasted_iota(jnp.int32, (ROWS, 128), 0)
        from_pole = jnp.where(south, ROWS - 1 - row, row) + 2 * ROWS
        for g in range(2):
            per = 3 * len(BACK[g])
            for k in range(2):
                landed(ret[g].at[pl.ds(part_start(k, 36) * per, 36 * per)], recv_d.at[g, k])
            for f in BACK[g]:
                for s in range(3):
                    lanes = slice(128 * s, 128 * (s + 1))
                    outs[f][0, :, lanes] = jnp.where(from_pole < FINAL, back(f, s), outs[f][0, :, lanes])

    for g in range(2):
        per = 3 * len(GROUPS[g])

        def left_parts(size, parts, g=g, per=per):
            for k in range(parts):
                other = jnp.logical_not(same(member(3 * band + k, z, lax.div(lon, 16))))
                pl.when(other)(lambda k=k: landed(src[g].at[pl.ds(0, size * per)], send_a.at[g, k]))

        pl.when(band < 2)(lambda f=left_parts: f(32, 3))
        pl.when(band == 2)(lambda f=left_parts: f(36, 2))
        for case, count in (
            (jnp.logical_and(jnp.logical_not(wide), owner), 15),
            (jnp.logical_and(jnp.logical_not(wide), jnp.logical_not(owner)), 16),
            (jnp.logical_and(wide, owner), 17),
            (jnp.logical_and(wide, jnp.logical_not(owner)), 18),
        ):
            pl.when(case)(
                lambda g=g, n=count * HOLD * per: landed(relay[g].at[pl.ds(0, n)], send_b.at[g])
            )
        ret_per = 3 * len(BACK[g])
        pl.when(owner)(lambda g=g, per=ret_per: landed(snd[g].at[pl.ds(0, 31 * HOLD * per)], send_c.at[g]))

        @pl.when(jnp.logical_not(same((my_lat, slab))))
        def _(g=g, per=ret_per):
            each_size(lambda size: landed(home[g].at[pl.ds(0, size * per)], send_d.at[g]))

    @pl.when(stencil)
    def _():
        for side in range(2):
            landed(packed.at[side], send_s.at[side])

        @pl.when(lat > 2)
        def _():
            landed(ext.at[:, 8:16, :], send_r.at[0])

        @pl.when(lat < 13)
        def _():
            landed(ext.at[:, 96:104, :], send_r.at[1])

    for e, (ref, wing) in enumerate(((tall, 2), (wind, 1), (tall_new, 2))):
        pl.when(has_before)(lambda e=e, ref=ref, wing=wing: landed(ref.at[pl.ds(0, wing)], send_x.at[e, 0]))
        pl.when(has_after)(lambda e=e, ref=ref, wing=wing: landed(ref.at[pl.ds(0, wing)], send_x.at[e, 1]))


def write(h_ref, u_ref, v_ref, h_out, u_out, v_out, sems):
    copies = [
        pltpu.make_async_copy(here, there, sems.at[n])
        for n, (here, there) in enumerate(((h_ref, h_out), (u_ref, u_out), (v_ref, v_out)))
    ]
    for copy in copies:
        copy.start()
    for copy in copies:
        copy.wait()


def body(height, east_wind, north_wind, wave_speed_sq):
    constants = [np.asarray(table, np.float32) for table in tables()]
    block = jax.ShapeDtypeStruct((1, ROWS, CELLS), F32)
    pairs = []
    for groups, rows in ((GROUPS, ROWS), (GROUPS, 36), (GROUPS, 32 * HOLD), (BACK, 32 * HOLD), (BACK, 36), (BACK, ROWS)):
        pairs += [pltpu.VMEM((rows * 3 * len(group), 128), F32) for group in groups]
    dma = pltpu.SemaphoreType.DMA
    vmem = pl.BlockSpec(memory_space=pltpu.VMEM)
    results = pl.pallas_call(
        kernel,
        out_shape=[pltpu.VMEM(block.shape, F32)] * 3,
        in_specs=[pl.BlockSpec(memory_space=pltpu.SMEM)] + [pl.BlockSpec(memory_space=pl.ANY)] * 8,
        out_specs=[vmem] * 3,
        scratch_shapes=[
            *[pltpu.VMEM((1, ROWS, CELLS), F32)] * 3,
            *[pltpu.VMEM(table.shape, table.dtype) for table in constants],
            *pairs,
            *[pltpu.VMEM((HOLD + 4, 2 * HALF, 128), F32)] * 2,
            *[pltpu.VMEM((WINGS, 2, 2 * HALF, 128), F32)] * 3,
            pltpu.VMEM((WINGS, 6, HALF, 128), F32),
            pltpu.VMEM((2, ROWS, 128), F32),
            pltpu.VMEM((2, ROWS, 128), F32),
            pltpu.VMEM((3, ROWS + 16, 512), F32),
            pltpu.SemaphoreType.REGULAR,
            dma((8,)), dma((2, 3)), dma((2,)), dma((2,)), dma((2,)), dma((2,)), dma((2,)), dma((2,)), dma((2, 3)),
            dma((3, 2)), dma((3, 2)), dma((2,)), dma((2,)), dma((2,)), dma((2,)),
        ],
        compiler_params=pltpu.CompilerParams(
            collective_id=0, has_side_effects=True, vmem_limit_bytes=60 * 1024 * 1024
        ),
        name="substeps",
    )(wave_speed_sq, height, east_wind, north_wind, *constants)
    return pl.pallas_call(
        write,
        out_shape=[block] * 3,
        in_specs=[vmem] * 3,
        out_specs=[pl.BlockSpec(memory_space=pl.ANY)] * 3,
        scratch_shapes=[dma((3,))],
        compiler_params=pltpu.CompilerParams(vmem_limit_bytes=16 * 1024 * 1024),
        name="write",
    )(*results)


def solution(mesh):
    block = P(None, "lat", "lon")
    return jax.shard_map(
        lambda *args: tuple(body(*args)),
        mesh=mesh, in_specs=(block, block, block, P()), out_specs=(block, block, block), check_vma=False,
    )
```

```python
import math

import jax
import jax.numpy as jnp
import ml_dtypes
import numpy as np
from jax import lax
from jax.experimental import pallas as pl
from jax.experimental.pallas import tpu as pltpu
from jax.sharding import PartitionSpec as P

NLON, NLAT = 12288, 1536
ROWS, CELLS = 96, 384
OUTER, INNER = 96, 128
HALF = 56
COURANT, SPIN = 0.45, 0.3
NORTH = COURANT * 2.0 * NLAT / NLON
FINAL = 260
HOLD = 2
OWNERS = 132
WINGS = HOLD + 2
MESH = pl.DeviceIdType.MESH
F32, BF16 = jnp.float32, jnp.bfloat16
GROUPS = ((0,), (1, 2))
BACK = ((1,), (2, 0))


def split(table):
    high = table.astype(ml_dtypes.bfloat16)
    low = (table - high.astype(np.float64)).astype(ml_dtypes.bfloat16)
    return high, low


def tables():
    a = np.array([3 * d + s for s in range(3) for d in range(32)])
    k1 = np.arange(HALF)
    live = (k1 <= OUTER // 2).astype(np.float64)
    angle = 2 * np.pi * ((k1[:, None] * a[None, :]) % OUTER) / OUTER
    first = np.concatenate([np.cos(angle) * live[:, None], -np.sin(angle) * live[:, None]], axis=0)
    weight = live * np.where((k1 == 0) | (k1 == OUTER // 2), 1.0, 2.0) / NLON
    last = np.concatenate([np.cos(angle) * weight[:, None], -np.sin(angle) * weight[:, None]], axis=0).T
    n = np.arange(INNER)
    turn = 2 * np.pi * (k1[:, None] * n[None, :]) / NLON
    inner = 2 * np.pi * ((n[:, None] * n[None, :]) % INNER) / INNER
    cos, sin = np.cos(inner), np.sin(inner)
    forward = np.block([[cos, -sin], [sin, cos]])
    backward = np.block([[cos, sin], [-sin, cos]])
    wave = k1[:, None] + OUTER * n[None, :]
    steep = np.sin(2 * np.pi * wave / NLON) * live[:, None]
    half_sine = np.where(live[:, None] > 0, 0.5 * np.abs(np.sin(np.pi * wave / NLON)), 1.0)
    first_high, first_low = split(first)
    last_high, last_low = split(last)
    forward_high, forward_low = split(forward)
    backward_high, backward_low = split(backward)
    grid = np.stack([np.cos(turn), np.sin(turn), steep, half_sine]).astype(np.float32)
    return (
        np.concatenate([first_high, first_low, first_high], axis=1),
        np.concatenate([last_high, last_low, last_high], axis=1),
        np.stack([forward_high, forward_low]),
        np.stack([backward_high, backward_low]),
        grid,
    )


def parts(value):
    high = value.astype(BF16)
    return high, (value - high.astype(F32)).astype(BF16)


def dot(left, right):
    return jnp.dot(left, right, preferred_element_type=F32)


def outer_step(table, value):
    high, low = parts(value)
    return dot(table.astype(BF16), jnp.concatenate([high, high, low], axis=0))


def inner_step(table, value):
    high, low = parts(value)
    table_high, table_low = table[0].astype(BF16), table[1].astype(BF16)
    return dot(high, table_high) + dot(low, table_high) + dot(high, table_low)


def kernel(
    speed_ref, h_hbm, u_hbm, v_hbm, first_hbm, last_hbm, fore_hbm, back_hbm, grid_hbm,
    h_out, u_out, v_out,
    h_ref, u_ref, v_ref, first_ref, last_ref, fore_ref, back_ref, grid_ref,
    src0, src1, relay0, relay1, recv0, recv1, snd0, snd1, home0, home1, ret0, ret1,
    tall, tall_new, wind, wind_new, wind_last, scale, packed, sides, ext,
    go, loads, send_a, recv_a, send_b, recv_b, send_c, recv_c, send_d, recv_d, send_x, recv_x, send_s, recv_s, send_r, recv_r,
):
    fields, outs = (h_ref, u_ref, v_ref), (h_out, u_out, v_out)
    operands = (h_hbm, u_hbm, v_hbm, first_hbm, last_hbm, fore_hbm, back_hbm, grid_hbm)
    held = (h_ref, u_ref, v_ref, first_ref, last_ref, fore_ref, back_ref, grid_ref)
    src, relay, recv = (src0, src1), (relay0, relay1), (recv0, recv1)
    snd, home, ret = (snd0, snd1), (home0, home1), (ret0, ret1)
    lat, lon = lax.axis_index("lat"), lax.axis_index("lon")
    south = lat >= 8
    band = jnp.where(south, 15 - lat, lat)
    core = lax.rem(band, 2)
    z = lax.rem(lon, 16)
    x = 2 * lax.div(lon, 16) + lax.rem(lax.div(band, 2), 2)

    def back_row(n):
        return jnp.where(n == 5, 1, jnp.where(n == 6, 2, jnp.where(n == 1, 5, jnp.where(n == 2, 6, 7 - n))))

    line = jnp.where(band < 4, x, back_row(x))
    wide = line >= 6
    near = lax.rem(z + line, 16)
    slab = 16 * core + z
    extra = jnp.logical_and(wide, jnp.logical_and(core == 0, jnp.logical_or(near == 0, near == 15)))
    owner = jnp.logical_or(core == 1, extra)
    owners = jnp.where(wide, 18, 16)
    nth = jnp.where(wide, jnp.where(core == 1, near + 1, jnp.where(near == 0, 0, 17)), near)
    chain = 16 * line + 2 * jnp.where(line == 7, 1, 0) + nth
    source = band <= 2
    stencil = band >= 2
    my_band = jnp.where(wide, 2, lax.div(line, 3))
    my_lat = jnp.where(south, 15 - my_band, my_band)
    my_part = line - 3 * my_band

    def member(to_line, to_z, to_core):
        to_x = jnp.where(to_line < 4, to_line, back_row(to_line))
        to_band = 4 * lax.div(to_line, 4) + 2 * lax.rem(to_x, 2) + to_core
        return jnp.where(south, 15 - to_band, to_band), 16 * lax.div(to_x, 2) + to_z

    def mate(to_z, to_core):
        shift = to_core - core
        return jnp.where(south, lat - shift, lat + shift), lon - z + to_z

    def holder(n):
        to_line = jnp.where(n < 96, lax.div(n, 16), 6 + lax.div(jnp.maximum(n - 96, 0), 18))
        to_nth = n - 16 * to_line - 2 * jnp.where(to_line == 7, 1, 0)
        broad = to_line >= 6
        to_near = jnp.where(broad, jnp.clip(to_nth - 1, 0, 15), to_nth)
        to_core = jnp.where(jnp.logical_and(broad, jnp.logical_or(to_nth == 0, to_nth == 17)), 0, 1)
        return member(to_line, lax.rem(to_near + 16 - to_line, 16), to_core)

    def chip(k):
        away = 8 - lax.div(k + 1, 2)
        return lax.rem(z + 16 + jnp.where(lax.rem(k, 2) == 1, away, -away), 16)

    def same(target):
        return jnp.logical_and(target[0] == lat, target[1] == lon)

    def remote(here, there, send_sem, recv_sem, target):
        pltpu.make_async_remote_copy(
            src_ref=here, dst_ref=there, send_sem=send_sem, recv_sem=recv_sem, device_id=target, device_id_type=MESH
        ).start()

    def send(here, there, send_sem, recv_sem, target):
        own = same(target)

        @pl.when(own)
        def _():
            pltpu.make_async_copy(here, there, recv_sem).start()

        @pl.when(jnp.logical_not(own))
        def _():
            remote(here, there, send_sem, recv_sem, target)

    def landed(ref, sem):
        pltpu.make_async_copy(ref, ref, sem).wait()

    def part_start(k, size):
        return jnp.where(south, ROWS - size * (k + 1), size * k)

    def owner_start(i):
        return HOLD * jnp.where(south, owners - 1 - i, i)

    def each_size(act):
        pl.when(jnp.logical_not(wide))(lambda: act(32))
        pl.when(wide)(lambda: act(36))

    right = jnp.where(lon == 31, 0, lon + 1)
    left = jnp.where(lon == 0, 31, lon - 1)
    before = chain + jnp.where(south, 1, -1)
    after = chain + jnp.where(south, -1, 1)
    has_before = jnp.logical_and(owner, jnp.logical_and(before >= 0, before < OWNERS))
    has_after = jnp.logical_and(owner, jnp.logical_and(after >= 0, after < OWNERS))
    before_device, after_device = holder(jnp.clip(before, 0, OWNERS - 1)), holder(jnp.clip(after, 0, OWNERS - 1))

    barrier = pltpu.get_barrier_semaphore()

    def greet(target):
        pl.semaphore_signal(barrier, inc=1, device_id=target, device_id_type=MESH)

    def greet_other(target):
        pl.when(jnp.logical_not(same(target)))(lambda: greet(target))

    pl.when(jnp.logical_not(same((my_lat, slab))))(lambda: greet((my_lat, slab)))

    def load(*indices):
        for index in indices:
            pltpu.make_async_copy(operands[index], held[index], loads.at[index]).start()

    def loaded(*indices):
        for index in indices:
            pltpu.make_async_copy(operands[index], held[index], loads.at[index]).wait()

    load(0, 1, 2)
    pl.when(owner)(lambda: load(3, 4, 5, 6, 7))

    def helper(of_line, to_z):
        of_x = jnp.where(of_line < 4, of_line, back_row(of_line))
        return member(back_row(of_x), to_z, lax.div(of_line, 4))

    helps = band >= 4
    helped = jnp.where(core == 1, back_row(x), x)

    def greet_helper(k, carry):
        greet(helper(line, chip(k)))
        return carry

    my_helper = helper(line, z)
    helped_from_afar = jnp.logical_not(same(my_helper))

    greeted = jnp.where(helps, jnp.where(helped >= 6, 18, 16) + 2 - 2 * core, 0)
    for k in range(3):
        target = member(jnp.minimum(3 * band + k, 7), z, lax.div(lon, 16))
        meant = jnp.logical_or(band < 2, jnp.logical_and(band == 2, k < 2))
        meant = jnp.logical_and(meant, jnp.logical_not(same(target)))
        greeted += meant.astype(jnp.int32)
    for meant, target in (
        (has_before, before_device), (has_after, after_device), (stencil, (lat, left)), (stencil, (lat, right)),
        (jnp.logical_and(stencil, lat > 2), (lat - 1, lon)), (jnp.logical_and(stencil, lat < 13), (lat + 1, lon)),
    ):
        pl.when(meant)(lambda target=target: greet(target))
        greeted += meant.astype(jnp.int32)

    @pl.when(owner)
    def _():
        lax.fori_loop(0, 15, greet_helper, 0)

    pl.when(jnp.logical_and(owner, helped_from_afar))(lambda: greet(my_helper))
    pl.when(helped_from_afar)(lambda: greet(my_helper))

    def gather(g):
        per = 3 * len(GROUPS[g])
        for pos, f in enumerate(GROUPS[g]):
            for s in range(3):
                src[g][pl.ds(3 * pos + s, ROWS, stride=per), :] = fields[f][0, :, 128 * s : 128 * (s + 1)]

    def send_rows(g):
        per = 3 * len(GROUPS[g])

        def one(k, size):
            send(
                src[g].at[pl.ds(part_start(k, size) * per, size * per)], relay[g].at[pl.ds(0, size * per)],
                send_a.at[g, k], recv_a.at[g], member(3 * band + k, z, lax.div(lon, 16)),
            )

        @pl.when(band < 2)
        def _():
            for k in range(3):
                one(k, 32)

        @pl.when(band == 2)
        def _():
            for k in range(2):
                one(k, 36)

    loaded(0)
    pl.when(source)(lambda: gather(0))
    pl.semaphore_wait(barrier, greeted)

    @pl.when(helps)
    def _():
        for to_core in range(2):
            target = member(helped, z, to_core)
            pl.when(jnp.logical_not(same(target)))(
                lambda target=target: pl.semaphore_signal(go, inc=1, device_id=target, device_id_type=MESH)
            )

    pl.when(source)(lambda: send_rows(0))
    loaded(1, 2)

    @pl.when(source)
    def _():
        gather(1)
        send_rows(1)

    @pl.when(stencil)
    def _():
        lane = lax.broadcasted_iota(jnp.int32, (ROWS, 128), 1)
        high = [ref[0, :, 256:384] for ref in fields]
        low = [ref[0, :, 0:128] for ref in fields]
        packed[0] = jnp.where(
            lane >= 124, high[0], jnp.where(lane >= 120, pltpu.roll(high[1], 124, 1), pltpu.roll(high[2], 120, 1))
        )
        packed[1] = jnp.where(lane < 4, low[0], jnp.where(lane < 8, pltpu.roll(low[1], 4, 1), pltpu.roll(low[2], 8, 1)))
        remote(packed.at[0], sides.at[0], send_s.at[0], recv_s.at[0], (lat, right))
        remote(packed.at[1], sides.at[1], send_s.at[1], recv_s.at[1], (lat, left))

    pl.when(helped_from_afar)(lambda: pl.semaphore_wait(go, 1))
    for g in range(2):
        per = 3 * len(GROUPS[g])
        each_size(lambda size, g=g, per=per: landed(relay[g].at[pl.ds(0, size * per)], recv_a.at[g]))

        def to_owner(how, i, target, g=g, per=per):
            how(
                relay[g].at[pl.ds(owner_start(i) * per, HOLD * per)],
                recv[g].at[pl.ds(slab * (HOLD * per), HOLD * per)],
                send_b.at[g], recv_b.at[g], target,
            )

        def spread(k, carry, to_owner=to_owner):
            to = chip(k)
            to_owner(remote, lax.rem(to + line, 16) + jnp.where(wide, 1, 0), mate(to, 1))
            return carry

        @pl.when(wide)
        def _(to_owner=to_owner):
            for i in (0, 17):
                to_owner(send, i, mate(lax.rem(min(i, 15) + 16 - line, 16), 0))

        lax.fori_loop(0, 15, spread, 0)
        to_owner(send, near + jnp.where(wide, 1, 0), mate(z, 1))

    @pl.when(stencil)
    def _():
        landed(sides.at[0], recv_s.at[0])
        landed(sides.at[1], recv_s.at[1])
        lane = lax.broadcasted_iota(jnp.int32, (ROWS, 128), 1)
        for f in range(3):
            ext[f, 8 : 8 + ROWS, 0:CELLS] = fields[f][0]
            east_side, west_side = sides[1], sides[0]
            if f:
                east_side, west_side = pltpu.roll(east_side, 128 - 4 * f, 1), pltpu.roll(west_side, 4 * f, 1)
            ext[f, 8 : 8 + ROWS, CELLS : CELLS + 128] = jnp.where(lane < 64, east_side, west_side)

        @pl.when(lat > 2)
        def _():
            remote(ext.at[:, 8:16, :], ext.at[:, 104:112, :], send_r.at[0], recv_r.at[0], (lat - 1, lon))

        @pl.when(lat < 13)
        def _():
            remote(ext.at[:, 96:104, :], ext.at[:, 0:8, :], send_r.at[1], recv_r.at[1], (lat + 1, lon))

        @pl.when(lat == 2)
        def _():
            ext[:, 0:8, :] = jnp.zeros((3, 8, 512), F32)

        @pl.when(lat == 13)
        def _():
            ext[:, 104:112, :] = jnp.zeros((3, 8, 512), F32)

    def transform(g):
        size = HOLD * 3 * len(GROUPS[g])
        order = [(row, pos) for row in range(HOLD) for pos in range(len(GROUPS[g]))]
        grids = [
            jnp.concatenate(
                [recv[g][pl.ds(row * (size // HOLD) + 3 * pos + s, 32, stride=size), :] for s in range(3)], axis=0
            )
            for row, pos in order
        ]
        mixed = outer_step(first_ref[...], jnp.concatenate(grids, axis=1))
        cos, sin = grid_ref[0], grid_ref[1]
        twisted = []
        for n in range(len(order)):
            real, imag = mixed[:HALF, 128 * n : 128 * (n + 1)], mixed[HALF:, 128 * n : 128 * (n + 1)]
            twisted.append(jnp.concatenate([real * cos + imag * sin, imag * cos - real * sin], axis=1))
        spectrum = inner_step(fore_ref, jnp.concatenate(twisted, axis=0))
        return {
            key: (spectrum[HALF * n : HALF * (n + 1), :128], spectrum[HALF * n : HALF * (n + 1), 128:])
            for n, key in enumerate(order)
        }

    def restore(g, spectra):
        size = HOLD * 3 * len(BACK[g])
        order = list(spectra)
        cos, sin = grid_ref[0], grid_ref[1]
        back = inner_step(
            back_ref, jnp.concatenate([jnp.concatenate(spectra[key], axis=1) for key in order], axis=0)
        )
        spun = []
        for n in range(len(order)):
            real, imag = back[HALF * n : HALF * (n + 1), :128], back[HALF * n : HALF * (n + 1), 128:]
            spun.append(jnp.concatenate([real * cos - imag * sin, imag * cos + real * sin], axis=0))
        cells = outer_step(last_ref[...], jnp.concatenate(spun, axis=1))
        for n, (row, pos) in enumerate(order):
            for s in range(3):
                snd[g][pl.ds(row * (size // HOLD) + 3 * pos + s, 32, stride=size), :] = cells[
                    32 * s : 32 * (s + 1), 128 * n : 128 * (n + 1)
                ]

    def put(ref, index, pair):
        ref[(*index, slice(0, HALF))] = pair[0]
        ref[(*index, slice(HALF, 2 * HALF))] = pair[1]

    def get(ref, *index):
        return ref[(*index, slice(0, HALF))], ref[(*index, slice(HALF, 2 * HALF))]

    row0 = jnp.where(south, NLAT - HOLD - HOLD * chain, HOLD * chain)

    def polar(row):
        steps = jnp.where(south, NLAT - 1 - row, row)
        return jnp.abs(jnp.full((1, 128), steps, jnp.int32).astype(F32) + 0.5) * (math.pi / NLAT)

    def cosine(w):
        return jnp.sin(polar(row0 + w - 1))

    def prepare():
        speed = speed_ref[0]
        share_of_pole = jnp.where(south, SPIN, -SPIN).astype(F32)
        for w in range(WINGS):
            there = 1.0
            if w == 0:
                there = jnp.where(has_before, 1.0, 0.0).astype(F32)
            if w == WINGS - 1:
                there = jnp.where(has_after, 1.0, 0.0).astype(F32)
            angle = polar(row0 + w - 1)
            share = 1.0 / jnp.maximum(grid_ref[3], jnp.sin(angle))
            keep = share * (jnp.sin(angle) * there)
            slope = share * (COURANT * grid_ref[2])
            scale[w, 0] = slope
            scale[w, 1] = keep * (share_of_pole * jnp.cos(angle))
            scale[w, 2] = keep * (0.5 * NORTH)
            if 0 < w < WINGS - 1:
                scale[w, 3] = speed * slope
                scale[w, 4] = share * (speed * (0.5 * NORTH) * cosine(w - 1))
                scale[w, 5] = share * (speed * (0.5 * NORTH) * cosine(w + 1))

    def push_east(heights, old, new, w):
        mid, east, north = get(heights, w + 1), get(old, w, 0), get(old, w, 1)
        slope, swirl = scale[w, 0], scale[w, 1]
        put(new, (w, 0), (
            east[0] + slope * mid[1] + swirl * north[0],
            east[1] - slope * mid[0] + swirl * north[1],
        ))

    def push_north(heights, old, new, w):
        low, high = get(heights, w), get(heights, w + 2)
        east, north = get(old, w, 0), get(old, w, 1)
        swirl, climb = scale[w, 1], scale[w, 2]
        put(new, (w, 1), tuple(north[p] - climb * (high[p] - low[p]) - swirl * east[p] for p in range(2)))

    def pushed_height(heights, winds, w):
        mid, east = get(heights, w + 1), get(winds, w, 0)
        low, high = get(winds, w - 1, 1), get(winds, w + 1, 1)
        slope, below, above = scale[w, 3], scale[w, 4], scale[w, 5]
        return (
            mid[0] + slope * east[1] - (above * high[0] - below * low[0]),
            mid[1] - slope * east[0] - (above * high[1] - below * low[1]),
        )

    def trade(e, ref, wing):
        @pl.when(has_before)
        def _():
            remote(
                ref.at[pl.ds(wing, wing)], ref.at[pl.ds(wing + HOLD, wing)],
                send_x.at[e, 0], recv_x.at[e, 1], before_device,
            )

        @pl.when(has_after)
        def _():
            remote(ref.at[pl.ds(HOLD, wing)], ref.at[pl.ds(0, wing)], send_x.at[e, 1], recv_x.at[e, 0], after_device)

    def traded(e, ref, wing):
        pl.when(has_before)(lambda: landed(ref.at[pl.ds(0, wing)], recv_x.at[e, 0]))
        pl.when(has_after)(lambda: landed(ref.at[pl.ds(wing + HOLD, wing)], recv_x.at[e, 1]))

    def send_back(g):
        size = HOLD * 3 * len(BACK[g])
        start = owner_start(nth) * (size // HOLD)

        def one(how, to_z, to_core):
            how(
                snd[g].at[pl.ds((16 * to_core + to_z) * size, size)], home[g].at[pl.ds(start, size)],
                send_c.at[g], recv_c.at[g], mate(to_z, to_core),
            )

        def both(k, carry):
            to = jnp.where(k < 5, lax.rem(z + k, 5), 5 + lax.rem(z + k, 11))
            one(send, to, 0)
            one(send, to, 1)
            return carry

        lax.fori_loop(0, 16, both, 0)

    @pl.when(owner)
    def _():
        loaded(3, 4, 5, 6, 7)
        prepare()

        @pl.when(jnp.logical_not(has_before))
        def _():
            tall[0:2] = jnp.zeros((2, 2 * HALF, 128), F32)
            tall_new[0:2] = jnp.zeros((2, 2 * HALF, 128), F32)
            wind[0] = jnp.zeros((2, 2 * HALF, 128), F32)

        @pl.when(jnp.logical_not(has_after))
        def _():
            tall[2 + HOLD : 4 + HOLD] = jnp.zeros((2, 2 * HALF, 128), F32)
            tall_new[2 + HOLD : 4 + HOLD] = jnp.zeros((2, 2 * HALF, 128), F32)
            wind[1 + HOLD] = jnp.zeros((2, 2 * HALF, 128), F32)

        landed(recv[0], recv_b.at[0])
        for (row, _), pair in transform(0).items():
            put(tall, (2 + row,), pair)
        trade(0, tall, 2)
        landed(recv[1], recv_b.at[1])
        for (row, which), pair in transform(1).items():
            put(wind, (1 + row, which), pair)
        trade(1, wind, 1)
        traded(0, tall, 2)
        traded(1, wind, 1)
        for w in range(WINGS):
            push_east(tall, wind, wind_new, w)
            push_north(tall, wind, wind_new, w)
        for w in range(1, 1 + HOLD):
            put(tall_new, (1 + w,), pushed_height(tall, wind_new, w))
        trade(2, tall_new, 2)
        for w in range(1, 1 + HOLD):
            push_east(tall_new, wind_new, wind_last, w)
        restore(0, {(row, 0): get(wind_last, 1 + row, 0) for row in range(HOLD)})
        send_back(0)
        traded(2, tall_new, 2)
        for w in range(WINGS):
            push_north(tall_new, wind_new, wind_last, w)
        last = {(row, 0): get(wind_last, 1 + row, 1) for row in range(HOLD)}
        last.update({(row, 1): pushed_height(tall_new, wind_last, 1 + row) for row in range(HOLD)})
        restore(1, last)
        send_back(1)

    @pl.when(stencil)
    def _():
        @pl.when(lat > 2)
        def _():
            landed(ext.at[:, 0:8, :], recv_r.at[1])

        @pl.when(lat < 13)
        def _():
            landed(ext.at[:, 104:112, :], recv_r.at[0])

        row = lax.broadcasted_iota(jnp.int32, (ROWS + 16, 128), 0) + (ROWS * lat - 8)
        latitude = (row.astype(F32) + (0.5 - NLAT // 2)) * (math.pi / NLAT)
        wide_cos = jnp.concatenate([jnp.cos(latitude)] * 4, axis=1)
        spin = jnp.concatenate([SPIN * jnp.sin(latitude)] * 4, axis=1)
        inverse = 1.0 / wide_cos
        east_scale = (0.5 * COURANT) * inverse
        speed = speed_ref[0]

        def across(value):
            return pltpu.roll(value, 511, 1) - pltpu.roll(value, 1, 1)

        def along(value):
            return pltpu.roll(value, ROWS + 15, 0) - pltpu.roll(value, 1, 0)

        height, east, north = ext[0], ext[1], ext[2]
        for _step in range(2):
            east_inc = spin * north - east_scale * across(height)
            north_inc = (-0.5 * NORTH) * along(height) - spin * east
            east, north = east + east_inc, north + north_inc
            spread_out = east_scale * across(east) + (0.5 * NORTH) * inverse * along(north * wide_cos)
            height = height - speed * spread_out
        for out, value in zip(outs, (height, east, north)):
            out[0] = value[8 : 8 + ROWS, 0:CELLS]

    for g in range(2):
        per = 3 * len(BACK[g])

        def deliver(size, g=g, per=per):
            landed(home[g].at[pl.ds(0, size * per)], recv_c.at[g])
            send(
                home[g].at[pl.ds(0, size * per)], ret[g].at[pl.ds(part_start(my_part, size) * per, size * per)],
                send_d.at[g], recv_d.at[g, my_part], (my_lat, slab),
            )

        each_size(deliver)

    def back(f, s):
        g = 0 if f in BACK[0] else 1
        return ret[g][pl.ds(3 * BACK[g].index(f) + s, ROWS, stride=3 * len(BACK[g])), :]

    @pl.when(band < 2)
    def _():
        for g in range(2):
            per = 3 * len(BACK[g])
            for k in range(3):
                landed(ret[g].at[pl.ds(part_start(k, 32) * per, 32 * per)], recv_d.at[g, k])
            for f in BACK[g]:
                for s in range(3):
                    outs[f][0, :, 128 * s : 128 * (s + 1)] = back(f, s)

    @pl.when(band == 2)
    def _():
        row = lax.broadcasted_iota(jnp.int32, (ROWS, 128), 0)
        from_pole = jnp.where(south, ROWS - 1 - row, row) + 2 * ROWS
        for g in range(2):
            per = 3 * len(BACK[g])
            for k in range(2):
                landed(ret[g].at[pl.ds(part_start(k, 36) * per, 36 * per)], recv_d.at[g, k])
            for f in BACK[g]:
                for s in range(3):
                    lanes = slice(128 * s, 128 * (s + 1))
                    outs[f][0, :, lanes] = jnp.where(from_pole < FINAL, back(f, s), outs[f][0, :, lanes])

    for g in range(2):
        per = 3 * len(GROUPS[g])

        def left_parts(size, parts, g=g, per=per):
            for k in range(parts):
                other = jnp.logical_not(same(member(3 * band + k, z, lax.div(lon, 16))))
                pl.when(other)(lambda k=k: landed(src[g].at[pl.ds(0, size * per)], send_a.at[g, k]))

        pl.when(band < 2)(lambda f=left_parts: f(32, 3))
        pl.when(band == 2)(lambda f=left_parts: f(36, 2))
        for case, count in (
            (jnp.logical_and(jnp.logical_not(wide), owner), 15),
            (jnp.logical_and(jnp.logical_not(wide), jnp.logical_not(owner)), 16),
            (jnp.logical_and(wide, owner), 17),
            (jnp.logical_and(wide, jnp.logical_not(owner)), 18),
        ):
            pl.when(case)(
                lambda g=g, n=count * HOLD * per: landed(relay[g].at[pl.ds(0, n)], send_b.at[g])
            )
        ret_per = 3 * len(BACK[g])
        pl.when(owner)(lambda g=g, per=ret_per: landed(snd[g].at[pl.ds(0, 31 * HOLD * per)], send_c.at[g]))

        @pl.when(jnp.logical_not(same((my_lat, slab))))
        def _(g=g, per=ret_per):
            each_size(lambda size: landed(home[g].at[pl.ds(0, size * per)], send_d.at[g]))

    @pl.when(stencil)
    def _():
        for side in range(2):
            landed(packed.at[side], send_s.at[side])

        @pl.when(lat > 2)
        def _():
            landed(ext.at[:, 8:16, :], send_r.at[0])

        @pl.when(lat < 13)
        def _():
            landed(ext.at[:, 96:104, :], send_r.at[1])

    for e, (ref, wing) in enumerate(((tall, 2), (wind, 1), (tall_new, 2))):
        pl.when(has_before)(lambda e=e, ref=ref, wing=wing: landed(ref.at[pl.ds(0, wing)], send_x.at[e, 0]))
        pl.when(has_after)(lambda e=e, ref=ref, wing=wing: landed(ref.at[pl.ds(0, wing)], send_x.at[e, 1]))


def write(h_ref, u_ref, v_ref, h_out, u_out, v_out, sems):
    copies = [
        pltpu.make_async_copy(here, there, sems.at[n])
        for n, (here, there) in enumerate(((h_ref, h_out), (u_ref, u_out), (v_ref, v_out)))
    ]
    for copy in copies:
        copy.start()
    for copy in copies:
        copy.wait()


def body(height, east_wind, north_wind, wave_speed_sq):
    constants = [np.asarray(table, np.float32) for table in tables()]
    block = jax.ShapeDtypeStruct((1, ROWS, CELLS), F32)
    pairs = []
    for groups, rows in ((GROUPS, ROWS), (GROUPS, 36), (GROUPS, 32 * HOLD), (BACK, 32 * HOLD), (BACK, 36), (BACK, ROWS)):
        pairs += [pltpu.VMEM((rows * 3 * len(group), 128), F32) for group in groups]
    dma = pltpu.SemaphoreType.DMA
    vmem = pl.BlockSpec(memory_space=pltpu.VMEM)
    results = pl.pallas_call(
        kernel,
        out_shape=[pltpu.VMEM(block.shape, F32)] * 3,
        in_specs=[pl.BlockSpec(memory_space=pltpu.SMEM)] + [pl.BlockSpec(memory_space=pl.ANY)] * 8,
        out_specs=[vmem] * 3,
        scratch_shapes=[
            *[pltpu.VMEM((1, ROWS, CELLS), F32)] * 3,
            *[pltpu.VMEM(table.shape, table.dtype) for table in constants],
            *pairs,
            *[pltpu.VMEM((HOLD + 4, 2 * HALF, 128), F32)] * 2,
            *[pltpu.VMEM((WINGS, 2, 2 * HALF, 128), F32)] * 3,
            pltpu.VMEM((WINGS, 6, HALF, 128), F32),
            pltpu.VMEM((2, ROWS, 128), F32),
            pltpu.VMEM((2, ROWS, 128), F32),
            pltpu.VMEM((3, ROWS + 16, 512), F32),
            pltpu.SemaphoreType.REGULAR,
            dma((8,)), dma((2, 3)), dma((2,)), dma((2,)), dma((2,)), dma((2,)), dma((2,)), dma((2,)), dma((2, 3)),
            dma((3, 2)), dma((3, 2)), dma((2,)), dma((2,)), dma((2,)), dma((2,)),
        ],
        compiler_params=pltpu.CompilerParams(
            collective_id=0, has_side_effects=True, vmem_limit_bytes=60 * 1024 * 1024
        ),
        name="substeps",
    )(wave_speed_sq, height, east_wind, north_wind, *constants)
    return pl.pallas_call(
        write,
        out_shape=[block] * 3,
        in_specs=[vmem] * 3,
        out_specs=[pl.BlockSpec(memory_space=pl.ANY)] * 3,
        scratch_shapes=[dma((3,))],
        compiler_params=pltpu.CompilerParams(vmem_limit_bytes=16 * 1024 * 1024),
        name="write",
    )(*results)


def solution(mesh):
    block = P(None, "lat", "lon")
    return jax.shard_map(
        lambda *args: tuple(body(*args)),
        mesh=mesh, in_specs=(block, block, block, P()), out_specs=(block, block, block), check_vma=False,
    )
```

```python
import math

import jax
import jax.numpy as jnp
import ml_dtypes
import numpy as np
from jax import lax
from jax.experimental import pallas as pl
from jax.experimental.pallas import tpu as pltpu
from jax.sharding import PartitionSpec as P

NLON, NLAT = 12288, 1536
ROWS, CELLS = 96, 384
OUTER, INNER = 96, 128
HALF = 56
COURANT, SPIN = 0.45, 0.3
NORTH = COURANT * 2.0 * NLAT / NLON
FINAL = 260
HOLD = 2
OWNERS = 132
WINGS = HOLD + 2
MESH = pl.DeviceIdType.MESH
F32, BF16 = jnp.float32, jnp.bfloat16
GROUPS = ((0,), (1, 2))
BACK_ROW = (3, 2, 1, 0)
BACK = ((1,), (2, 0))


def split(table):
    high = table.astype(ml_dtypes.bfloat16)
    low = (table - high.astype(np.float64)).astype(ml_dtypes.bfloat16)
    return high, low


def tables():
    a = np.array([3 * d + s for s in range(3) for d in range(32)])
    k1 = np.arange(HALF)
    live = (k1 <= OUTER // 2).astype(np.float64)
    angle = 2 * np.pi * ((k1[:, None] * a[None, :]) % OUTER) / OUTER
    first = np.concatenate([np.cos(angle) * live[:, None], -np.sin(angle) * live[:, None]], axis=0)
    weight = live * np.where((k1 == 0) | (k1 == OUTER // 2), 1.0, 2.0) / NLON
    last = np.concatenate([np.cos(angle) * weight[:, None], -np.sin(angle) * weight[:, None]], axis=0).T
    n = np.arange(INNER)
    turn = 2 * np.pi * (k1[:, None] * n[None, :]) / NLON
    inner = 2 * np.pi * ((n[:, None] * n[None, :]) % INNER) / INNER
    cos, sin = np.cos(inner), np.sin(inner)
    forward = np.block([[cos, -sin], [sin, cos]])
    backward = np.block([[cos, sin], [-sin, cos]])
    wave = k1[:, None] + OUTER * n[None, :]
    steep = np.sin(2 * np.pi * wave / NLON) * live[:, None]
    half_sine = np.where(live[:, None] > 0, 0.5 * np.abs(np.sin(np.pi * wave / NLON)), 1.0)
    first_high, first_low = split(first)
    last_high, last_low = split(last)
    forward_high, forward_low = split(forward)
    backward_high, backward_low = split(backward)
    grid = np.stack([np.cos(turn), np.sin(turn), steep, half_sine]).astype(np.float32)
    return (
        np.concatenate([first_high, first_low, first_high], axis=1),
        np.concatenate([last_high, last_low, last_high], axis=1),
        np.stack([forward_high, forward_low]),
        np.stack([backward_high, backward_low]),
        grid,
    )


def parts(value):
    high = value.astype(BF16)
    return high, (value - high.astype(F32)).astype(BF16)


def dot(left, right):
    return jnp.dot(left, right, preferred_element_type=F32)


def outer_step(table, value):
    high, low = parts(value)
    return dot(table.astype(BF16), jnp.concatenate([high, high, low], axis=0))


def inner_step(table, value):
    high, low = parts(value)
    table_high, table_low = table[0].astype(BF16), table[1].astype(BF16)
    return dot(high, table_high) + dot(low, table_high) + dot(high, table_low)


def kernel(
    speed_ref, h_hbm, u_hbm, v_hbm, first_hbm, last_hbm, fore_hbm, back_hbm, grid_hbm,
    h_out, u_out, v_out,
    h_ref, u_ref, v_ref, first_ref, last_ref, fore_ref, back_ref, grid_ref,
    src0, src1, relay0, relay1, recv0, recv1, snd0, snd1, home0, home1, ret0, ret1,
    tall, tall_new, wind, wind_new, wind_last, scale, packed, sides, ext,
    go, loads, send_a, recv_a, send_b, recv_b, send_c, recv_c, send_d, recv_d, send_x, recv_x, send_s, recv_s, send_r, recv_r,
):
    fields, outs = (h_ref, u_ref, v_ref), (h_out, u_out, v_out)
    operands = (h_hbm, u_hbm, v_hbm, first_hbm, last_hbm, fore_hbm, back_hbm, grid_hbm)
    held = (h_ref, u_ref, v_ref, first_ref, last_ref, fore_ref, back_ref, grid_ref)
    src, relay, recv = (src0, src1), (relay0, relay1), (recv0, recv1)
    snd, home, ret = (snd0, snd1), (home0, home1), (ret0, ret1)
    lat, lon = lax.axis_index("lat"), lax.axis_index("lon")
    south = lat >= 8
    band = jnp.where(south, 15 - lat, lat)
    core = lax.rem(band, 2)
    z = lax.rem(lon, 16)
    x = 2 * lax.div(lon, 16) + lax.rem(lax.div(band, 2), 2)

    def back_x(n):
        return jnp.where(n == 4, BACK_ROW[0], jnp.where(n == 5, BACK_ROW[1], jnp.where(n == 6, BACK_ROW[2], BACK_ROW[3])))

    def back_line(n):
        return jnp.where(n == BACK_ROW[0], 4, jnp.where(n == BACK_ROW[1], 5, jnp.where(n == BACK_ROW[2], 6, 7)))

    line = jnp.where(band < 4, x, back_line(x))
    wide = line >= 6
    near = lax.rem(z + line, 16)
    slab = 16 * core + z
    extra = jnp.logical_and(wide, jnp.logical_and(core == 0, jnp.logical_or(near == 0, near == 8)))
    owner = jnp.logical_or(core == 1, extra)
    owners = jnp.where(wide, 18, 16)

    def nth_at(to_near):
        return to_near + jnp.where(wide, 1 + jnp.where(to_near > 8, 1, 0), 0)

    nth = jnp.where(core == 1, nth_at(near), jnp.where(near == 0, 0, 10))
    chain = 16 * line + 2 * jnp.where(line == 7, 1, 0) + nth
    source = band <= 2
    stencil = band >= 2
    my_band = jnp.where(wide, 2, lax.div(line, 3))
    my_lat = jnp.where(south, 15 - my_band, my_band)
    my_part = line - 3 * my_band

    def member(to_line, to_z, to_core):
        to_x = jnp.where(to_line < 4, to_line, back_x(to_line))
        to_band = 4 * lax.div(to_line, 4) + 2 * lax.rem(to_x, 2) + to_core
        return jnp.where(south, 15 - to_band, to_band), 16 * lax.div(to_x, 2) + to_z

    def mate(to_z, to_core):
        shift = to_core - core
        return jnp.where(south, lat - shift, lat + shift), lon - z + to_z

    def holder(n):
        to_line = jnp.where(n < 96, lax.div(n, 16), 6 + lax.div(jnp.maximum(n - 96, 0), 18))
        to_nth = n - 16 * to_line - 2 * jnp.where(to_line == 7, 1, 0)
        broad = to_line >= 6
        to_near = jnp.where(broad, jnp.maximum(to_nth - jnp.where(to_nth > 9, 2, 1), 0), to_nth)
        to_core = jnp.where(jnp.logical_and(broad, jnp.logical_or(to_nth == 0, to_nth == 10)), 0, 1)
        return member(to_line, lax.rem(to_near + 16 - to_line, 16), to_core)

    def chip(k):
        away = 8 - lax.div(k + 1, 2)
        return lax.rem(z + 16 + jnp.where(lax.rem(k, 2) == 1, away, -away), 16)

    def same(target):
        return jnp.logical_and(target[0] == lat, target[1] == lon)

    def remote(here, there, send_sem, recv_sem, target):
        pltpu.make_async_remote_copy(
            src_ref=here, dst_ref=there, send_sem=send_sem, recv_sem=recv_sem, device_id=target, device_id_type=MESH
        ).start()

    def send(here, there, send_sem, recv_sem, target):
        own = same(target)

        @pl.when(own)
        def _():
            pltpu.make_async_copy(here, there, recv_sem).start()

        @pl.when(jnp.logical_not(own))
        def _():
            remote(here, there, send_sem, recv_sem, target)

    def landed(ref, sem):
        pltpu.make_async_copy(ref, ref, sem).wait()

    def part_start(k, size):
        return jnp.where(south, ROWS - size * (k + 1), size * k)

    def owner_start(i):
        return HOLD * jnp.where(south, owners - 1 - i, i)

    def each_size(act):
        pl.when(jnp.logical_not(wide))(lambda: act(32))
        pl.when(wide)(lambda: act(36))

    right = jnp.where(lon == 31, 0, lon + 1)
    left = jnp.where(lon == 0, 31, lon - 1)
    before = chain + jnp.where(south, 1, -1)
    after = chain + jnp.where(south, -1, 1)
    has_before = jnp.logical_and(owner, jnp.logical_and(before >= 0, before < OWNERS))
    has_after = jnp.logical_and(owner, jnp.logical_and(after >= 0, after < OWNERS))
    before_device, after_device = holder(jnp.clip(before, 0, OWNERS - 1)), holder(jnp.clip(after, 0, OWNERS - 1))

    barrier = pltpu.get_barrier_semaphore()

    def greet(target):
        pl.semaphore_signal(barrier, inc=1, device_id=target, device_id_type=MESH)

    def greet_other(target):
        pl.when(jnp.logical_not(same(target)))(lambda: greet(target))

    pl.when(jnp.logical_not(same((my_lat, slab))))(lambda: greet((my_lat, slab)))

    def load(*indices):
        for index in indices:
            pltpu.make_async_copy(operands[index], held[index], loads.at[index]).start()

    def loaded(*indices):
        for index in indices:
            pltpu.make_async_copy(operands[index], held[index], loads.at[index]).wait()

    load(0, 1, 2)
    pl.when(owner)(lambda: load(3, 4, 5, 6, 7))

    def helper(of_line, to_z):
        of_x = jnp.where(of_line < 4, of_line, back_x(of_line))
        return member(back_line(of_x), to_z, lax.div(of_line, 4))

    helps = band >= 4
    helped = jnp.where(core == 1, back_line(x), x)

    def greet_helper(k, carry):
        greet(helper(line, chip(k)))
        return carry

    my_helper = helper(line, z)
    helped_from_afar = jnp.logical_not(same(my_helper))

    greeted = jnp.where(helps, jnp.where(helped >= 6, 18, 16) + 2 - 2 * core, 0)
    for k in range(3):
        target = member(jnp.minimum(3 * band + k, 7), z, lax.div(lon, 16))
        meant = jnp.logical_or(band < 2, jnp.logical_and(band == 2, k < 2))
        meant = jnp.logical_and(meant, jnp.logical_not(same(target)))
        greeted += meant.astype(jnp.int32)
    for meant, target in (
        (has_before, before_device), (has_after, after_device), (stencil, (lat, left)), (stencil, (lat, right)),
        (jnp.logical_and(stencil, lat > 2), (lat - 1, lon)), (jnp.logical_and(stencil, lat < 13), (lat + 1, lon)),
    ):
        pl.when(meant)(lambda target=target: greet(target))
        greeted += meant.astype(jnp.int32)

    @pl.when(owner)
    def _():
        lax.fori_loop(0, 15, greet_helper, 0)

    pl.when(jnp.logical_and(owner, helped_from_afar))(lambda: greet(my_helper))
    pl.when(helped_from_afar)(lambda: greet(my_helper))

    def gather(g):
        per = 3 * len(GROUPS[g])
        for pos, f in enumerate(GROUPS[g]):
            for s in range(3):
                src[g][pl.ds(3 * pos + s, ROWS, stride=per), :] = fields[f][0, :, 128 * s : 128 * (s + 1)]

    def send_rows(g):
        per = 3 * len(GROUPS[g])

        def one(k, size):
            send(
                src[g].at[pl.ds(part_start(k, size) * per, size * per)], relay[g].at[pl.ds(0, size * per)],
                send_a.at[g, k], recv_a.at[g], member(3 * band + k, z, lax.div(lon, 16)),
            )

        @pl.when(band < 2)
        def _():
            for k in range(3):
                one(k, 32)

        @pl.when(band == 2)
        def _():
            for k in range(2):
                one(k, 36)

    loaded(0)
    pl.when(source)(lambda: gather(0))
    pl.semaphore_wait(barrier, greeted)

    @pl.when(helps)
    def _():
        for to_core in range(2):
            target = member(helped, z, to_core)
            pl.when(jnp.logical_not(same(target)))(
                lambda target=target: pl.semaphore_signal(go, inc=1, device_id=target, device_id_type=MESH)
            )

    pl.when(source)(lambda: send_rows(0))
    loaded(1, 2)

    @pl.when(source)
    def _():
        gather(1)
        send_rows(1)

    @pl.when(stencil)
    def _():
        lane = lax.broadcasted_iota(jnp.int32, (ROWS, 128), 1)
        high = [ref[0, :, 256:384] for ref in fields]
        low = [ref[0, :, 0:128] for ref in fields]
        packed[0] = jnp.where(
            lane >= 124, high[0], jnp.where(lane >= 120, pltpu.roll(high[1], 124, 1), pltpu.roll(high[2], 120, 1))
        )
        packed[1] = jnp.where(lane < 4, low[0], jnp.where(lane < 8, pltpu.roll(low[1], 4, 1), pltpu.roll(low[2], 8, 1)))
        remote(packed.at[0], sides.at[0], send_s.at[0], recv_s.at[0], (lat, right))
        remote(packed.at[1], sides.at[1], send_s.at[1], recv_s.at[1], (lat, left))

    pl.when(helped_from_afar)(lambda: pl.semaphore_wait(go, 1))
    for g in range(2):
        per = 3 * len(GROUPS[g])
        each_size(lambda size, g=g, per=per: landed(relay[g].at[pl.ds(0, size * per)], recv_a.at[g]))

        def to_owner(how, i, target, g=g, per=per):
            how(
                relay[g].at[pl.ds(owner_start(i) * per, HOLD * per)],
                recv[g].at[pl.ds(slab * (HOLD * per), HOLD * per)],
                send_b.at[g], recv_b.at[g], target,
            )

        def spread(k, carry, to_owner=to_owner):
            to = chip(k)
            to_owner(remote, nth_at(lax.rem(to + line, 16)), mate(to, 1))
            return carry

        @pl.when(wide)
        def _(to_owner=to_owner):
            for i, to_near in ((0, 0), (10, 8)):
                to_owner(send, i, mate(lax.rem(to_near + 16 - line, 16), 0))

        lax.fori_loop(0, 15, spread, 0)
        to_owner(send, nth_at(near), mate(z, 1))

    @pl.when(stencil)
    def _():
        landed(sides.at[0], recv_s.at[0])
        landed(sides.at[1], recv_s.at[1])
        lane = lax.broadcasted_iota(jnp.int32, (ROWS, 128), 1)
        for f in range(3):
            ext[f, 8 : 8 + ROWS, 0:CELLS] = fields[f][0]
            east_side, west_side = sides[1], sides[0]
            if f:
                east_side, west_side = pltpu.roll(east_side, 128 - 4 * f, 1), pltpu.roll(west_side, 4 * f, 1)
            ext[f, 8 : 8 + ROWS, CELLS : CELLS + 128] = jnp.where(lane < 64, east_side, west_side)

        @pl.when(lat > 2)
        def _():
            remote(ext.at[:, 8:16, :], ext.at[:, 104:112, :], send_r.at[0], recv_r.at[0], (lat - 1, lon))

        @pl.when(lat < 13)
        def _():
            remote(ext.at[:, 96:104, :], ext.at[:, 0:8, :], send_r.at[1], recv_r.at[1], (lat + 1, lon))

        @pl.when(lat == 2)
        def _():
            ext[:, 0:8, :] = jnp.zeros((3, 8, 512), F32)

        @pl.when(lat == 13)
        def _():
            ext[:, 104:112, :] = jnp.zeros((3, 8, 512), F32)

    def transform(g):
        size = HOLD * 3 * len(GROUPS[g])
        order = [(row, pos) for row in range(HOLD) for pos in range(len(GROUPS[g]))]
        grids = [
            jnp.concatenate(
                [recv[g][pl.ds(row * (size // HOLD) + 3 * pos + s, 32, stride=size), :] for s in range(3)], axis=0
            )
            for row, pos in order
        ]
        mixed = outer_step(first_ref[...], jnp.concatenate(grids, axis=1))
        cos, sin = grid_ref[0], grid_ref[1]
        twisted = []
        for n in range(len(order)):
            real, imag = mixed[:HALF, 128 * n : 128 * (n + 1)], mixed[HALF:, 128 * n : 128 * (n + 1)]
            twisted.append(jnp.concatenate([real * cos + imag * sin, imag * cos - real * sin], axis=1))
        spectrum = inner_step(fore_ref, jnp.concatenate(twisted, axis=0))
        return {
            key: (spectrum[HALF * n : HALF * (n + 1), :128], spectrum[HALF * n : HALF * (n + 1), 128:])
            for n, key in enumerate(order)
        }

    def restore(g, spectra):
        size = HOLD * 3 * len(BACK[g])
        order = list(spectra)
        cos, sin = grid_ref[0], grid_ref[1]
        back = inner_step(
            back_ref, jnp.concatenate([jnp.concatenate(spectra[key], axis=1) for key in order], axis=0)
        )
        spun = []
        for n in range(len(order)):
            real, imag = back[HALF * n : HALF * (n + 1), :128], back[HALF * n : HALF * (n + 1), 128:]
            spun.append(jnp.concatenate([real * cos - imag * sin, imag * cos + real * sin], axis=0))
        cells = outer_step(last_ref[...], jnp.concatenate(spun, axis=1))
        for n, (row, pos) in enumerate(order):
            for s in range(3):
                snd[g][pl.ds(row * (size // HOLD) + 3 * pos + s, 32, stride=size), :] = cells[
                    32 * s : 32 * (s + 1), 128 * n : 128 * (n + 1)
                ]

    def put(ref, index, pair):
        ref[(*index, slice(0, HALF))] = pair[0]
        ref[(*index, slice(HALF, 2 * HALF))] = pair[1]

    def get(ref, *index):
        return ref[(*index, slice(0, HALF))], ref[(*index, slice(HALF, 2 * HALF))]

    row0 = jnp.where(south, NLAT - HOLD - HOLD * chain, HOLD * chain)

    def polar(row):
        steps = jnp.where(south, NLAT - 1 - row, row)
        return jnp.abs(jnp.full((1, 128), steps, jnp.int32).astype(F32) + 0.5) * (math.pi / NLAT)

    def cosine(w):
        return jnp.sin(polar(row0 + w - 1))

    def prepare():
        speed = speed_ref[0]
        share_of_pole = jnp.where(south, SPIN, -SPIN).astype(F32)
        for w in range(WINGS):
            there = 1.0
            if w == 0:
                there = jnp.where(has_before, 1.0, 0.0).astype(F32)
            if w == WINGS - 1:
                there = jnp.where(has_after, 1.0, 0.0).astype(F32)
            angle = polar(row0 + w - 1)
            share = 1.0 / jnp.maximum(grid_ref[3], jnp.sin(angle))
            keep = share * (jnp.sin(angle) * there)
            slope = share * (COURANT * grid_ref[2])
            scale[w, 0] = slope
            scale[w, 1] = keep * (share_of_pole * jnp.cos(angle))
            scale[w, 2] = keep * (0.5 * NORTH)
            if 0 < w < WINGS - 1:
                scale[w, 3] = speed * slope
                scale[w, 4] = share * (speed * (0.5 * NORTH) * cosine(w - 1))
                scale[w, 5] = share * (speed * (0.5 * NORTH) * cosine(w + 1))

    def push_east(heights, old, new, w):
        mid, east, north = get(heights, w + 1), get(old, w, 0), get(old, w, 1)
        slope, swirl = scale[w, 0], scale[w, 1]
        put(new, (w, 0), (
            east[0] + slope * mid[1] + swirl * north[0],
            east[1] - slope * mid[0] + swirl * north[1],
        ))

    def push_north(heights, old, new, w):
        low, high = get(heights, w), get(heights, w + 2)
        east, north = get(old, w, 0), get(old, w, 1)
        swirl, climb = scale[w, 1], scale[w, 2]
        put(new, (w, 1), tuple(north[p] - climb * (high[p] - low[p]) - swirl * east[p] for p in range(2)))

    def pushed_height(heights, winds, w):
        mid, east = get(heights, w + 1), get(winds, w, 0)
        low, high = get(winds, w - 1, 1), get(winds, w + 1, 1)
        slope, below, above = scale[w, 3], scale[w, 4], scale[w, 5]
        return (
            mid[0] + slope * east[1] - (above * high[0] - below * low[0]),
            mid[1] - slope * east[0] - (above * high[1] - below * low[1]),
        )

    def trade(e, ref, wing):
        @pl.when(has_before)
        def _():
            remote(
                ref.at[pl.ds(wing, wing)], ref.at[pl.ds(wing + HOLD, wing)],
                send_x.at[e, 0], recv_x.at[e, 1], before_device,
            )

        @pl.when(has_after)
        def _():
            remote(ref.at[pl.ds(HOLD, wing)], ref.at[pl.ds(0, wing)], send_x.at[e, 1], recv_x.at[e, 0], after_device)

    def traded(e, ref, wing):
        pl.when(has_before)(lambda: landed(ref.at[pl.ds(0, wing)], recv_x.at[e, 0]))
        pl.when(has_after)(lambda: landed(ref.at[pl.ds(wing + HOLD, wing)], recv_x.at[e, 1]))

    def send_back(g):
        size = HOLD * 3 * len(BACK[g])
        start = owner_start(nth) * (size // HOLD)

        def one(how, to_z, to_core):
            how(
                snd[g].at[pl.ds((16 * to_core + to_z) * size, size)], home[g].at[pl.ds(start, size)],
                send_c.at[g], recv_c.at[g], mate(to_z, to_core),
            )

        def both(k, carry):
            to = jnp.where(k < 5, lax.rem(z + k, 5), 5 + lax.rem(z + k, 11))
            one(send, to, 0)
            one(send, to, 1)
            return carry

        lax.fori_loop(0, 16, both, 0)

    @pl.when(owner)
    def _():
        loaded(3, 4, 5, 6, 7)
        prepare()

        @pl.when(jnp.logical_not(has_before))
        def _():
            tall[0:2] = jnp.zeros((2, 2 * HALF, 128), F32)
            tall_new[0:2] = jnp.zeros((2, 2 * HALF, 128), F32)
            wind[0] = jnp.zeros((2, 2 * HALF, 128), F32)

        @pl.when(jnp.logical_not(has_after))
        def _():
            tall[2 + HOLD : 4 + HOLD] = jnp.zeros((2, 2 * HALF, 128), F32)
            tall_new[2 + HOLD : 4 + HOLD] = jnp.zeros((2, 2 * HALF, 128), F32)
            wind[1 + HOLD] = jnp.zeros((2, 2 * HALF, 128), F32)

        landed(recv[0], recv_b.at[0])
        for (row, _), pair in transform(0).items():
            put(tall, (2 + row,), pair)
        trade(0, tall, 2)
        landed(recv[1], recv_b.at[1])
        for (row, which), pair in transform(1).items():
            put(wind, (1 + row, which), pair)
        trade(1, wind, 1)
        traded(0, tall, 2)
        traded(1, wind, 1)
        for w in range(WINGS):
            push_east(tall, wind, wind_new, w)
            push_north(tall, wind, wind_new, w)
        for w in range(1, 1 + HOLD):
            put(tall_new, (1 + w,), pushed_height(tall, wind_new, w))
        trade(2, tall_new, 2)
        for w in range(1, 1 + HOLD):
            push_east(tall_new, wind_new, wind_last, w)
        restore(0, {(row, 0): get(wind_last, 1 + row, 0) for row in range(HOLD)})
        send_back(0)
        traded(2, tall_new, 2)
        for w in range(WINGS):
            push_north(tall_new, wind_new, wind_last, w)
        last = {(row, 0): get(wind_last, 1 + row, 1) for row in range(HOLD)}
        last.update({(row, 1): pushed_height(tall_new, wind_last, 1 + row) for row in range(HOLD)})
        restore(1, last)
        send_back(1)

    @pl.when(stencil)
    def _():
        @pl.when(lat > 2)
        def _():
            landed(ext.at[:, 0:8, :], recv_r.at[1])

        @pl.when(lat < 13)
        def _():
            landed(ext.at[:, 104:112, :], recv_r.at[0])

        row = lax.broadcasted_iota(jnp.int32, (ROWS + 16, 128), 0) + (ROWS * lat - 8)
        latitude = (row.astype(F32) + (0.5 - NLAT // 2)) * (math.pi / NLAT)
        wide_cos = jnp.concatenate([jnp.cos(latitude)] * 4, axis=1)
        spin = jnp.concatenate([SPIN * jnp.sin(latitude)] * 4, axis=1)
        inverse = 1.0 / wide_cos
        east_scale = (0.5 * COURANT) * inverse
        speed = speed_ref[0]

        def across(value):
            return pltpu.roll(value, 511, 1) - pltpu.roll(value, 1, 1)

        def along(value):
            return pltpu.roll(value, ROWS + 15, 0) - pltpu.roll(value, 1, 0)

        height, east, north = ext[0], ext[1], ext[2]
        for _step in range(2):
            east_inc = spin * north - east_scale * across(height)
            north_inc = (-0.5 * NORTH) * along(height) - spin * east
            east, north = east + east_inc, north + north_inc
            spread_out = east_scale * across(east) + (0.5 * NORTH) * inverse * along(north * wide_cos)
            height = height - speed * spread_out
        for out, value in zip(outs, (height, east, north)):
            out[0] = value[8 : 8 + ROWS, 0:CELLS]

    for g in range(2):
        per = 3 * len(BACK[g])

        def deliver(size, g=g, per=per):
            landed(home[g].at[pl.ds(0, size * per)], recv_c.at[g])
            send(
                home[g].at[pl.ds(0, size * per)], ret[g].at[pl.ds(part_start(my_part, size) * per, size * per)],
                send_d.at[g], recv_d.at[g, my_part], (my_lat, slab),
            )

        each_size(deliver)

    def back(f, s):
        g = 0 if f in BACK[0] else 1
        return ret[g][pl.ds(3 * BACK[g].index(f) + s, ROWS, stride=3 * len(BACK[g])), :]

    @pl.when(band < 2)
    def _():
        for g in range(2):
            per = 3 * len(BACK[g])
            for k in range(3):
                landed(ret[g].at[pl.ds(part_start(k, 32) * per, 32 * per)], recv_d.at[g, k])
            for f in BACK[g]:
                for s in range(3):
                    outs[f][0, :, 128 * s : 128 * (s + 1)] = back(f, s)

    @pl.when(band == 2)
    def _():
        row = lax.broadcasted_iota(jnp.int32, (ROWS, 128), 0)
        from_pole = jnp.where(south, ROWS - 1 - row, row) + 2 * ROWS
        for g in range(2):
            per = 3 * len(BACK[g])
            for k in range(2):
                landed(ret[g].at[pl.ds(part_start(k, 36) * per, 36 * per)], recv_d.at[g, k])
            for f in BACK[g]:
                for s in range(3):
                    lanes = slice(128 * s, 128 * (s + 1))
                    outs[f][0, :, lanes] = jnp.where(from_pole < FINAL, back(f, s), outs[f][0, :, lanes])

    for g in range(2):
        per = 3 * len(GROUPS[g])

        def left_parts(size, parts, g=g, per=per):
            for k in range(parts):
                other = jnp.logical_not(same(member(3 * band + k, z, lax.div(lon, 16))))
                pl.when(other)(lambda k=k: landed(src[g].at[pl.ds(0, size * per)], send_a.at[g, k]))

        pl.when(band < 2)(lambda f=left_parts: f(32, 3))
        pl.when(band == 2)(lambda f=left_parts: f(36, 2))
        for case, count in (
            (jnp.logical_and(jnp.logical_not(wide), owner), 15),
            (jnp.logical_and(jnp.logical_not(wide), jnp.logical_not(owner)), 16),
            (jnp.logical_and(wide, owner), 17),
            (jnp.logical_and(wide, jnp.logical_not(owner)), 18),
        ):
            pl.when(case)(
                lambda g=g, n=count * HOLD * per: landed(relay[g].at[pl.ds(0, n)], send_b.at[g])
            )
        ret_per = 3 * len(BACK[g])
        pl.when(owner)(lambda g=g, per=ret_per: landed(snd[g].at[pl.ds(0, 31 * HOLD * per)], send_c.at[g]))

        @pl.when(jnp.logical_not(same((my_lat, slab))))
        def _(g=g, per=ret_per):
            each_size(lambda size: landed(home[g].at[pl.ds(0, size * per)], send_d.at[g]))

    @pl.when(stencil)
    def _():
        for side in range(2):
            landed(packed.at[side], send_s.at[side])

        @pl.when(lat > 2)
        def _():
            landed(ext.at[:, 8:16, :], send_r.at[0])

        @pl.when(lat < 13)
        def _():
            landed(ext.at[:, 96:104, :], send_r.at[1])

    for e, (ref, wing) in enumerate(((tall, 2), (wind, 1), (tall_new, 2))):
        pl.when(has_before)(lambda e=e, ref=ref, wing=wing: landed(ref.at[pl.ds(0, wing)], send_x.at[e, 0]))
        pl.when(has_after)(lambda e=e, ref=ref, wing=wing: landed(ref.at[pl.ds(0, wing)], send_x.at[e, 1]))


def write(h_ref, u_ref, v_ref, h_out, u_out, v_out, sems):
    copies = [
        pltpu.make_async_copy(here, there, sems.at[n])
        for n, (here, there) in enumerate(((h_ref, h_out), (u_ref, u_out), (v_ref, v_out)))
    ]
    for copy in copies:
        copy.start()
    for copy in copies:
        copy.wait()


def body(height, east_wind, north_wind, wave_speed_sq):
    constants = [np.asarray(table, np.float32) for table in tables()]
    block = jax.ShapeDtypeStruct((1, ROWS, CELLS), F32)
    pairs = []
    for groups, rows in ((GROUPS, ROWS), (GROUPS, 36), (GROUPS, 32 * HOLD), (BACK, 32 * HOLD), (BACK, 36), (BACK, ROWS)):
        pairs += [pltpu.VMEM((rows * 3 * len(group), 128), F32) for group in groups]
    dma = pltpu.SemaphoreType.DMA
    vmem = pl.BlockSpec(memory_space=pltpu.VMEM)
    results = pl.pallas_call(
        kernel,
        out_shape=[pltpu.VMEM(block.shape, F32)] * 3,
        in_specs=[pl.BlockSpec(memory_space=pltpu.SMEM)] + [pl.BlockSpec(memory_space=pl.ANY)] * 8,
        out_specs=[vmem] * 3,
        scratch_shapes=[
            *[pltpu.VMEM((1, ROWS, CELLS), F32)] * 3,
            *[pltpu.VMEM(table.shape, table.dtype) for table in constants],
            *pairs,
            *[pltpu.VMEM((HOLD + 4, 2 * HALF, 128), F32)] * 2,
            *[pltpu.VMEM((WINGS, 2, 2 * HALF, 128), F32)] * 3,
            pltpu.VMEM((WINGS, 6, HALF, 128), F32),
            pltpu.VMEM((2, ROWS, 128), F32),
            pltpu.VMEM((2, ROWS, 128), F32),
            pltpu.VMEM((3, ROWS + 16, 512), F32),
            pltpu.SemaphoreType.REGULAR,
            dma((8,)), dma((2, 3)), dma((2,)), dma((2,)), dma((2,)), dma((2,)), dma((2,)), dma((2,)), dma((2, 3)),
            dma((3, 2)), dma((3, 2)), dma((2,)), dma((2,)), dma((2,)), dma((2,)),
        ],
        compiler_params=pltpu.CompilerParams(
            collective_id=0, has_side_effects=True, vmem_limit_bytes=60 * 1024 * 1024
        ),
        name="substeps",
    )(wave_speed_sq, height, east_wind, north_wind, *constants)
    return pl.pallas_call(
        write,
        out_shape=[block] * 3,
        in_specs=[vmem] * 3,
        out_specs=[pl.BlockSpec(memory_space=pl.ANY)] * 3,
        scratch_shapes=[dma((3,))],
        compiler_params=pltpu.CompilerParams(vmem_limit_bytes=16 * 1024 * 1024),
        name="write",
    )(*results)


def solution(mesh):
    block = P(None, "lat", "lon")
    return jax.shard_map(
        lambda *args: tuple(body(*args)),
        mesh=mesh, in_specs=(block, block, block, P()), out_specs=(block, block, block), check_vma=False,
    )
```

```python
import math

import jax
import jax.numpy as jnp
import ml_dtypes
import numpy as np
from jax import lax
from jax.experimental import pallas as pl
from jax.experimental.pallas import tpu as pltpu
from jax.sharding import PartitionSpec as P

NLON, NLAT = 12288, 1536
ROWS, CELLS = 96, 384
OUTER, INNER = 96, 128
HALF = 56
COURANT, SPIN = 0.45, 0.3
NORTH = COURANT * 2.0 * NLAT / NLON
FINAL = 260
HOLD = 2
OWNERS = 132
WINGS = HOLD + 2
MESH = pl.DeviceIdType.MESH
F32, BF16 = jnp.float32, jnp.bfloat16
GROUPS = ((0,), (1, 2))
BACK_ROW = (3, 2, 1, 0)
BACK = ((1,), (2, 0))


def split(table):
    high = table.astype(ml_dtypes.bfloat16)
    low = (table - high.astype(np.float64)).astype(ml_dtypes.bfloat16)
    return high, low


def tables():
    a = np.array([3 * d + s for s in range(3) for d in range(32)])
    k1 = np.arange(HALF)
    live = (k1 <= OUTER // 2).astype(np.float64)
    angle = 2 * np.pi * ((k1[:, None] * a[None, :]) % OUTER) / OUTER
    first = np.concatenate([np.cos(angle) * live[:, None], -np.sin(angle) * live[:, None]], axis=0)
    weight = live * np.where((k1 == 0) | (k1 == OUTER // 2), 1.0, 2.0) / NLON
    last = np.concatenate([np.cos(angle) * weight[:, None], -np.sin(angle) * weight[:, None]], axis=0).T
    n = np.arange(INNER)
    turn = 2 * np.pi * (k1[:, None] * n[None, :]) / NLON
    inner = 2 * np.pi * ((n[:, None] * n[None, :]) % INNER) / INNER
    cos, sin = np.cos(inner), np.sin(inner)
    forward = np.block([[cos, -sin], [sin, cos]])
    backward = np.block([[cos, sin], [-sin, cos]])
    wave = k1[:, None] + OUTER * n[None, :]
    steep = np.sin(2 * np.pi * wave / NLON) * live[:, None]
    half_sine = np.where(live[:, None] > 0, 0.5 * np.abs(np.sin(np.pi * wave / NLON)), 1.0)
    first_high, first_low = split(first)
    last_high, last_low = split(last)
    forward_high, forward_low = split(forward)
    backward_high, backward_low = split(backward)
    grid = np.stack([np.cos(turn), np.sin(turn), steep, half_sine]).astype(np.float32)
    return (
        np.concatenate([first_high, first_low, first_high], axis=1),
        np.concatenate([last_high, last_low, last_high], axis=1),
        np.stack([forward_high, forward_low]),
        np.stack([backward_high, backward_low]),
        grid,
    )


def parts(value):
    high = value.astype(BF16)
    return high, (value - high.astype(F32)).astype(BF16)


def dot(left, right):
    return jnp.dot(left, right, preferred_element_type=F32)


def outer_step(table, value):
    high, low = parts(value)
    return dot(table.astype(BF16), jnp.concatenate([high, high, low], axis=0))


def inner_step(table, value):
    high, low = parts(value)
    table_high, table_low = table[0].astype(BF16), table[1].astype(BF16)
    return dot(high, table_high) + dot(low, table_high) + dot(high, table_low)


def kernel(
    speed_ref, h_hbm, u_hbm, v_hbm, first_hbm, last_hbm, fore_hbm, back_hbm, grid_hbm,
    h_out, u_out, v_out,
    h_ref, u_ref, v_ref, first_ref, last_ref, fore_ref, back_ref, grid_ref,
    src0, src1, relay0, relay1, recv0, recv1, snd0, snd1, home0, home1, ret0, ret1,
    tall, tall_new, wind, wind_new, wind_last, scale, packed, sides, ext,
    go, loads, send_a, recv_a, send_b, recv_b, send_c, recv_c, send_d, recv_d, send_x, recv_x, send_s, recv_s, send_r, recv_r,
):
    fields, outs = (h_ref, u_ref, v_ref), (h_out, u_out, v_out)
    operands = (h_hbm, u_hbm, v_hbm, first_hbm, last_hbm, fore_hbm, back_hbm, grid_hbm)
    held = (h_ref, u_ref, v_ref, first_ref, last_ref, fore_ref, back_ref, grid_ref)
    src, relay, recv = (src0, src1), (relay0, relay1), (recv0, recv1)
    snd, home, ret = (snd0, snd1), (home0, home1), (ret0, ret1)
    lat, lon = lax.axis_index("lat"), lax.axis_index("lon")
    south = lat >= 8
    band = jnp.where(south, 15 - lat, lat)
    core = lax.rem(band, 2)
    z = lax.rem(lon, 16)
    x = 2 * lax.div(lon, 16) + lax.rem(lax.div(band, 2), 2)

    def back_x(n):
        return jnp.where(n == 4, BACK_ROW[0], jnp.where(n == 5, BACK_ROW[1], jnp.where(n == 6, BACK_ROW[2], BACK_ROW[3])))

    def back_line(n):
        return jnp.where(n == BACK_ROW[0], 4, jnp.where(n == BACK_ROW[1], 5, jnp.where(n == BACK_ROW[2], 6, 7)))

    line = jnp.where(band < 4, x, back_line(x))
    wide = line >= 6
    near = lax.rem(z + line, 16)
    slab = 16 * core + z
    extra = jnp.logical_and(wide, jnp.logical_and(core == 0, jnp.logical_or(near == 0, near == 8)))
    owner = jnp.logical_or(core == 1, extra)
    owners = jnp.where(wide, 18, 16)

    def nth_at(to_near):
        return to_near + jnp.where(wide, 1 + jnp.where(to_near > 8, 1, 0), 0)

    nth = jnp.where(core == 1, nth_at(near), jnp.where(near == 0, 0, 10))
    chain = 16 * line + 2 * jnp.where(line == 7, 1, 0) + nth
    source = band <= 2
    stencil = band >= 2
    my_band = jnp.where(wide, 2, lax.div(line, 3))
    my_lat = jnp.where(south, 15 - my_band, my_band)
    my_part = line - 3 * my_band

    def member(to_line, to_z, to_core):
        to_x = jnp.where(to_line < 4, to_line, back_x(to_line))
        to_band = 4 * lax.div(to_line, 4) + 2 * lax.rem(to_x, 2) + to_core
        return jnp.where(south, 15 - to_band, to_band), 16 * lax.div(to_x, 2) + to_z

    def mate(to_z, to_core):
        shift = to_core - core
        return jnp.where(south, lat - shift, lat + shift), lon - z + to_z

    def holder(n):
        to_line = jnp.where(n < 96, lax.div(n, 16), 6 + lax.div(jnp.maximum(n - 96, 0), 18))
        to_nth = n - 16 * to_line - 2 * jnp.where(to_line == 7, 1, 0)
        broad = to_line >= 6
        to_near = jnp.where(broad, jnp.maximum(to_nth - jnp.where(to_nth > 9, 2, 1), 0), to_nth)
        to_core = jnp.where(jnp.logical_and(broad, jnp.logical_or(to_nth == 0, to_nth == 10)), 0, 1)
        return member(to_line, lax.rem(to_near + 16 - to_line, 16), to_core)

    def chip(k):
        away = 8 - lax.div(k + 1, 2)
        return lax.rem(z + 16 + jnp.where(lax.rem(k, 2) == 1, away, -away), 16)

    def same(target):
        return jnp.logical_and(target[0] == lat, target[1] == lon)

    def remote(here, there, send_sem, recv_sem, target):
        pltpu.make_async_remote_copy(
            src_ref=here, dst_ref=there, send_sem=send_sem, recv_sem=recv_sem, device_id=target, device_id_type=MESH
        ).start()

    def send(here, there, send_sem, recv_sem, target):
        own = same(target)

        @pl.when(own)
        def _():
            pltpu.make_async_copy(here, there, recv_sem).start()

        @pl.when(jnp.logical_not(own))
        def _():
            remote(here, there, send_sem, recv_sem, target)

    def landed(ref, sem):
        pltpu.make_async_copy(ref, ref, sem).wait()

    def part_start(k, size):
        return jnp.where(south, ROWS - size * (k + 1), size * k)

    def owner_start(i):
        return HOLD * jnp.where(south, owners - 1 - i, i)

    def each_size(act):
        pl.when(jnp.logical_not(wide))(lambda: act(32))
        pl.when(wide)(lambda: act(36))

    right = jnp.where(lon == 31, 0, lon + 1)
    left = jnp.where(lon == 0, 31, lon - 1)
    before = chain + jnp.where(south, 1, -1)
    after = chain + jnp.where(south, -1, 1)
    has_before = jnp.logical_and(owner, jnp.logical_and(before >= 0, before < OWNERS))
    has_after = jnp.logical_and(owner, jnp.logical_and(after >= 0, after < OWNERS))
    before_device, after_device = holder(jnp.clip(before, 0, OWNERS - 1)), holder(jnp.clip(after, 0, OWNERS - 1))

    barrier = pltpu.get_barrier_semaphore()

    def greet(target):
        pl.semaphore_signal(barrier, inc=1, device_id=target, device_id_type=MESH)

    def greet_other(target):
        pl.when(jnp.logical_not(same(target)))(lambda: greet(target))

    pl.when(jnp.logical_not(same((my_lat, slab))))(lambda: greet((my_lat, slab)))

    def load(*indices):
        for index in indices:
            pltpu.make_async_copy(operands[index], held[index], loads.at[index]).start()

    def loaded(*indices):
        for index in indices:
            pltpu.make_async_copy(operands[index], held[index], loads.at[index]).wait()

    load(0, 1, 2)
    pl.when(owner)(lambda: load(3, 4, 5, 6, 7))

    def helper(of_line, to_z):
        of_x = jnp.where(of_line < 4, of_line, back_x(of_line))
        return member(back_line(of_x), to_z, lax.div(of_line, 4))

    helps = band >= 4
    helped = jnp.where(core == 1, back_line(x), x)

    def greet_helper(k, carry):
        greet(helper(line, chip(k)))
        return carry

    my_helper = helper(line, z)
    helped_from_afar = jnp.logical_not(same(my_helper))

    greeted = jnp.where(helps, jnp.where(helped >= 6, 18, 16) + 2 - 2 * core, 0)
    for k in range(3):
        target = member(jnp.minimum(3 * band + k, 7), z, lax.div(lon, 16))
        meant = jnp.logical_or(band < 2, jnp.logical_and(band == 2, k < 2))
        meant = jnp.logical_and(meant, jnp.logical_not(same(target)))
        greeted += meant.astype(jnp.int32)
    for meant, target in (
        (has_before, before_device), (has_after, after_device), (stencil, (lat, left)), (stencil, (lat, right)),
        (jnp.logical_and(stencil, lat > 2), (lat - 1, lon)), (jnp.logical_and(stencil, lat < 13), (lat + 1, lon)),
    ):
        pl.when(meant)(lambda target=target: greet(target))
        greeted += meant.astype(jnp.int32)

    @pl.when(owner)
    def _():
        lax.fori_loop(0, 15, greet_helper, 0)

    pl.when(jnp.logical_and(owner, helped_from_afar))(lambda: greet(my_helper))
    pl.when(helped_from_afar)(lambda: greet(my_helper))

    def gather(g):
        per = 3 * len(GROUPS[g])
        for pos, f in enumerate(GROUPS[g]):
            for s in range(3):
                src[g][pl.ds(3 * pos + s, ROWS, stride=per), :] = fields[f][0, :, 128 * s : 128 * (s + 1)]

    def send_rows(g):
        per = 3 * len(GROUPS[g])

        def one(k, size):
            send(
                src[g].at[pl.ds(part_start(k, size) * per, size * per)], relay[g].at[pl.ds(0, size * per)],
                send_a.at[g, k], recv_a.at[g], member(3 * band + k, z, lax.div(lon, 16)),
            )

        @pl.when(band < 2)
        def _():
            for k in range(3):
                one(k, 32)

        @pl.when(band == 2)
        def _():
            for k in range(2):
                one(k, 36)

    loaded(0)
    pl.when(source)(lambda: gather(0))
    pl.semaphore_wait(barrier, greeted)

    @pl.when(helps)
    def _():
        for to_core in range(2):
            target = member(helped, z, to_core)
            pl.when(jnp.logical_not(same(target)))(
                lambda target=target: pl.semaphore_signal(go, inc=1, device_id=target, device_id_type=MESH)
            )

    pl.when(source)(lambda: send_rows(0))
    loaded(1, 2)

    @pl.when(source)
    def _():
        gather(1)
        send_rows(1)

    @pl.when(stencil)
    def _():
        lane = lax.broadcasted_iota(jnp.int32, (ROWS, 128), 1)
        high = [ref[0, :, 256:384] for ref in fields]
        low = [ref[0, :, 0:128] for ref in fields]
        packed[0] = jnp.where(
            lane >= 124, high[0], jnp.where(lane >= 120, pltpu.roll(high[1], 124, 1), pltpu.roll(high[2], 120, 1))
        )
        packed[1] = jnp.where(lane < 4, low[0], jnp.where(lane < 8, pltpu.roll(low[1], 4, 1), pltpu.roll(low[2], 8, 1)))
        remote(packed.at[0], sides.at[0], send_s.at[0], recv_s.at[0], (lat, right))
        remote(packed.at[1], sides.at[1], send_s.at[1], recv_s.at[1], (lat, left))

    pl.when(helped_from_afar)(lambda: pl.semaphore_wait(go, 1))
    for g in range(2):
        per = 3 * len(GROUPS[g])
        each_size(lambda size, g=g, per=per: landed(relay[g].at[pl.ds(0, size * per)], recv_a.at[g]))

        def to_owner(how, i, target, g=g, per=per):
            how(
                relay[g].at[pl.ds(owner_start(i) * per, HOLD * per)],
                recv[g].at[pl.ds(slab * (HOLD * per), HOLD * per)],
                send_b.at[g], recv_b.at[g], target,
            )

        def spread(k, carry, to_owner=to_owner):
            to = chip(k)
            to_owner(remote, nth_at(lax.rem(to + line, 16)), mate(to, 1))
            return carry

        @pl.when(wide)
        def _(to_owner=to_owner):
            for i, to_near in ((0, 0), (10, 8)):
                to_owner(send, i, mate(lax.rem(to_near + 16 - line, 16), 0))

        lax.fori_loop(0, 15, spread, 0)
        to_owner(send, nth_at(near), mate(z, 1))

    @pl.when(stencil)
    def _():
        landed(sides.at[0], recv_s.at[0])
        landed(sides.at[1], recv_s.at[1])
        lane = lax.broadcasted_iota(jnp.int32, (ROWS, 128), 1)
        for f in range(3):
            ext[f, 8 : 8 + ROWS, 0:CELLS] = fields[f][0]
            east_side, west_side = sides[1], sides[0]
            if f:
                east_side, west_side = pltpu.roll(east_side, 128 - 4 * f, 1), pltpu.roll(west_side, 4 * f, 1)
            ext[f, 8 : 8 + ROWS, CELLS : CELLS + 128] = jnp.where(lane < 64, east_side, west_side)

        @pl.when(lat > 2)
        def _():
            remote(ext.at[:, 8:16, :], ext.at[:, 104:112, :], send_r.at[0], recv_r.at[0], (lat - 1, lon))

        @pl.when(lat < 13)
        def _():
            remote(ext.at[:, 96:104, :], ext.at[:, 0:8, :], send_r.at[1], recv_r.at[1], (lat + 1, lon))

        @pl.when(lat == 2)
        def _():
            ext[:, 0:8, :] = jnp.zeros((3, 8, 512), F32)

        @pl.when(lat == 13)
        def _():
            ext[:, 104:112, :] = jnp.zeros((3, 8, 512), F32)

    def transform(g):
        size = HOLD * 3 * len(GROUPS[g])
        order = [(row, pos) for row in range(HOLD) for pos in range(len(GROUPS[g]))]
        grids = [
            jnp.concatenate(
                [recv[g][pl.ds(row * (size // HOLD) + 3 * pos + s, 32, stride=size), :] for s in range(3)], axis=0
            )
            for row, pos in order
        ]
        mixed = outer_step(first_ref[...], jnp.concatenate(grids, axis=1))
        cos, sin = grid_ref[0], grid_ref[1]
        twisted = []
        for n in range(len(order)):
            real, imag = mixed[:HALF, 128 * n : 128 * (n + 1)], mixed[HALF:, 128 * n : 128 * (n + 1)]
            twisted.append(jnp.concatenate([real * cos + imag * sin, imag * cos - real * sin], axis=1))
        spectrum = inner_step(fore_ref, jnp.concatenate(twisted, axis=0))
        return {
            key: (spectrum[HALF * n : HALF * (n + 1), :128], spectrum[HALF * n : HALF * (n + 1), 128:])
            for n, key in enumerate(order)
        }

    def restore(g, spectra):
        size = HOLD * 3 * len(BACK[g])
        order = list(spectra)
        cos, sin = grid_ref[0], grid_ref[1]
        back = inner_step(
            back_ref, jnp.concatenate([jnp.concatenate(spectra[key], axis=1) for key in order], axis=0)
        )
        spun = []
        for n in range(len(order)):
            real, imag = back[HALF * n : HALF * (n + 1), :128], back[HALF * n : HALF * (n + 1), 128:]
            spun.append(jnp.concatenate([real * cos - imag * sin, imag * cos + real * sin], axis=0))
        cells = outer_step(last_ref[...], jnp.concatenate(spun, axis=1))
        for n, (row, pos) in enumerate(order):
            for s in range(3):
                snd[g][pl.ds(row * (size // HOLD) + 3 * pos + s, 32, stride=size), :] = cells[
                    32 * s : 32 * (s + 1), 128 * n : 128 * (n + 1)
                ]

    def put(ref, index, pair):
        ref[(*index, slice(0, HALF))] = pair[0]
        ref[(*index, slice(HALF, 2 * HALF))] = pair[1]

    def get(ref, *index):
        return ref[(*index, slice(0, HALF))], ref[(*index, slice(HALF, 2 * HALF))]

    row0 = jnp.where(south, NLAT - HOLD - HOLD * chain, HOLD * chain)

    def polar(row):
        steps = jnp.where(south, NLAT - 1 - row, row)
        return jnp.abs(jnp.full((1, 128), steps, jnp.int32).astype(F32) + 0.5) * (math.pi / NLAT)

    def cosine(w):
        return jnp.sin(polar(row0 + w - 1))

    def prepare():
        speed = speed_ref[0]
        share_of_pole = jnp.where(south, SPIN, -SPIN).astype(F32)
        for w in range(WINGS):
            there = 1.0
            if w == 0:
                there = jnp.where(has_before, 1.0, 0.0).astype(F32)
            if w == WINGS - 1:
                there = jnp.where(has_after, 1.0, 0.0).astype(F32)
            angle = polar(row0 + w - 1)
            share = 1.0 / jnp.maximum(grid_ref[3], jnp.sin(angle))
            keep = share * (jnp.sin(angle) * there)
            slope = share * (COURANT * grid_ref[2])
            scale[w, 0] = slope
            scale[w, 1] = keep * (share_of_pole * jnp.cos(angle))
            scale[w, 2] = keep * (0.5 * NORTH)
            if 0 < w < WINGS - 1:
                scale[w, 3] = speed * slope
                scale[w, 4] = share * (speed * (0.5 * NORTH) * cosine(w - 1))
                scale[w, 5] = share * (speed * (0.5 * NORTH) * cosine(w + 1))

    def push_east(heights, old, new, w):
        mid, east, north = get(heights, w + 1), get(old, w, 0), get(old, w, 1)
        slope, swirl = scale[w, 0], scale[w, 1]
        put(new, (w, 0), (
            east[0] + slope * mid[1] + swirl * north[0],
            east[1] - slope * mid[0] + swirl * north[1],
        ))

    def push_north(heights, old, new, w):
        low, high = get(heights, w), get(heights, w + 2)
        east, north = get(old, w, 0), get(old, w, 1)
        swirl, climb = scale[w, 1], scale[w, 2]
        put(new, (w, 1), tuple(north[p] - climb * (high[p] - low[p]) - swirl * east[p] for p in range(2)))

    def pushed_height(heights, winds, w):
        mid, east = get(heights, w + 1), get(winds, w, 0)
        low, high = get(winds, w - 1, 1), get(winds, w + 1, 1)
        slope, below, above = scale[w, 3], scale[w, 4], scale[w, 5]
        return (
            mid[0] + slope * east[1] - (above * high[0] - below * low[0]),
            mid[1] - slope * east[0] - (above * high[1] - below * low[1]),
        )

    def trade(e, ref, wing):
        @pl.when(has_before)
        def _():
            remote(
                ref.at[pl.ds(wing, wing)], ref.at[pl.ds(wing + HOLD, wing)],
                send_x.at[e, 0], recv_x.at[e, 1], before_device,
            )

        @pl.when(has_after)
        def _():
            remote(ref.at[pl.ds(HOLD, wing)], ref.at[pl.ds(0, wing)], send_x.at[e, 1], recv_x.at[e, 0], after_device)

    def traded(e, ref, wing):
        pl.when(has_before)(lambda: landed(ref.at[pl.ds(0, wing)], recv_x.at[e, 0]))
        pl.when(has_after)(lambda: landed(ref.at[pl.ds(wing + HOLD, wing)], recv_x.at[e, 1]))

    def send_back(g):
        size = HOLD * 3 * len(BACK[g])
        start = owner_start(nth) * (size // HOLD)

        def one(how, to_z, to_core):
            how(
                snd[g].at[pl.ds((16 * to_core + to_z) * size, size)], home[g].at[pl.ds(start, size)],
                send_c.at[g], recv_c.at[g, lax.div(near, 4) if g else 0], mate(to_z, to_core),
            )

        def both(k, carry):
            to = jnp.where(k < 5, lax.rem(z + k, 5), 5 + lax.rem(z + k, 11))
            one(send, to, 0)
            one(send, to, 1)
            return carry

        lax.fori_loop(0, 16, both, 0)

    @pl.when(owner)
    def _():
        loaded(3, 4, 5, 6, 7)
        prepare()

        @pl.when(jnp.logical_not(has_before))
        def _():
            tall[0:2] = jnp.zeros((2, 2 * HALF, 128), F32)
            tall_new[0:2] = jnp.zeros((2, 2 * HALF, 128), F32)
            wind[0] = jnp.zeros((2, 2 * HALF, 128), F32)

        @pl.when(jnp.logical_not(has_after))
        def _():
            tall[2 + HOLD : 4 + HOLD] = jnp.zeros((2, 2 * HALF, 128), F32)
            tall_new[2 + HOLD : 4 + HOLD] = jnp.zeros((2, 2 * HALF, 128), F32)
            wind[1 + HOLD] = jnp.zeros((2, 2 * HALF, 128), F32)

        landed(recv[0], recv_b.at[0])
        for (row, _), pair in transform(0).items():
            put(tall, (2 + row,), pair)
        trade(0, tall, 2)
        landed(recv[1], recv_b.at[1])
        for (row, which), pair in transform(1).items():
            put(wind, (1 + row, which), pair)
        trade(1, wind, 1)
        traded(0, tall, 2)
        traded(1, wind, 1)
        for w in range(WINGS):
            push_east(tall, wind, wind_new, w)
            push_north(tall, wind, wind_new, w)
        for w in range(1, 1 + HOLD):
            put(tall_new, (1 + w,), pushed_height(tall, wind_new, w))
        trade(2, tall_new, 2)
        for w in range(1, 1 + HOLD):
            push_east(tall_new, wind_new, wind_last, w)
        restore(0, {(row, 0): get(wind_last, 1 + row, 0) for row in range(HOLD)})
        send_back(0)
        traded(2, tall_new, 2)
        for w in range(WINGS):
            push_north(tall_new, wind_new, wind_last, w)
        last = {(row, 0): get(wind_last, 1 + row, 1) for row in range(HOLD)}
        last.update({(row, 1): pushed_height(tall_new, wind_last, 1 + row) for row in range(HOLD)})
        restore(1, last)
        send_back(1)

    @pl.when(stencil)
    def _():
        @pl.when(lat > 2)
        def _():
            landed(ext.at[:, 0:8, :], recv_r.at[1])

        @pl.when(lat < 13)
        def _():
            landed(ext.at[:, 104:112, :], recv_r.at[0])

        row = lax.broadcasted_iota(jnp.int32, (ROWS + 16, 128), 0) + (ROWS * lat - 8)
        latitude = (row.astype(F32) + (0.5 - NLAT // 2)) * (math.pi / NLAT)
        wide_cos = jnp.concatenate([jnp.cos(latitude)] * 4, axis=1)
        spin = jnp.concatenate([SPIN * jnp.sin(latitude)] * 4, axis=1)
        inverse = 1.0 / wide_cos
        east_scale = (0.5 * COURANT) * inverse
        speed = speed_ref[0]

        def across(value):
            return pltpu.roll(value, 511, 1) - pltpu.roll(value, 1, 1)

        def along(value):
            return pltpu.roll(value, ROWS + 15, 0) - pltpu.roll(value, 1, 0)

        height, east, north = ext[0], ext[1], ext[2]
        for _step in range(2):
            east_inc = spin * north - east_scale * across(height)
            north_inc = (-0.5 * NORTH) * along(height) - spin * east
            east, north = east + east_inc, north + north_inc
            spread_out = east_scale * across(east) + (0.5 * NORTH) * inverse * along(north * wide_cos)
            height = height - speed * spread_out
        for out, value in zip(outs, (height, east, north)):
            out[0] = value[8 : 8 + ROWS, 0:CELLS]

    def deliver(size):
        per = 3 * len(BACK[0])
        landed(home[0].at[pl.ds(0, size * per)], recv_c.at[0, 0])
        send(
            home[0].at[pl.ds(0, size * per)], ret[0].at[pl.ds(part_start(my_part, size) * per, size * per)],
            send_d.at[0], recv_d.at[0, my_part], (my_lat, slab),
        )

    def deliver_quarter(k):
        per = 3 * len(BACK[1])
        turn = jnp.where(lax.rem(near, 4) < 2, 3, 1)
        quarter = lax.rem(lax.div(near, 4) + (0, turn, 4 - turn, 2)[k], 4)

        def rows(size, line_size):
            first = jnp.where(quarter == 0, 0, nth_at(4 * quarter))
            start = jnp.where(south, line_size - size - HOLD * first, HOLD * first)
            here = home[1].at[pl.ds(start * per, size * per)]
            landed(here, recv_c.at[1, quarter])
            send(
                here, ret[1].at[pl.ds((part_start(my_part, line_size) + start) * per, size * per)],
                send_d.at[1], recv_d.at[1, my_part], (my_lat, slab),
            )

        large = jnp.logical_and(wide, lax.rem(quarter, 2) == 0)
        pl.when(jnp.logical_not(wide))(lambda: rows(8, 32))
        pl.when(large)(lambda: rows(10, 36))
        pl.when(jnp.logical_and(wide, jnp.logical_not(large)))(lambda: rows(8, 36))

    each_size(deliver)
    for k in range(4):
        deliver_quarter(k)

    def back(f, s):
        g = 0 if f in BACK[0] else 1
        return ret[g][pl.ds(3 * BACK[g].index(f) + s, ROWS, stride=3 * len(BACK[g])), :]

    @pl.when(band < 2)
    def _():
        for g in range(2):
            per = 3 * len(BACK[g])
            for k in range(3):
                landed(ret[g].at[pl.ds(part_start(k, 32) * per, 32 * per)], recv_d.at[g, k])
            for f in BACK[g]:
                for s in range(3):
                    outs[f][0, :, 128 * s : 128 * (s + 1)] = back(f, s)

    @pl.when(band == 2)
    def _():
        row = lax.broadcasted_iota(jnp.int32, (ROWS, 128), 0)
        from_pole = jnp.where(south, ROWS - 1 - row, row) + 2 * ROWS
        for g in range(2):
            per = 3 * len(BACK[g])
            for k in range(2):
                landed(ret[g].at[pl.ds(part_start(k, 36) * per, 36 * per)], recv_d.at[g, k])
            for f in BACK[g]:
                for s in range(3):
                    lanes = slice(128 * s, 128 * (s + 1))
                    outs[f][0, :, lanes] = jnp.where(from_pole < FINAL, back(f, s), outs[f][0, :, lanes])

    for g in range(2):
        per = 3 * len(GROUPS[g])

        def left_parts(size, parts, g=g, per=per):
            for k in range(parts):
                other = jnp.logical_not(same(member(3 * band + k, z, lax.div(lon, 16))))
                pl.when(other)(lambda k=k: landed(src[g].at[pl.ds(0, size * per)], send_a.at[g, k]))

        pl.when(band < 2)(lambda f=left_parts: f(32, 3))
        pl.when(band == 2)(lambda f=left_parts: f(36, 2))
        for case, count in (
            (jnp.logical_and(jnp.logical_not(wide), owner), 15),
            (jnp.logical_and(jnp.logical_not(wide), jnp.logical_not(owner)), 16),
            (jnp.logical_and(wide, owner), 17),
            (jnp.logical_and(wide, jnp.logical_not(owner)), 18),
        ):
            pl.when(case)(
                lambda g=g, n=count * HOLD * per: landed(relay[g].at[pl.ds(0, n)], send_b.at[g])
            )
        ret_per = 3 * len(BACK[g])
        pl.when(owner)(lambda g=g, per=ret_per: landed(snd[g].at[pl.ds(0, 31 * HOLD * per)], send_c.at[g]))

        @pl.when(jnp.logical_not(same((my_lat, slab))))
        def _(g=g, per=ret_per):
            each_size(lambda size: landed(home[g].at[pl.ds(0, size * per)], send_d.at[g]))

    @pl.when(stencil)
    def _():
        for side in range(2):
            landed(packed.at[side], send_s.at[side])

        @pl.when(lat > 2)
        def _():
            landed(ext.at[:, 8:16, :], send_r.at[0])

        @pl.when(lat < 13)
        def _():
            landed(ext.at[:, 96:104, :], send_r.at[1])

    for e, (ref, wing) in enumerate(((tall, 2), (wind, 1), (tall_new, 2))):
        pl.when(has_before)(lambda e=e, ref=ref, wing=wing: landed(ref.at[pl.ds(0, wing)], send_x.at[e, 0]))
        pl.when(has_after)(lambda e=e, ref=ref, wing=wing: landed(ref.at[pl.ds(0, wing)], send_x.at[e, 1]))


def write(h_ref, u_ref, v_ref, h_out, u_out, v_out, sems):
    copies = [
        pltpu.make_async_copy(here, there, sems.at[n])
        for n, (here, there) in enumerate(((h_ref, h_out), (u_ref, u_out), (v_ref, v_out)))
    ]
    for copy in copies:
        copy.start()
    for copy in copies:
        copy.wait()


def body(height, east_wind, north_wind, wave_speed_sq):
    constants = [np.asarray(table, np.float32) for table in tables()]
    block = jax.ShapeDtypeStruct((1, ROWS, CELLS), F32)
    pairs = []
    for groups, rows in ((GROUPS, ROWS), (GROUPS, 36), (GROUPS, 32 * HOLD), (BACK, 32 * HOLD), (BACK, 36), (BACK, ROWS)):
        pairs += [pltpu.VMEM((rows * 3 * len(group), 128), F32) for group in groups]
    dma = pltpu.SemaphoreType.DMA
    vmem = pl.BlockSpec(memory_space=pltpu.VMEM)
    results = pl.pallas_call(
        kernel,
        out_shape=[pltpu.VMEM(block.shape, F32)] * 3,
        in_specs=[pl.BlockSpec(memory_space=pltpu.SMEM)] + [pl.BlockSpec(memory_space=pl.ANY)] * 8,
        out_specs=[vmem] * 3,
        scratch_shapes=[
            *[pltpu.VMEM((1, ROWS, CELLS), F32)] * 3,
            *[pltpu.VMEM(table.shape, table.dtype) for table in constants],
            *pairs,
            *[pltpu.VMEM((HOLD + 4, 2 * HALF, 128), F32)] * 2,
            *[pltpu.VMEM((WINGS, 2, 2 * HALF, 128), F32)] * 3,
            pltpu.VMEM((WINGS, 6, HALF, 128), F32),
            pltpu.VMEM((2, ROWS, 128), F32),
            pltpu.VMEM((2, ROWS, 128), F32),
            pltpu.VMEM((3, ROWS + 16, 512), F32),
            pltpu.SemaphoreType.REGULAR,
            dma((8,)), dma((2, 3)), dma((2,)), dma((2,)), dma((2,)), dma((2,)), dma((2, 4)), dma((2,)), dma((2, 3)),
            dma((3, 2)), dma((3, 2)), dma((2,)), dma((2,)), dma((2,)), dma((2,)),
        ],
        compiler_params=pltpu.CompilerParams(
            collective_id=0, has_side_effects=True, vmem_limit_bytes=60 * 1024 * 1024
        ),
        name="substeps",
    )(wave_speed_sq, height, east_wind, north_wind, *constants)
    return pl.pallas_call(
        write,
        out_shape=[block] * 3,
        in_specs=[vmem] * 3,
        out_specs=[pl.BlockSpec(memory_space=pl.ANY)] * 3,
        scratch_shapes=[dma((3,))],
        compiler_params=pltpu.CompilerParams(vmem_limit_bytes=16 * 1024 * 1024),
        name="write",
    )(*results)


def solution(mesh):
    block = P(None, "lat", "lon")
    return jax.shard_map(
        lambda *args: tuple(body(*args)),
        mesh=mesh, in_specs=(block, block, block, P()), out_specs=(block, block, block), check_vma=False,
    )
```

```python
import math

import jax
import jax.numpy as jnp
import ml_dtypes
import numpy as np
from jax import lax
from jax.experimental import pallas as pl
from jax.experimental.pallas import tpu as pltpu
from jax.sharding import PartitionSpec as P

NLON, NLAT = 12288, 1536
ROWS, CELLS = 96, 384
OUTER, INNER = 96, 128
HALF = 56
COURANT, SPIN = 0.45, 0.3
NORTH = COURANT * 2.0 * NLAT / NLON
FINAL = 260
HOLD = 2
OWNERS = 132
WINGS = HOLD + 2
MESH = pl.DeviceIdType.MESH
F32, BF16 = jnp.float32, jnp.bfloat16
GROUPS = ((0,), (1, 2))
BACK_ROW = (3, 2, 1, 0)
BACK = ((1,), (2, 0))


def split(table):
    high = table.astype(ml_dtypes.bfloat16)
    low = (table - high.astype(np.float64)).astype(ml_dtypes.bfloat16)
    return high, low


def tables():
    a = np.array([3 * d + s for s in range(3) for d in range(32)])
    k1 = np.arange(HALF)
    live = (k1 <= OUTER // 2).astype(np.float64)
    angle = 2 * np.pi * ((k1[:, None] * a[None, :]) % OUTER) / OUTER
    first = np.concatenate([np.cos(angle) * live[:, None], -np.sin(angle) * live[:, None]], axis=0)
    weight = live * np.where((k1 == 0) | (k1 == OUTER // 2), 1.0, 2.0) / NLON
    last = np.concatenate([np.cos(angle) * weight[:, None], -np.sin(angle) * weight[:, None]], axis=0).T
    n = np.arange(INNER)
    turn = 2 * np.pi * (k1[:, None] * n[None, :]) / NLON
    inner = 2 * np.pi * ((n[:, None] * n[None, :]) % INNER) / INNER
    cos, sin = np.cos(inner), np.sin(inner)
    forward = np.block([[cos, -sin], [sin, cos]])
    backward = np.block([[cos, sin], [-sin, cos]])
    wave = k1[:, None] + OUTER * n[None, :]
    steep = np.sin(2 * np.pi * wave / NLON) * live[:, None]
    half_sine = np.where(live[:, None] > 0, 0.5 * np.abs(np.sin(np.pi * wave / NLON)), 1.0)
    first_high, first_low = split(first)
    last_high, last_low = split(last)
    forward_high, forward_low = split(forward)
    backward_high, backward_low = split(backward)
    grid = np.stack([np.cos(turn), np.sin(turn), steep, half_sine]).astype(np.float32)
    return (
        np.concatenate([first_high, first_low, first_high], axis=1),
        np.concatenate([last_high, last_low, last_high], axis=1),
        np.stack([forward_high, forward_low]),
        np.stack([backward_high, backward_low]),
        grid,
    )


def parts(value):
    high = value.astype(BF16)
    return high, (value - high.astype(F32)).astype(BF16)


def dot(left, right):
    return jnp.dot(left, right, preferred_element_type=F32)


def outer_step(table, value):
    high, low = parts(value)
    return dot(table.astype(BF16), jnp.concatenate([high, high, low], axis=0))


def inner_step(table, value):
    high, low = parts(value)
    table_high, table_low = table[0].astype(BF16), table[1].astype(BF16)
    return dot(high, table_high) + dot(low, table_high) + dot(high, table_low)


def kernel(
    speed_ref, h_hbm, u_hbm, v_hbm, first_hbm, last_hbm, fore_hbm, back_hbm, grid_hbm,
    h_out, u_out, v_out,
    h_ref, u_ref, v_ref, first_ref, last_ref, fore_ref, back_ref, grid_ref,
    src0, src1, relay0, relay1, recv0, recv1, snd0, snd1, home0, home1, ret0, ret1,
    tall, tall_new, wind, wind_new, wind_last, scale, packed, sides, ext,
    go, loads, send_a, recv_a, send_b, recv_b, send_c, recv_c, send_d, recv_d, send_x, recv_x, send_s, recv_s, send_r, recv_r,
):
    fields, outs = (h_ref, u_ref, v_ref), (h_out, u_out, v_out)
    operands = (h_hbm, u_hbm, v_hbm, first_hbm, last_hbm, fore_hbm, back_hbm, grid_hbm)
    held = (h_ref, u_ref, v_ref, first_ref, last_ref, fore_ref, back_ref, grid_ref)
    src, relay, recv = (src0, src1), (relay0, relay1), (recv0, recv1)
    snd, home, ret = (snd0, snd1), (home0, home1), (ret0, ret1)
    lat, lon = lax.axis_index("lat"), lax.axis_index("lon")
    south = lat >= 8
    band = jnp.where(south, 15 - lat, lat)
    core = lax.rem(band, 2)
    z = lax.rem(lon, 16)
    x = 2 * lax.div(lon, 16) + lax.rem(lax.div(band, 2), 2)

    def back_x(n):
        return jnp.where(n == 4, BACK_ROW[0], jnp.where(n == 5, BACK_ROW[1], jnp.where(n == 6, BACK_ROW[2], BACK_ROW[3])))

    def back_line(n):
        return jnp.where(n == BACK_ROW[0], 4, jnp.where(n == BACK_ROW[1], 5, jnp.where(n == BACK_ROW[2], 6, 7)))

    line = jnp.where(band < 4, x, back_line(x))
    wide = line >= 6
    near = lax.rem(z + line, 16)
    slab = 16 * core + z
    extra = jnp.logical_and(wide, jnp.logical_and(core == 0, jnp.logical_or(near == 0, near == 8)))
    owner = jnp.logical_or(core == 1, extra)
    owners = jnp.where(wide, 18, 16)

    def nth_at(to_near):
        return to_near + jnp.where(wide, 1 + jnp.where(to_near > 8, 1, 0), 0)

    nth = jnp.where(core == 1, nth_at(near), jnp.where(near == 0, 0, 10))
    chain = 16 * line + 2 * jnp.where(line == 7, 1, 0) + nth
    source = band <= 2
    stencil = band >= 2
    my_band = jnp.where(wide, 2, lax.div(line, 3))
    my_lat = jnp.where(south, 15 - my_band, my_band)
    my_part = line - 3 * my_band

    def member(to_line, to_z, to_core):
        to_x = jnp.where(to_line < 4, to_line, back_x(to_line))
        to_band = 4 * lax.div(to_line, 4) + 2 * lax.rem(to_x, 2) + to_core
        return jnp.where(south, 15 - to_band, to_band), 16 * lax.div(to_x, 2) + to_z

    def mate(to_z, to_core):
        shift = to_core - core
        return jnp.where(south, lat - shift, lat + shift), lon - z + to_z

    def holder(n):
        to_line = jnp.where(n < 96, lax.div(n, 16), 6 + lax.div(jnp.maximum(n - 96, 0), 18))
        to_nth = n - 16 * to_line - 2 * jnp.where(to_line == 7, 1, 0)
        broad = to_line >= 6
        to_near = jnp.where(broad, jnp.maximum(to_nth - jnp.where(to_nth > 9, 2, 1), 0), to_nth)
        to_core = jnp.where(jnp.logical_and(broad, jnp.logical_or(to_nth == 0, to_nth == 10)), 0, 1)
        return member(to_line, lax.rem(to_near + 16 - to_line, 16), to_core)

    def chip(k):
        away = 8 - lax.div(k + 1, 2)
        return lax.rem(z + 16 + jnp.where(lax.rem(k, 2) == 1, away, -away), 16)

    def same(target):
        return jnp.logical_and(target[0] == lat, target[1] == lon)

    def remote(here, there, send_sem, recv_sem, target):
        pltpu.make_async_remote_copy(
            src_ref=here, dst_ref=there, send_sem=send_sem, recv_sem=recv_sem, device_id=target, device_id_type=MESH
        ).start()

    def send(here, there, send_sem, recv_sem, target):
        own = same(target)

        @pl.when(own)
        def _():
            pltpu.make_async_copy(here, there, recv_sem).start()

        @pl.when(jnp.logical_not(own))
        def _():
            remote(here, there, send_sem, recv_sem, target)

    def landed(ref, sem):
        pltpu.make_async_copy(ref, ref, sem).wait()

    def part_start(k, size):
        return jnp.where(south, ROWS - size * (k + 1), size * k)

    def owner_start(i):
        return HOLD * jnp.where(south, owners - 1 - i, i)

    def each_size(act):
        pl.when(jnp.logical_not(wide))(lambda: act(32))
        pl.when(wide)(lambda: act(36))

    right = jnp.where(lon == 31, 0, lon + 1)
    left = jnp.where(lon == 0, 31, lon - 1)
    before = chain + jnp.where(south, 1, -1)
    after = chain + jnp.where(south, -1, 1)
    has_before = jnp.logical_and(owner, jnp.logical_and(before >= 0, before < OWNERS))
    has_after = jnp.logical_and(owner, jnp.logical_and(after >= 0, after < OWNERS))
    before_device, after_device = holder(jnp.clip(before, 0, OWNERS - 1)), holder(jnp.clip(after, 0, OWNERS - 1))

    barrier = pltpu.get_barrier_semaphore()

    def greet(target):
        pl.semaphore_signal(barrier, inc=1, device_id=target, device_id_type=MESH)

    def greet_other(target):
        pl.when(jnp.logical_not(same(target)))(lambda: greet(target))

    pl.when(jnp.logical_not(same((my_lat, slab))))(lambda: greet((my_lat, slab)))

    def load(*indices):
        for index in indices:
            pltpu.make_async_copy(operands[index], held[index], loads.at[index]).start()

    def loaded(*indices):
        for index in indices:
            pltpu.make_async_copy(operands[index], held[index], loads.at[index]).wait()

    load(0, 1, 2)
    pl.when(owner)(lambda: load(3, 4, 5, 6, 7))

    def helper(of_line, to_z):
        of_x = jnp.where(of_line < 4, of_line, back_x(of_line))
        return member(back_line(of_x), to_z, lax.div(of_line, 4))

    helps = band >= 4
    helped = jnp.where(core == 1, back_line(x), x)

    def greet_helper(k, carry):
        greet(helper(line, chip(k)))
        return carry

    my_helper = helper(line, z)
    helped_from_afar = jnp.logical_not(same(my_helper))

    greeted = jnp.where(helps, jnp.where(helped >= 6, 18, 16) + 2 - 2 * core, 0)
    for k in range(3):
        target = member(jnp.minimum(3 * band + k, 7), z, lax.div(lon, 16))
        meant = jnp.logical_or(band < 2, jnp.logical_and(band == 2, k < 2))
        meant = jnp.logical_and(meant, jnp.logical_not(same(target)))
        greeted += meant.astype(jnp.int32)
    for meant, target in (
        (has_before, before_device), (has_after, after_device), (stencil, (lat, left)), (stencil, (lat, right)),
        (jnp.logical_and(stencil, lat > 2), (lat - 1, lon)), (jnp.logical_and(stencil, lat < 13), (lat + 1, lon)),
    ):
        pl.when(meant)(lambda target=target: greet(target))
        greeted += meant.astype(jnp.int32)

    @pl.when(owner)
    def _():
        lax.fori_loop(0, 15, greet_helper, 0)

    pl.when(jnp.logical_and(owner, helped_from_afar))(lambda: greet(my_helper))
    pl.when(helped_from_afar)(lambda: greet(my_helper))

    def gather(g):
        per = 3 * len(GROUPS[g])
        for pos, f in enumerate(GROUPS[g]):
            for s in range(3):
                src[g][pl.ds(3 * pos + s, ROWS, stride=per), :] = fields[f][0, :, 128 * s : 128 * (s + 1)]

    def send_rows(g):
        per = 3 * len(GROUPS[g])

        def one(k, size):
            send(
                src[g].at[pl.ds(part_start(k, size) * per, size * per)], relay[g].at[pl.ds(0, size * per)],
                send_a.at[g, k], recv_a.at[g], member(3 * band + k, z, lax.div(lon, 16)),
            )

        @pl.when(band < 2)
        def _():
            for k in range(3):
                one(k, 32)

        @pl.when(band == 2)
        def _():
            for k in range(2):
                one(k, 36)

    loaded(0)
    pl.when(source)(lambda: gather(0))
    pl.semaphore_wait(barrier, greeted)

    @pl.when(helps)
    def _():
        for to_core in range(2):
            target = member(helped, z, to_core)
            pl.when(jnp.logical_not(same(target)))(
                lambda target=target: pl.semaphore_signal(go, inc=1, device_id=target, device_id_type=MESH)
            )

    pl.when(source)(lambda: send_rows(0))
    loaded(1, 2)

    @pl.when(source)
    def _():
        gather(1)
        send_rows(1)

    @pl.when(stencil)
    def _():
        lane = lax.broadcasted_iota(jnp.int32, (ROWS, 128), 1)
        high = [ref[0, :, 256:384] for ref in fields]
        low = [ref[0, :, 0:128] for ref in fields]
        packed[0] = jnp.where(
            lane >= 124, high[0], jnp.where(lane >= 120, pltpu.roll(high[1], 124, 1), pltpu.roll(high[2], 120, 1))
        )
        packed[1] = jnp.where(lane < 4, low[0], jnp.where(lane < 8, pltpu.roll(low[1], 4, 1), pltpu.roll(low[2], 8, 1)))
        remote(packed.at[0], sides.at[0], send_s.at[0], recv_s.at[0], (lat, right))
        remote(packed.at[1], sides.at[1], send_s.at[1], recv_s.at[1], (lat, left))

    pl.when(helped_from_afar)(lambda: pl.semaphore_wait(go, 1))
    for g in range(2):
        per = 3 * len(GROUPS[g])
        each_size(lambda size, g=g, per=per: landed(relay[g].at[pl.ds(0, size * per)], recv_a.at[g]))

        def to_owner(how, i, target, g=g, per=per):
            how(
                relay[g].at[pl.ds(owner_start(i) * per, HOLD * per)],
                recv[g].at[pl.ds(slab * (HOLD * per), HOLD * per)],
                send_b.at[g], recv_b.at[g], target,
            )

        def spread(k, carry, to_owner=to_owner):
            to = chip(k)
            to_owner(remote, nth_at(lax.rem(to + line, 16)), mate(to, 1))
            return carry

        @pl.when(wide)
        def _(to_owner=to_owner):
            for i, to_near in ((0, 0), (10, 8)):
                to_owner(send, i, mate(lax.rem(to_near + 16 - line, 16), 0))

        lax.fori_loop(0, 15, spread, 0)
        to_owner(send, nth_at(near), mate(z, 1))

    @pl.when(stencil)
    def _():
        landed(sides.at[0], recv_s.at[0])
        landed(sides.at[1], recv_s.at[1])
        lane = lax.broadcasted_iota(jnp.int32, (ROWS, 128), 1)
        for f in range(3):
            ext[f, 8 : 8 + ROWS, 0:CELLS] = fields[f][0]
            east_side, west_side = sides[1], sides[0]
            if f:
                east_side, west_side = pltpu.roll(east_side, 128 - 4 * f, 1), pltpu.roll(west_side, 4 * f, 1)
            ext[f, 8 : 8 + ROWS, CELLS : CELLS + 128] = jnp.where(lane < 64, east_side, west_side)

        @pl.when(lat > 2)
        def _():
            remote(ext.at[:, 8:16, :], ext.at[:, 104:112, :], send_r.at[0], recv_r.at[0], (lat - 1, lon))

        @pl.when(lat < 13)
        def _():
            remote(ext.at[:, 96:104, :], ext.at[:, 0:8, :], send_r.at[1], recv_r.at[1], (lat + 1, lon))

        @pl.when(lat == 2)
        def _():
            ext[:, 0:8, :] = jnp.zeros((3, 8, 512), F32)

        @pl.when(lat == 13)
        def _():
            ext[:, 104:112, :] = jnp.zeros((3, 8, 512), F32)

    def transform(g):
        size = HOLD * 3 * len(GROUPS[g])
        order = [(row, pos) for row in range(HOLD) for pos in range(len(GROUPS[g]))]
        grids = [
            jnp.concatenate(
                [recv[g][pl.ds(row * (size // HOLD) + 3 * pos + s, 32, stride=size), :] for s in range(3)], axis=0
            )
            for row, pos in order
        ]
        mixed = outer_step(first_ref[...], jnp.concatenate(grids, axis=1))
        cos, sin = grid_ref[0], grid_ref[1]
        twisted = []
        for n in range(len(order)):
            real, imag = mixed[:HALF, 128 * n : 128 * (n + 1)], mixed[HALF:, 128 * n : 128 * (n + 1)]
            twisted.append(jnp.concatenate([real * cos + imag * sin, imag * cos - real * sin], axis=1))
        spectrum = inner_step(fore_ref, jnp.concatenate(twisted, axis=0))
        return {
            key: (spectrum[HALF * n : HALF * (n + 1), :128], spectrum[HALF * n : HALF * (n + 1), 128:])
            for n, key in enumerate(order)
        }

    def restore(g, spectra):
        size = HOLD * 3 * len(BACK[g])
        order = list(spectra)
        cos, sin = grid_ref[0], grid_ref[1]
        back = inner_step(
            back_ref, jnp.concatenate([jnp.concatenate(spectra[key], axis=1) for key in order], axis=0)
        )
        spun = []
        for n in range(len(order)):
            real, imag = back[HALF * n : HALF * (n + 1), :128], back[HALF * n : HALF * (n + 1), 128:]
            spun.append(jnp.concatenate([real * cos - imag * sin, imag * cos + real * sin], axis=0))
        cells = outer_step(last_ref[...], jnp.concatenate(spun, axis=1))
        for n, (row, pos) in enumerate(order):
            for s in range(3):
                snd[g][pl.ds(row * (size // HOLD) + 3 * pos + s, 32, stride=size), :] = cells[
                    32 * s : 32 * (s + 1), 128 * n : 128 * (n + 1)
                ]

    def put(ref, index, pair):
        ref[(*index, slice(0, HALF))] = pair[0]
        ref[(*index, slice(HALF, 2 * HALF))] = pair[1]

    def get(ref, *index):
        return ref[(*index, slice(0, HALF))], ref[(*index, slice(HALF, 2 * HALF))]

    row0 = jnp.where(south, NLAT - HOLD - HOLD * chain, HOLD * chain)

    def polar(row):
        steps = jnp.where(south, NLAT - 1 - row, row)
        return jnp.abs(jnp.full((1, 128), steps, jnp.int32).astype(F32) + 0.5) * (math.pi / NLAT)

    def cosine(w):
        return jnp.sin(polar(row0 + w - 1))

    def prepare():
        speed = speed_ref[0]
        share_of_pole = jnp.where(south, SPIN, -SPIN).astype(F32)
        for w in range(WINGS):
            there = 1.0
            if w == 0:
                there = jnp.where(has_before, 1.0, 0.0).astype(F32)
            if w == WINGS - 1:
                there = jnp.where(has_after, 1.0, 0.0).astype(F32)
            angle = polar(row0 + w - 1)
            share = 1.0 / jnp.maximum(grid_ref[3], jnp.sin(angle))
            keep = share * (jnp.sin(angle) * there)
            slope = share * (COURANT * grid_ref[2])
            scale[w, 0] = slope
            scale[w, 1] = keep * (share_of_pole * jnp.cos(angle))
            scale[w, 2] = keep * (0.5 * NORTH)
            if 0 < w < WINGS - 1:
                scale[w, 3] = speed * slope
                scale[w, 4] = share * (speed * (0.5 * NORTH) * cosine(w - 1))
                scale[w, 5] = share * (speed * (0.5 * NORTH) * cosine(w + 1))

    def push_east(heights, old, new, w):
        mid, east, north = get(heights, w + 1), get(old, w, 0), get(old, w, 1)
        slope, swirl = scale[w, 0], scale[w, 1]
        put(new, (w, 0), (
            east[0] + slope * mid[1] + swirl * north[0],
            east[1] - slope * mid[0] + swirl * north[1],
        ))

    def push_north(heights, old, new, w):
        low, high = get(heights, w), get(heights, w + 2)
        east, north = get(old, w, 0), get(old, w, 1)
        swirl, climb = scale[w, 1], scale[w, 2]
        put(new, (w, 1), tuple(north[p] - climb * (high[p] - low[p]) - swirl * east[p] for p in range(2)))

    def pushed_height(heights, winds, w):
        mid, east = get(heights, w + 1), get(winds, w, 0)
        low, high = get(winds, w - 1, 1), get(winds, w + 1, 1)
        slope, below, above = scale[w, 3], scale[w, 4], scale[w, 5]
        return (
            mid[0] + slope * east[1] - (above * high[0] - below * low[0]),
            mid[1] - slope * east[0] - (above * high[1] - below * low[1]),
        )

    def trade(e, ref, wing):
        @pl.when(has_before)
        def _():
            remote(
                ref.at[pl.ds(wing, wing)], ref.at[pl.ds(wing + HOLD, wing)],
                send_x.at[e, 0], recv_x.at[e, 1], before_device,
            )

        @pl.when(has_after)
        def _():
            remote(ref.at[pl.ds(HOLD, wing)], ref.at[pl.ds(0, wing)], send_x.at[e, 1], recv_x.at[e, 0], after_device)

    def traded(e, ref, wing):
        pl.when(has_before)(lambda: landed(ref.at[pl.ds(0, wing)], recv_x.at[e, 0]))
        pl.when(has_after)(lambda: landed(ref.at[pl.ds(wing + HOLD, wing)], recv_x.at[e, 1]))

    def send_back(g):
        size = HOLD * 3 * len(BACK[g])
        start = owner_start(nth) * (size // HOLD)

        def one(how, to_z, to_core):
            how(
                snd[g].at[pl.ds((16 * to_core + to_z) * size, size)], home[g].at[pl.ds(start, size)],
                send_c.at[g], recv_c.at[g, lax.div(near, 4) if g else 0], mate(to_z, to_core),
            )

        def both(k, carry):
            to = jnp.where(k < 1, 0 + lax.rem(z + k, 1), jnp.where(k < 3, 1 + lax.rem(z + k, 2), jnp.where(k < 6, 3 + lax.rem(z + k, 3), 6 + lax.rem(z + k, 10))))
            one(remote, to, 1 - core)
            one(send, to, core)
            return carry

        lax.fori_loop(0, 16, both, 0)

    @pl.when(owner)
    def _():
        loaded(3, 4, 5, 6, 7)
        prepare()

        @pl.when(jnp.logical_not(has_before))
        def _():
            tall[0:2] = jnp.zeros((2, 2 * HALF, 128), F32)
            tall_new[0:2] = jnp.zeros((2, 2 * HALF, 128), F32)
            wind[0] = jnp.zeros((2, 2 * HALF, 128), F32)

        @pl.when(jnp.logical_not(has_after))
        def _():
            tall[2 + HOLD : 4 + HOLD] = jnp.zeros((2, 2 * HALF, 128), F32)
            tall_new[2 + HOLD : 4 + HOLD] = jnp.zeros((2, 2 * HALF, 128), F32)
            wind[1 + HOLD] = jnp.zeros((2, 2 * HALF, 128), F32)

        landed(recv[0], recv_b.at[0])
        for (row, _), pair in transform(0).items():
            put(tall, (2 + row,), pair)
        trade(0, tall, 2)
        landed(recv[1], recv_b.at[1])
        for (row, which), pair in transform(1).items():
            put(wind, (1 + row, which), pair)
        trade(1, wind, 1)
        traded(0, tall, 2)
        traded(1, wind, 1)
        for w in range(WINGS):
            push_east(tall, wind, wind_new, w)
            push_north(tall, wind, wind_new, w)
        for w in range(1, 1 + HOLD):
            put(tall_new, (1 + w,), pushed_height(tall, wind_new, w))
        trade(2, tall_new, 2)
        for w in range(1, 1 + HOLD):
            push_east(tall_new, wind_new, wind_last, w)
        restore(0, {(row, 0): get(wind_last, 1 + row, 0) for row in range(HOLD)})
        send_back(0)
        traded(2, tall_new, 2)
        for w in range(WINGS):
            push_north(tall_new, wind_new, wind_last, w)
        last = {(row, 0): get(wind_last, 1 + row, 1) for row in range(HOLD)}
        last.update({(row, 1): pushed_height(tall_new, wind_last, 1 + row) for row in range(HOLD)})
        restore(1, last)
        send_back(1)

    @pl.when(stencil)
    def _():
        @pl.when(lat > 2)
        def _():
            landed(ext.at[:, 0:8, :], recv_r.at[1])

        @pl.when(lat < 13)
        def _():
            landed(ext.at[:, 104:112, :], recv_r.at[0])

        row = lax.broadcasted_iota(jnp.int32, (ROWS + 16, 128), 0) + (ROWS * lat - 8)
        latitude = (row.astype(F32) + (0.5 - NLAT // 2)) * (math.pi / NLAT)
        wide_cos = jnp.concatenate([jnp.cos(latitude)] * 4, axis=1)
        spin = jnp.concatenate([SPIN * jnp.sin(latitude)] * 4, axis=1)
        inverse = 1.0 / wide_cos
        east_scale = (0.5 * COURANT) * inverse
        speed = speed_ref[0]

        def across(value):
            return pltpu.roll(value, 511, 1) - pltpu.roll(value, 1, 1)

        def along(value):
            return pltpu.roll(value, ROWS + 15, 0) - pltpu.roll(value, 1, 0)

        height, east, north = ext[0], ext[1], ext[2]
        for _step in range(2):
            east_inc = spin * north - east_scale * across(height)
            north_inc = (-0.5 * NORTH) * along(height) - spin * east
            east, north = east + east_inc, north + north_inc
            spread_out = east_scale * across(east) + (0.5 * NORTH) * inverse * along(north * wide_cos)
            height = height - speed * spread_out
        for out, value in zip(outs, (height, east, north)):
            out[0] = value[8 : 8 + ROWS, 0:CELLS]

    def deliver(size):
        per = 3 * len(BACK[0])
        landed(home[0].at[pl.ds(0, size * per)], recv_c.at[0, 0])
        send(
            home[0].at[pl.ds(0, size * per)], ret[0].at[pl.ds(part_start(my_part, size) * per, size * per)],
            send_d.at[0], recv_d.at[0, my_part], (my_lat, slab),
        )

    def deliver_quarter(k):
        per = 3 * len(BACK[1])
        turn = jnp.where(lax.rem(near, 4) < 2, 3, 1)
        quarter = lax.rem(lax.div(near, 4) + (0, turn, 4 - turn, 2)[k], 4)

        def rows(size, line_size):
            first = jnp.where(quarter == 0, 0, nth_at(4 * quarter))
            start = jnp.where(south, line_size - size - HOLD * first, HOLD * first)
            here = home[1].at[pl.ds(start * per, size * per)]
            landed(here, recv_c.at[1, quarter])
            send(
                here, ret[1].at[pl.ds((part_start(my_part, line_size) + start) * per, size * per)],
                send_d.at[1], recv_d.at[1, my_part], (my_lat, slab),
            )

        large = jnp.logical_and(wide, lax.rem(quarter, 2) == 0)
        pl.when(jnp.logical_not(wide))(lambda: rows(8, 32))
        pl.when(large)(lambda: rows(10, 36))
        pl.when(jnp.logical_and(wide, jnp.logical_not(large)))(lambda: rows(8, 36))

    each_size(deliver)
    for k in range(4):
        deliver_quarter(k)

    def back(f, s):
        g = 0 if f in BACK[0] else 1
        return ret[g][pl.ds(3 * BACK[g].index(f) + s, ROWS, stride=3 * len(BACK[g])), :]

    @pl.when(band < 2)
    def _():
        for g in range(2):
            per = 3 * len(BACK[g])
            for k in range(3):
                landed(ret[g].at[pl.ds(part_start(k, 32) * per, 32 * per)], recv_d.at[g, k])
            for f in BACK[g]:
                for s in range(3):
                    outs[f][0, :, 128 * s : 128 * (s + 1)] = back(f, s)

    @pl.when(band == 2)
    def _():
        row = lax.broadcasted_iota(jnp.int32, (ROWS, 128), 0)
        from_pole = jnp.where(south, ROWS - 1 - row, row) + 2 * ROWS
        for g in range(2):
            per = 3 * len(BACK[g])
            for k in range(2):
                landed(ret[g].at[pl.ds(part_start(k, 36) * per, 36 * per)], recv_d.at[g, k])
            for f in BACK[g]:
                for s in range(3):
                    lanes = slice(128 * s, 128 * (s + 1))
                    outs[f][0, :, lanes] = jnp.where(from_pole < FINAL, back(f, s), outs[f][0, :, lanes])

    for g in range(2):
        per = 3 * len(GROUPS[g])

        def left_parts(size, parts, g=g, per=per):
            for k in range(parts):
                other = jnp.logical_not(same(member(3 * band + k, z, lax.div(lon, 16))))
                pl.when(other)(lambda k=k: landed(src[g].at[pl.ds(0, size * per)], send_a.at[g, k]))

        pl.when(band < 2)(lambda f=left_parts: f(32, 3))
        pl.when(band == 2)(lambda f=left_parts: f(36, 2))
        for case, count in (
            (jnp.logical_and(jnp.logical_not(wide), owner), 15),
            (jnp.logical_and(jnp.logical_not(wide), jnp.logical_not(owner)), 16),
            (jnp.logical_and(wide, owner), 17),
            (jnp.logical_and(wide, jnp.logical_not(owner)), 18),
        ):
            pl.when(case)(
                lambda g=g, n=count * HOLD * per: landed(relay[g].at[pl.ds(0, n)], send_b.at[g])
            )
        ret_per = 3 * len(BACK[g])
        pl.when(owner)(lambda g=g, per=ret_per: landed(snd[g].at[pl.ds(0, 31 * HOLD * per)], send_c.at[g]))

        @pl.when(jnp.logical_not(same((my_lat, slab))))
        def _(g=g, per=ret_per):
            each_size(lambda size: landed(home[g].at[pl.ds(0, size * per)], send_d.at[g]))

    @pl.when(stencil)
    def _():
        for side in range(2):
            landed(packed.at[side], send_s.at[side])

        @pl.when(lat > 2)
        def _():
            landed(ext.at[:, 8:16, :], send_r.at[0])

        @pl.when(lat < 13)
        def _():
            landed(ext.at[:, 96:104, :], send_r.at[1])

    for e, (ref, wing) in enumerate(((tall, 2), (wind, 1), (tall_new, 2))):
        pl.when(has_before)(lambda e=e, ref=ref, wing=wing: landed(ref.at[pl.ds(0, wing)], send_x.at[e, 0]))
        pl.when(has_after)(lambda e=e, ref=ref, wing=wing: landed(ref.at[pl.ds(0, wing)], send_x.at[e, 1]))


def write(h_ref, u_ref, v_ref, h_out, u_out, v_out, sems):
    copies = [
        pltpu.make_async_copy(here, there, sems.at[n])
        for n, (here, there) in enumerate(((h_ref, h_out), (u_ref, u_out), (v_ref, v_out)))
    ]
    for copy in copies:
        copy.start()
    for copy in copies:
        copy.wait()


def body(height, east_wind, north_wind, wave_speed_sq):
    constants = [np.asarray(table, np.float32) for table in tables()]
    block = jax.ShapeDtypeStruct((1, ROWS, CELLS), F32)
    pairs = []
    for groups, rows in ((GROUPS, ROWS), (GROUPS, 36), (GROUPS, 32 * HOLD), (BACK, 32 * HOLD), (BACK, 36), (BACK, ROWS)):
        pairs += [pltpu.VMEM((rows * 3 * len(group), 128), F32) for group in groups]
    dma = pltpu.SemaphoreType.DMA
    vmem = pl.BlockSpec(memory_space=pltpu.VMEM)
    results = pl.pallas_call(
        kernel,
        out_shape=[pltpu.VMEM(block.shape, F32)] * 3,
        in_specs=[pl.BlockSpec(memory_space=pltpu.SMEM)] + [pl.BlockSpec(memory_space=pl.ANY)] * 8,
        out_specs=[vmem] * 3,
        scratch_shapes=[
            *[pltpu.VMEM((1, ROWS, CELLS), F32)] * 3,
            *[pltpu.VMEM(table.shape, table.dtype) for table in constants],
            *pairs,
            *[pltpu.VMEM((HOLD + 4, 2 * HALF, 128), F32)] * 2,
            *[pltpu.VMEM((WINGS, 2, 2 * HALF, 128), F32)] * 3,
            pltpu.VMEM((WINGS, 6, HALF, 128), F32),
            pltpu.VMEM((2, ROWS, 128), F32),
            pltpu.VMEM((2, ROWS, 128), F32),
            pltpu.VMEM((3, ROWS + 16, 512), F32),
            pltpu.SemaphoreType.REGULAR,
            dma((8,)), dma((2, 3)), dma((2,)), dma((2,)), dma((2,)), dma((2,)), dma((2, 4)), dma((2,)), dma((2, 3)),
            dma((3, 2)), dma((3, 2)), dma((2,)), dma((2,)), dma((2,)), dma((2,)),
        ],
        compiler_params=pltpu.CompilerParams(
            collective_id=0, has_side_effects=True, vmem_limit_bytes=60 * 1024 * 1024
        ),
        name="substeps",
    )(wave_speed_sq, height, east_wind, north_wind, *constants)
    return pl.pallas_call(
        write,
        out_shape=[block] * 3,
        in_specs=[vmem] * 3,
        out_specs=[pl.BlockSpec(memory_space=pl.ANY)] * 3,
        scratch_shapes=[dma((3,))],
        compiler_params=pltpu.CompilerParams(vmem_limit_bytes=16 * 1024 * 1024),
        name="write",
    )(*results)


def solution(mesh):
    block = P(None, "lat", "lon")
    return jax.shard_map(
        lambda *args: tuple(body(*args)),
        mesh=mesh, in_specs=(block, block, block, P()), out_specs=(block, block, block), check_vma=False,
    )
```
